32 devices in a mesh: fsdp: 4 (over y, x), ctx: 4 (over z), tp: 2 (over core).
Axes of the slice: x: 2, y: 2, z: 4, core: 2. Of those that a mesh axis runs over, the one named last changes fastest.
Arguments:
- tokens: bfloat16 [8, 4096, 512], P('fsdp', 'ctx'), may hold values from -6 to 6
- expert_routes: int32 [8, 4096, 2], P('fsdp', 'ctx'), may hold values from 0 to 7, all different within a row
- picture_start: int32 [8, 2], P('fsdp'), may hold values from 0 to 3840, as said below
- picture_mode: int32 [8, 2], P('fsdp'), may hold values from 0 to 1
- norm1_gain: bfloat16 [512], replicated, may hold values from 0.5 to 1.5
- norm1_bias: bfloat16 [512], replicated, may hold values from -1.1953125 to 1.1953125
- router_weight: bfloat16 [512, 8], P('fsdp'), may hold values from -0.125 to 0.125
- query_weight: bfloat16 [8, 512, 64], P('tp', 'fsdp'), may hold values from -0.5 to 0.5
- output_weight: bfloat16 [8, 64, 512], P('tp', None, 'fsdp'), may hold values from -3 to 3
- key_value_weight: bfloat16 [512, 128], P('fsdp'), may hold values from -0.25 to 0.25
- norm2_gain: bfloat16 [512], replicated, may hold values from 0.5 to 1.5
- norm2_bias: bfloat16 [512], replicated, may hold values from -1.1953125 to 1.1953125
- up_weight: bfloat16 [512, 2048], P('fsdp', 'tp'), may hold values from -0.25 to 0.25
- up_bias: bfloat16 [2048], P('tp'), may hold values from -1.1953125 to 1.1953125
- down_weight: bfloat16 [2048, 512], P('tp', 'fsdp'), may hold values from -0.125 to 0.125
- down_bias: bfloat16 [512], replicated, may hold values from -1.1953125 to 1.1953125
- result_derivative_tokens: bfloat16 [8, 4096, 512], P('fsdp', 'ctx'), may hold values from -6 to 6
Outputs:
- output: bfloat16 [8, 4096, 512], P('fsdp', 'ctx')
- input_grad: bfloat16 [8, 4096, 512], P('fsdp', 'ctx')
- norm1_gain_grad: float32 [512], replicated
- norm1_bias_grad: float32 [512], replicated
- router_weight_grad: float32 [512, 8], P('fsdp')
- query_weight_grad: float32 [8, 512, 64], P('tp', 'fsdp')
- output_weight_grad: float32 [8, 64, 512], P('tp', None, 'fsdp')
- key_value_weight_grad: float32 [512, 128], P('fsdp')
- norm2_gain_grad: float32 [512], replicated
- norm2_bias_grad: float32 [512], replicated
- up_weight_grad: float32 [512, 2048], P('fsdp', 'tp')
- up_bias_grad: float32 [2048], P('tp')
- down_weight_grad: float32 [2048, 512], P('tp', 'fsdp')
- down_bias_grad: float32 [512], replicated
The draws below stay inside these ranges and needn't reach their ends.
Inputs may be any that keep to these rules, and one draw needn't show every extreme that they name: `picture_start`: picture segment k of a sequence starts inside the k-th of 2 equal regions of its positions and ends inside it, so segments never meet; some segment starts at position 0 and some ends at the end of the last region. `expert_routes`: the two experts of a token differ.
All inputs are finite; a program needn't handle non-finite values.
Results may differ from the reference program's by a relative error of at most 0.012.
The reference program's roundings to bfloat16 on the way count: a program that leaves them out, or rounds other values in their place, can miss the bound.
Values may be sent and summed in bfloat16 or wider, within the bound.
A program may use at most 576 MiB of HBM per device.

```python
import math
import jax
import jax.numpy as jnp
from jax import lax

D = 512
E = 8
HD = 64
FF = 2048
PIC = 256
PICS = 2
LENGTH = 4096
SEQS = 8


def draw_picture_start(key, part):
    key = jax.random.fold_in(key, 3)
    region = LENGTH // PICS
    offset = jax.random.randint(key, (SEQS, PICS), 0, region - PIC + 1)
    offset = offset.at[0, 0].set(0)
    offset = offset.at[SEQS - 1, PICS - 1].set(region - PIC)
    return (offset + region * jnp.arange(PICS, dtype=jnp.int32)[None, :]).astype(jnp.int32)


def place_ends(values, rng, smallest, largest):
    longest = values.shape.index(max(values.shape))
    spots = []
    for shift in (0, 1):
        where = [jax.random.randint(jax.random.fold_in(rng, axis), (), 0, length) for axis, length in enumerate(values.shape)]
        where[longest] = (where[longest] + shift) % values.shape[longest]
        spots.append(tuple(where))
    return values.at[spots[0]].set(smallest).at[spots[1]].set(largest)


def block_levels(stream_key, shape, shards, low, largest):
    gain = 1.0
    for axis_at, shards_of in shards:
        heights = jax.random.uniform(jax.random.fold_in(jax.random.fold_in(stream_key, 6), axis_at), (shards_of,), jnp.float32, low / len(shards), largest / len(shards))
        gain = gain * jnp.repeat(jnp.exp(heights), shape[axis_at] // shards_of).reshape((-1,) + (1,) * (len(shape) - 1 - axis_at))
    return gain


def different_ones(key, rows, amount, top, lift):
    order = jax.random.permutation(jax.random.fold_in(key, 1), amount)
    boost = order
    for power in range(3):
        boost = boost * boost // amount
    boost = boost * lift // amount
    chance = jax.random.randint(jax.random.fold_in(key, 2), (rows, amount), 0, 4096) + boost
    fixed_rows = jax.random.permutation(jax.random.fold_in(key, 3), rows)[jnp.arange(amount) % rows]
    chance = jnp.where(jnp.arange(rows)[:, None] == fixed_rows[None, :], 1 << 14, chance)
    score = chance * amount + jnp.arange(amount)
    return lax.top_k(score.astype(jnp.int32), top)[1].astype(jnp.int32)


def gaussian(stream_key, extent, deviation, most, split=(), held_as=jnp.bfloat16):
    values = jax.random.normal(stream_key, extent, jnp.float32) * deviation
    if len(split) > 0:
        values = block_levels(stream_key, extent, split, -0.22, 0.18) * values
    return jnp.clip(values, min=-most, max=most).astype(held_as)


def setup_inputs(seed: int = 0) -> dict:
    streams_of = jax.random.split(jax.random.key(seed), 18)
    tokens = gaussian(streams_of[0], (SEQS, LENGTH, D), 1.0, 6.0, ((0, 4), (1, 4)))
    expert_routes = different_ones(streams_of[1], SEQS * LENGTH, E, 2, 2048).reshape((SEQS, LENGTH, 2))
    picture_start = draw_picture_start(jax.random.fold_in(streams_of[17], 71), 0)
    picture_mode = place_ends(jax.random.randint(streams_of[3], (SEQS, PICS), 0, 2), jax.random.fold_in(streams_of[3], 1), 0, 1).astype(jnp.int32)
    norm1_gain = jnp.clip(1.0 + 0.1 * jax.random.normal(streams_of[4], (D,), jnp.float32), 0.5, 1.5).astype(jnp.bfloat16)
    norm1_bias = gaussian(streams_of[5], (D,), 0.2, 1.1953125)
    router_weight = gaussian(streams_of[6], (D, E), (4 * D) ** -0.5, 0.125, ((0, 4),))
    query_weight = gaussian(streams_of[7], (E, D, HD), (D // 4) ** -0.5, 0.5, ((0, 2), (1, 4)))
    output_weight = gaussian(streams_of[8], (E, HD, D), (HD // 16) ** -0.5, 3.0, ((0, 2), (2, 4)))
    key_value_weight = gaussian(streams_of[9], (D, 2 * HD), D ** -0.5, 0.25, ((0, 4),))
    norm2_gain = jnp.clip(1.0 + 0.1 * jax.random.normal(streams_of[10], (D,), jnp.float32), 0.5, 1.5).astype(jnp.bfloat16)
    norm2_bias = gaussian(streams_of[11], (D,), 0.2, 1.1953125)
    up_weight = gaussian(streams_of[12], (D, FF), D ** -0.5, 0.25, ((0, 4), (1, 2)))
    up_bias = gaussian(streams_of[13], (FF,), 0.2, 1.1953125, ((0, 2),))
    down_weight = gaussian(streams_of[14], (FF, D), FF ** -0.5, 0.125, ((0, 2), (1, 4)))
    down_bias = gaussian(streams_of[15], (D,), 0.2, 1.1953125)
    result_derivative_tokens = gaussian(streams_of[16], (SEQS, LENGTH, D), 1.0, 6.0, ((0, 4), (1, 4)))
    return dict(tokens=tokens, expert_routes=expert_routes, picture_start=picture_start, picture_mode=picture_mode, norm1_gain=norm1_gain, norm1_bias=norm1_bias, router_weight=router_weight, query_weight=query_weight, output_weight=output_weight, key_value_weight=key_value_weight, norm2_gain=norm2_gain, norm2_bias=norm2_bias, up_weight=up_weight, up_bias=up_bias, down_weight=down_weight, down_bias=down_bias, result_derivative_tokens=result_derivative_tokens)


@jax.custom_vjp
def low(v):
    return lax.optimization_barrier(v.astype(jnp.bfloat16)).astype(jnp.float32)

@jax.custom_vjp
def low_back(v):
    return v

def low_keep(v):
    return (low(v), None)

def low_pass(kept, grad):
    return (grad,)

def back_keep(v):
    return (v, None)

def back_low(kept, grad):
    return (low(grad),)
low.defvjp(low_keep, low_pass)
low_back.defvjp(back_keep, back_low)
stabilizer_tiny = 1e-05
neg_large = -1e+30
highest_precision = lax.Precision.HIGHEST

def layer_norm(values, norm_gain, norm_shift):
    center = values - lax.optimization_barrier(jnp.mean(values, axis=-1, keepdims=True))
    inverse = lax.rsqrt(lax.optimization_barrier(jnp.mean(center * center, axis=-1, keepdims=True)) + stabilizer_tiny)
    return center * inverse * norm_gain + norm_shift

def picture_ids(positions, starts, picture_mode):
    inside = (positions[None, :, None] >= starts[:, None, :]) & (positions[None, :, None] < starts[:, None, :] + PIC) & (picture_mode[:, None, :] == 1)
    labels = jnp.arange(1, starts.shape[1] + 1, dtype=jnp.int32)
    return lax.optimization_barrier(jnp.sum(jnp.where(inside, labels[None, None, :], 0), axis=-1)) - 1

def visible(query_pos, key_pos, starts, picture_mode):
    asker_ids = picture_ids(query_pos, starts, picture_mode)
    key_ids = picture_ids(key_pos, starts, picture_mode)
    future_masking = key_pos[None, None, :] <= query_pos[None, :, None]
    shared = (asker_ids[:, :, None] == key_ids[:, None, :]) & (asker_ids[:, :, None] >= 0)
    return future_masking | shared

def gates_of(router_logits, routes, expert_count):
    expert_iota = jnp.arange(expert_count, dtype=jnp.int32)
    first_hot = (routes[..., 0:1] == expert_iota).astype(router_logits.dtype)
    second_hot = (routes[..., 1:2] == expert_iota).astype(router_logits.dtype)
    first_logit = lax.optimization_barrier(jnp.sum(router_logits * first_hot, axis=-1))
    second_logit = lax.optimization_barrier(jnp.sum(router_logits * second_hot, axis=-1))
    top_logit = jnp.maximum(first_logit, second_logit)
    first_exp = jnp.exp(first_logit - top_logit)
    second_exp = jnp.exp(second_logit - top_logit)
    total_exp = first_exp + second_exp
    return (first_hot, second_hot, first_exp / total_exp, second_exp / total_exp)

def attend(pieces):
    query_rows_all, key_value_pair, allowed = pieces
    key_rows = key_value_pair[:, :HD]
    value_rows = key_value_pair[:, HD:]
    raw_scores = low_back(jnp.einsum('eih,jh->eij', query_rows_all, key_rows, precision=highest_precision) * (1.0 / math.sqrt(HD)))
    scores = jnp.where(allowed[None, :, :], raw_scores, neg_large)
    log_total = jax.nn.logsumexp(scores, axis=-1, keepdims=True)
    prob_rows = low(jnp.exp(scores - log_total))
    return jnp.einsum('eij,jh->eih', prob_rows, value_rows, precision=highest_precision)

def reference(tokens, expert_routes, picture_start, picture_mode, norm1_gain, norm1_bias, router_weight, query_weight, output_weight, key_value_weight, norm2_gain, norm2_bias, up_weight, up_bias, down_weight, down_bias, result_derivative_tokens):
    positions = jnp.arange(LENGTH, dtype=jnp.int32)
    allowed = visible(positions, positions, picture_start, picture_mode)

    def forward(inputs, gain_one, shift_one, router_matrix, query_matrix, output_mat, key_value_matrix, gain_two, shift_two, up_matrix, up_offset, down_matrix, down_shift):
        hidden_first = low(layer_norm(inputs, gain_one, shift_one))
        router_logits = jnp.einsum('cfz,zv->cfv', hidden_first, router_matrix, precision=highest_precision)
        first_hot, second_hot, first_gate, second_gate = gates_of(router_logits, expert_routes, E)
        gate_all = first_hot * first_gate[..., None] + second_hot * second_gate[..., None]
        query_rows_all = low(low_back(jnp.einsum('iok,ukm->iuom', hidden_first, query_matrix, precision=highest_precision)))
        key_value_pair = low(low_back(jnp.einsum('rwv,vk->rwk', hidden_first, key_value_matrix, precision=highest_precision)))
        attended = lax.map(jax.checkpoint(attend), (query_rows_all, key_value_pair, allowed))
        attended = low(low_back(attended))
        projected = low_back(jnp.einsum('selh,ehd->seld', attended, output_mat, precision=highest_precision))
        gate_rows = jnp.transpose(gate_all, (0, 2, 1))
        after_attention = inputs + lax.optimization_barrier(jnp.sum(gate_rows[..., None] * projected, axis=1))
        hidden_second = low(layer_norm(after_attention, gain_two, shift_two))
        before_activation = low_back(jnp.einsum('tjx,xe->tje', hidden_second, up_matrix, precision=highest_precision) + up_offset)
        active_rows = low(jax.nn.silu(before_activation))
        down_output = low_back(jnp.einsum('rct,tm->rcm', active_rows, down_matrix, precision=highest_precision))
        return after_attention + down_output + down_shift
    result, pullback = jax.vjp(forward, tokens.astype(jnp.float32), norm1_gain.astype(jnp.float32), norm1_bias.astype(jnp.float32), router_weight.astype(jnp.float32), query_weight.astype(jnp.float32), output_weight.astype(jnp.float32), key_value_weight.astype(jnp.float32), norm2_gain.astype(jnp.float32), norm2_bias.astype(jnp.float32), up_weight.astype(jnp.float32), up_bias.astype(jnp.float32), down_weight.astype(jnp.float32), down_bias.astype(jnp.float32))
    gradients = pullback(result_derivative_tokens.astype(jnp.float32))
    return (result.astype(jnp.bfloat16), gradients[0].astype(jnp.bfloat16), gradients[1], gradients[2], gradients[3], gradients[4], gradients[5], gradients[6], gradients[7], gradients[8], gradients[9], gradients[10], gradients[11], gradients[12])
```

```python
import functools
import math

import jax
import jax.numpy as jnp
from jax import lax
from jax.experimental import pallas as pl
from jax.experimental.pallas import tpu as pltpu
from jax.sharding import PartitionSpec as P

PIC = 256
TINY = 1e-05
NEG = -1e30
F32 = jnp.float32
BF16 = jnp.bfloat16
TQ = 256
TK = 256
BIG = 512
NT = (((1,), (1,)), ((), ()))
TN = (((0,), (0,)), ((), ()))
HIGH = lax.Precision.HIGHEST


def dot(a, b):
    return jnp.dot(a, b, preferred_element_type=F32)


def dot_nt(a, b):
    return lax.dot_general(a, b, NT, preferred_element_type=F32)


def dot_tn(a, b):
    return lax.dot_general(a, b, TN, preferred_element_type=F32)


def picture_starts(pic_ref, pics):
    return [jnp.where(pic_ref[1, k] == 1, pic_ref[0, k], -(1 << 20)) for k in range(pics)]


def mask_of(q0, k0, keys, queries, starts):
    key_pos = k0 + lax.broadcasted_iota(jnp.int32, (keys, 1), 0)
    query_pos = q0 + lax.broadcasted_iota(jnp.int32, (1, queries), 1)
    key_id = jnp.full((keys, 1), -2, jnp.int32)
    query_id = jnp.full((1, queries), -1, jnp.int32)
    for k, start in enumerate(starts):
        key_id = jnp.where((key_pos >= start) & (key_pos < start + PIC), k, key_id)
        query_id = jnp.where((query_pos >= start) & (query_pos < start + PIC), k, query_id)
    allowed = (key_pos <= query_pos) | (key_id == query_id)
    return jnp.concatenate([allowed, allowed], axis=1)


def key_tiles(q0, starts, length):
    whole = q0 // BIG
    last = q0 + TQ
    for start in starts:
        meets = (start < q0 + TQ) & (start + PIC > q0)
        last = jnp.maximum(last, jnp.where(meets, start + PIC, 0))
    last = jnp.minimum(last, length)
    return whole, whole * (BIG // TK), (last + TK - 1) // TK


def attend_forward(pos_ref, pic_ref, q_ref, kv_ref, att_ref, log_ref, top, total, acc, *, pics):
    length = kv_ref.shape[0]
    q0 = pos_ref[0] + pl.program_id(0) * TQ
    starts = picture_starts(pic_ref, pics)
    q = q_ref[...].reshape(2 * TQ, 128)
    top[...] = jnp.full_like(top, NEG)
    total[...] = jnp.zeros_like(total)
    acc[...] = jnp.zeros_like(acc)

    def step(k0, size, masked):
        kv = kv_ref[pl.ds(pl.multiple_of(k0, TK), size), :]
        scores = dot_nt(kv, q)
        if masked:
            scores = jnp.where(mask_of(q0, k0, size, TQ, starts), scores, NEG)
        before = top[...]
        now = jnp.maximum(before, jnp.max(scores, axis=0, keepdims=True))
        probs = jnp.exp(scores - now)
        scale = jnp.exp(before - now)
        top[...] = now
        total[...] = total[...] * scale + jnp.sum(probs, axis=0, keepdims=True)
        acc[...] = acc[...] * scale + dot_tn(kv, probs.astype(BF16))

    whole, low, high = key_tiles(q0, starts, length)

    @pl.loop(low, high)
    def _(j):
        step(j * TK, TK, True)

    @pl.loop(0, whole)
    def _(j):
        step(j * BIG, BIG, False)

    att = (acc[...] / total[...]).T
    att_ref[...] = att.reshape(2, TQ, 128)
    log_ref[0] = top[...] + jnp.log(total[...])


def attend_backward(
    pos_ref, pic_ref, q_ref, da_ref, log_ref, delta_ref, kv_ref, dq_ref, dkv_ref, acc, *, pics
):
    length = kv_ref.shape[0]
    q0 = pos_ref[0] + pl.program_id(0) * TQ
    starts = picture_starts(pic_ref, pics)
    q = q_ref[...].reshape(2 * TQ, 128)
    da = da_ref[...].reshape(2 * TQ, 128)
    log_total = log_ref[0]
    delta = delta_ref[0]

    @pl.when(pl.program_id(0) == 0)
    def _():
        dkv_ref[...] = jnp.zeros_like(dkv_ref)

    acc[...] = jnp.zeros_like(acc)

    def step(k0, size, masked):
        rows = pl.ds(pl.multiple_of(k0, TK), size)
        kv = kv_ref[rows, :]
        scores = dot_nt(kv, q)
        if masked:
            scores = jnp.where(mask_of(q0, k0, size, TQ, starts), scores, NEG)
        probs = jnp.exp(scores - log_total)
        prob_grad = dot_nt(kv, da)
        score_grad = (probs * (prob_grad - delta)).astype(BF16)
        dkv_ref[rows, :] += dot(score_grad, q) + dot(probs.astype(BF16), da)
        acc[...] += dot_tn(kv, score_grad)

    whole, low, high = key_tiles(q0, starts, length)

    @pl.loop(low, high)
    def _(j):
        step(j * TK, TK, True)

    @pl.loop(0, whole)
    def _(j):
        step(j * BIG, BIG, False)

    dq_ref[...] = (acc[...] * 0.125).T.reshape(2, TQ, 128)


SMEM = pl.BlockSpec(memory_space=pltpu.SMEM)
VMEM = pl.BlockSpec(memory_space=pltpu.VMEM)


def attention_forward(position, pictures, q_pad, kv):
    tokens = q_pad.shape[1]
    tiles = tokens // TQ
    return pl.pallas_call(
        functools.partial(attend_forward, pics=pictures.shape[1]),
        grid=(tiles,),
        in_specs=[SMEM, SMEM, pl.BlockSpec((2, TQ, 128), lambda i: (0, i, 0)), VMEM],
        out_specs=[
            pl.BlockSpec((2, TQ, 128), lambda i: (0, i, 0)),
            pl.BlockSpec((1, 1, 2 * TQ), lambda i: (i, 0, 0)),
        ],
        out_shape=[
            jax.ShapeDtypeStruct((2, tokens, 128), F32),
            jax.ShapeDtypeStruct((tiles, 1, 2 * TQ), F32),
        ],
        scratch_shapes=[
            pltpu.VMEM((1, 2 * TQ), F32),
            pltpu.VMEM((1, 2 * TQ), F32),
            pltpu.VMEM((128, 2 * TQ), F32),
        ],
        compiler_params=pltpu.CompilerParams(vmem_limit_bytes=40 << 20),
        name="attend_forward",
    )(position, pictures, q_pad, kv)


def attention_backward(position, pictures, q_pad, da_pad, log_total, delta, kv):
    tokens = q_pad.shape[1]
    tiles = tokens // TQ
    tile = pl.BlockSpec((2, TQ, 128), lambda i: (0, i, 0))
    line = pl.BlockSpec((1, 1, 2 * TQ), lambda i: (i, 0, 0))
    return pl.pallas_call(
        functools.partial(attend_backward, pics=pictures.shape[1]),
        grid=(tiles,),
        in_specs=[SMEM, SMEM, tile, tile, line, line, VMEM],
        out_specs=[tile, pl.BlockSpec(kv.shape, lambda i: (0, 0))],
        out_shape=[
            jax.ShapeDtypeStruct((2, tokens, 128), F32),
            jax.ShapeDtypeStruct(kv.shape, F32),
        ],
        scratch_shapes=[pltpu.VMEM((128, 2 * TQ), F32)],
        compiler_params=pltpu.CompilerParams(vmem_limit_bytes=40 << 20),
        name="attend_backward",
    )(position, pictures, q_pad, da_pad, log_total, delta, kv)


def layer_norm(values, gain, bias):
    center = values - jnp.mean(values, axis=-1, keepdims=True)
    inverse = lax.rsqrt(jnp.mean(center * center, axis=-1, keepdims=True) + TINY)
    normed = center * inverse
    return normed * gain + bias, normed, inverse


def norm_pullback(grad, normed, inverse, gain):
    scaled = grad * gain
    inner = (
        scaled
        - jnp.mean(scaled, axis=-1, keepdims=True)
        - normed * jnp.mean(scaled * normed, axis=-1, keepdims=True)
    )
    return inner * inverse, jnp.sum(grad * normed, axis=0), jnp.sum(grad, axis=0)


def pick(wide, route, experts):
    parts = wide.reshape(wide.shape[0], experts, -1)
    hot = route[:, None] == jnp.arange(experts, dtype=jnp.int32)
    return jnp.sum(jnp.where(hot[..., None], parts, 0), axis=1)


def spread(narrow, route, experts):
    hot = route[:, None] == jnp.arange(experts, dtype=jnp.int32)
    wide = jnp.where(hot[..., None], narrow[:, None, :], 0)
    return wide.reshape(narrow.shape[0], -1)


def gather2(shard):
    return lax.all_gather(lax.all_gather(shard, "fsdp", axis=0, tiled=True), "tp", axis=1, tiled=True)


def per_device(
    tokens,
    expert_routes,
    picture_start,
    picture_mode,
    norm1_gain,
    norm1_bias,
    router_weight,
    query_weight,
    output_weight,
    key_value_weight,
    norm2_gain,
    norm2_bias,
    up_weight,
    up_bias,
    down_weight,
    down_bias,
    upstream_tokens,
):
    sequences, block, width = tokens.shape
    tp_size = lax.axis_size("tp")
    subs = tp_size // sequences
    own = block // subs
    tp_rank = lax.axis_index("tp")
    sequence, sub = tp_rank // subs, tp_rank % subs
    position = lax.axis_index("ctx") * block + sub * own
    local_experts, rows_d, head = query_weight.shape
    experts = local_experts * tp_size

    def mine(array):
        return lax.dynamic_slice(
            array, (sequence, sub * own, 0), (1, own, array.shape[2])
        )[0]

    pictures = jnp.stack([picture_start, picture_mode])
    pictures = lax.dynamic_slice(
        pictures, (0, sequence, 0), (2, 1, pictures.shape[2])
    )[:, 0]
    inputs = mine(tokens).astype(F32)
    routes = mine(expert_routes)
    upstream_low = mine(upstream_tokens)
    upstream = upstream_low.astype(F32)

    wq = gather2(jnp.transpose(query_weight, (1, 0, 2)).reshape(rows_d, -1))
    shared = lax.all_gather(
        jnp.concatenate([key_value_weight, router_weight], axis=1), "fsdp", axis=0, tiled=True
    )
    wkv, router = shared[:, : 2 * head], shared[:, 2 * head :]
    wo = gather2(output_weight.reshape(local_experts * head, -1).T)
    up = gather2(up_weight)
    down = gather2(down_weight.T)
    up_shift = lax.all_gather(up_bias, "tp", axis=0, tiled=True).astype(F32)

    gain_one, gain_two = norm1_gain.astype(F32), norm2_gain.astype(F32)
    hidden, norm_one, inv_one = layer_norm(inputs, gain_one, norm1_bias.astype(F32))
    hidden1 = hidden.astype(BF16)
    pair = dot(hidden1, wkv).astype(BF16)
    kv = pair
    if subs > 1:
        by_tp = lax.all_gather(kv, "tp", axis=0, tiled=False)
        kv = lax.dynamic_slice_in_dim(by_tp, sequence * subs, subs, 0).reshape(block, -1)
    kv = lax.all_gather(kv, "ctx", axis=0, tiled=True)

    logits = dot(hidden1, router)
    r0, r1 = routes[:, 0], routes[:, 1]
    l0, l1 = pick(logits, r0, experts)[:, 0], pick(logits, r1, experts)[:, 0]
    top = jnp.maximum(l0, l1)
    e0, e1 = jnp.exp(l0 - top), jnp.exp(l1 - top)
    g0, g1 = e0 / (e0 + e1), e1 / (e0 + e1)

    queries = dot(hidden1, wq).astype(BF16)
    q = jnp.stack([pick(queries, r0, experts), pick(queries, r1, experts)])
    q_pad = jnp.pad(q * 0.125, ((0, 0), (0, 0), (0, head)))
    att, log_total = attention_forward(position[None], pictures, q_pad, kv)
    att = att[..., head:]
    att_low = att.astype(BF16)
    wide0, wide1 = spread(att_low[0], r0, experts), spread(att_low[1], r1, experts)
    projected0, projected1 = dot_nt(wide0, wo), dot_nt(wide1, wo)
    after = inputs + g0[:, None] * projected0 + g1[:, None] * projected1

    hidden, norm_two, inv_two = layer_norm(after, gain_two, norm2_bias.astype(F32))
    hidden2 = hidden.astype(BF16)
    pre = dot(hidden2, up) + up_shift
    sig = jax.nn.sigmoid(pre)
    active = (pre * sig).astype(BF16)
    result = (after + dot_nt(active, down) + down_bias.astype(F32)).astype(BF16)
    down_bias_grad = jnp.sum(upstream, axis=0)
    down_grad = dot_tn(upstream_low, active)
    act_grad = dot(upstream_low, down)
    pre_grad = (act_grad * sig * (1.0 + pre * (1.0 - sig))).astype(BF16)
    up_bias_grad = jnp.sum(pre_grad.astype(F32), axis=0)
    up_grad = dot_tn(hidden2, pre_grad)
    mid_grad = dot_nt(pre_grad, up)
    back_two, gain_two_grad, bias_two_grad = norm_pullback(mid_grad, norm_two, inv_two, gain_two)
    resid = upstream + back_two

    d0 = jnp.sum(projected0 * resid, axis=-1)
    d1 = jnp.sum(projected1 * resid, axis=-1)
    pg0 = (g0[:, None] * resid).astype(BF16)
    pg1 = (g1[:, None] * resid).astype(BF16)
    out_grad = dot_tn(pg0, wide0) + dot_tn(pg1, wide1)
    da = jnp.stack(
        [
            pick(dot(pg0, wo).astype(BF16), r0, experts),
            pick(dot(pg1, wo).astype(BF16), r1, experts),
        ]
    )
    mean = g0 * d0 + g1 * d1
    logit_grad = spread((g0 * (d0 - mean))[:, None], r0, experts) + spread(
        (g1 * (d1 - mean))[:, None], r1, experts
    )
    router_grad = lax.dot_general(hidden1.astype(F32), logit_grad, TN, precision=HIGH)
    router_back = lax.dot_general(logit_grad, router.astype(F32), NT, precision=HIGH)

    def scatter(grad, tp=True):
        if tp:
            grad = lax.psum_scatter(grad, "tp", scatter_dimension=1, tiled=True)
        grad = lax.psum_scatter(grad, "fsdp", scatter_dimension=0, tiled=True)
        return lax.psum(grad, "ctx" if tp else ("ctx", "tp"))

    up_out = scatter(up_grad)
    down_out = scatter(down_grad).T
    output_out = scatter(out_grad).T.reshape(output_weight.shape)

    delta = jnp.sum(da.astype(F32) * att, axis=-1)
    delta = delta.reshape(2, -1, TQ).transpose(1, 0, 2).reshape(-1, 1, 2 * TQ)
    da_pad = jnp.pad(da, ((0, 0), (0, 0), (head, 0)))
    dq, dkv = attention_backward(position[None], pictures, q_pad, da_pad, log_total, delta, kv)
    dq = dq[..., :head].astype(BF16)
    dkv = lax.psum_scatter(dkv, "ctx", scatter_dimension=0, tiled=True)
    if subs > 1:
        spot = jnp.zeros((tp_size,) + (own, dkv.shape[1]), F32)
        spot = lax.dynamic_update_slice(spot, dkv.reshape(subs, own, -1), (sequence * subs, 0, 0))
        dkv = lax.psum_scatter(spot, "tp", scatter_dimension=0, tiled=False)
    pair_grad = dkv.astype(BF16)
    dq_wide = spread(dq[0], r0, experts) + spread(dq[1], r1, experts)
    in_grad = dot_nt(dq_wide, wq) + router_back + dot_nt(pair_grad, wkv)
    back_one, gain_one_grad, bias_one_grad = norm_pullback(in_grad, norm_one, inv_one, gain_one)
    input_grad = (resid + back_one).astype(BF16)

    query_out = scatter(dot_tn(hidden1, dq_wide))
    query_out = query_out.reshape(rows_d, local_experts, head).transpose(1, 0, 2)
    shared_out = scatter(
        jnp.concatenate([dot_tn(hidden1, pair_grad), router_grad], axis=1), tp=False
    )
    pair_out, router_out = shared_out[:, : 2 * head], shared_out[:, 2 * head :]

    vectors = lax.psum(
        jnp.concatenate(
            [gain_one_grad, bias_one_grad, gain_two_grad, bias_two_grad, down_bias_grad, up_bias_grad]
        ),
        ("fsdp", "ctx", "tp"),
    )
    gain_one_sum, bias_one_sum, gain_two_sum, bias_two_sum, down_bias_sum, up_bias_sum = jnp.split(
        vectors, [width * (k + 1) for k in range(5)]
    )
    up_bias_sum = lax.dynamic_slice_in_dim(
        up_bias_sum, tp_rank * up_bias.shape[0], up_bias.shape[0], 0
    )

    def whole(array):
        parts = lax.all_gather(array, "tp", axis=0, tiled=True)
        return parts.reshape(sequences, block, width)

    return (
        whole(result),
        whole(input_grad),
        gain_one_sum,
        bias_one_sum,
        router_out,
        query_out,
        output_out,
        pair_out,
        gain_two_sum,
        bias_two_sum,
        up_out,
        up_bias_sum,
        down_out,
        down_bias_sum,
    )


def solution(mesh):
    rows = P("fsdp", "ctx", None)
    placed = (
        rows,
        rows,
        P("fsdp", None),
        P("fsdp", None),
        P(),
        P(),
        P("fsdp", None),
        P("tp", "fsdp", None),
        P("tp", None, "fsdp"),
        P("fsdp", None),
        P(),
        P(),
        P("fsdp", "tp"),
        P("tp"),
        P("tp", "fsdp"),
        P(),
        rows,
    )
    return jax.shard_map(
        per_device,
        mesh=mesh,
        in_specs=placed,
        out_specs=(
            rows,
            rows,
            P(),
            P(),
            P("fsdp", None),
            P("tp", "fsdp", None),
            P("tp", None, "fsdp"),
            P("fsdp", None),
            P(),
            P(),
            P("fsdp", "tp"),
            P("tp"),
            P("tp", "fsdp"),
            P(),
        ),
        check_vma=False,
    )
```

```python
import functools
import math

import jax
import jax.numpy as jnp
from jax import lax
from jax.experimental import pallas as pl
from jax.experimental.pallas import tpu as pltpu
from jax.sharding import PartitionSpec as P

PIC = 256
TINY = 1e-05
NEG = -1e30
F32 = jnp.float32
BF16 = jnp.bfloat16
TQ = 256
TK = 256
BIG = 512
NT = (((1,), (1,)), ((), ()))
TN = (((0,), (0,)), ((), ()))
HIGH = lax.Precision.HIGHEST


def dot(a, b):
    return jnp.dot(a, b, preferred_element_type=F32)


def dot_nt(a, b):
    return lax.dot_general(a, b, NT, preferred_element_type=F32)


def dot_tn(a, b):
    return lax.dot_general(a, b, TN, preferred_element_type=F32)


def picture_starts(pic_ref, pics):
    return [jnp.where(pic_ref[1, k] == 1, pic_ref[0, k], -(1 << 20)) for k in range(pics)]


def mask_of(q0, k0, keys, queries, starts):
    key_pos = k0 + lax.broadcasted_iota(jnp.int32, (keys, 1), 0)
    query_pos = q0 + lax.broadcasted_iota(jnp.int32, (1, queries), 1)
    key_id = jnp.full((keys, 1), -2, jnp.int32)
    query_id = jnp.full((1, queries), -1, jnp.int32)
    for k, start in enumerate(starts):
        key_id = jnp.where((key_pos >= start) & (key_pos < start + PIC), k, key_id)
        query_id = jnp.where((query_pos >= start) & (query_pos < start + PIC), k, query_id)
    allowed = (key_pos <= query_pos) | (key_id == query_id)
    return jnp.concatenate([allowed, allowed], axis=1)


def key_tiles(q0, starts, length):
    whole = q0 // BIG
    last = q0 + TQ
    for start in starts:
        meets = (start < q0 + TQ) & (start + PIC > q0)
        last = jnp.maximum(last, jnp.where(meets, start + PIC, 0))
    last = jnp.minimum(last, length)
    return whole, whole * (BIG // TK), (last + TK - 1) // TK


def attend_forward(pos_ref, pic_ref, q_ref, kv_ref, att_ref, log_ref, top, total, acc, *, pics):
    length = kv_ref.shape[0]
    q0 = pos_ref[0] + pl.program_id(0) * TQ
    starts = picture_starts(pic_ref, pics)
    q = q_ref[...].reshape(2 * TQ, 128)
    top[...] = jnp.full_like(top, NEG)
    total[...] = jnp.zeros_like(total)
    acc[...] = jnp.zeros_like(acc)

    def step(k0, size, masked):
        kv = kv_ref[pl.ds(pl.multiple_of(k0, TK), size), :]
        scores = dot_nt(kv, q)
        if masked:
            scores = jnp.where(mask_of(q0, k0, size, TQ, starts), scores, NEG)
        before = top[...]
        now = jnp.maximum(before, jnp.max(scores, axis=0, keepdims=True))
        probs = jnp.exp(scores - now)
        scale = jnp.exp(before - now)
        top[...] = now
        total[...] = total[...] * scale + jnp.sum(probs, axis=0, keepdims=True)
        acc[...] = acc[...] * scale + dot_tn(kv, probs.astype(BF16))

    whole, low, high = key_tiles(q0, starts, length)

    @pl.loop(low, high)
    def _(j):
        step(j * TK, TK, True)

    @pl.loop(0, whole)
    def _(j):
        step(j * BIG, BIG, False)

    att = (acc[...] / total[...]).T
    att_ref[...] = att.reshape(2, TQ, 128)
    log_ref[0] = top[...] + jnp.log(total[...])


SMEM = pl.BlockSpec(memory_space=pltpu.SMEM)
VMEM = pl.BlockSpec(memory_space=pltpu.VMEM)
ANY = pl.BlockSpec(memory_space=pl.ANY)
MESH = pl.DeviceIdType.MESH


def attention_forward(position, pictures, q_pad, kv):
    tokens = q_pad.shape[1]
    tiles = tokens // TQ
    return pl.pallas_call(
        functools.partial(attend_forward, pics=pictures.shape[1]),
        grid=(tiles,),
        in_specs=[SMEM, SMEM, pl.BlockSpec((2, TQ, 128), lambda i: (0, i, 0)), VMEM],
        out_specs=[
            pl.BlockSpec((2, TQ, 128), lambda i: (0, i, 0)),
            pl.BlockSpec((1, 1, 2 * TQ), lambda i: (i, 0, 0)),
        ],
        out_shape=[
            jax.ShapeDtypeStruct((2, tokens, 128), F32),
            jax.ShapeDtypeStruct((tiles, 1, 2 * TQ), F32),
        ],
        scratch_shapes=[
            pltpu.VMEM((1, 2 * TQ), F32),
            pltpu.VMEM((1, 2 * TQ), F32),
            pltpu.VMEM((128, 2 * TQ), F32),
        ],
        compiler_params=pltpu.CompilerParams(vmem_limit_bytes=40 << 20),
        name="attend_forward",
    )(position, pictures, q_pad, kv)


def remote(src, dst, send, recv, to):
    return pltpu.make_async_remote_copy(
        src_ref=src, dst_ref=dst, send_sem=send, recv_sem=recv, device_id=to, device_id_type=MESH
    )


class Place:
    def __init__(self, sizes, sequences):
        self.fsdp, self.ctx, self.tp = sizes
        self.subs = self.tp // sequences
        self.blocks = self.ctx * self.subs
        self.f, self.x, self.t = (lax.axis_index(a) for a in ("fsdp", "ctx", "tp"))
        self.seq, self.sub = self.t // self.subs, self.t % self.subs
        self.block = self.x * self.subs + self.sub

    def owner(self, block):
        return {"ctx": block // self.subs, "tp": self.seq * self.subs + block % self.subs}

    def barrier(self):
        semaphore = pltpu.get_barrier_semaphore()
        count = 0
        for axis, size, me in (("fsdp", self.fsdp, self.f), ("ctx", self.ctx, self.x), ("tp", self.tp, self.t)):
            for r in range(1, size):
                pl.semaphore_signal(
                    semaphore, inc=1, device_id={axis: lax.rem(me + r, size)}, device_id_type=MESH
                )
                count += 1
        if self.subs > 1:
            for r in range(1, self.blocks):
                pl.semaphore_signal(
                    semaphore,
                    inc=1,
                    device_id=self.owner(lax.rem(self.block + r, self.blocks)),
                    device_id_type=MESH,
                )
                count += 1
        pl.semaphore_wait(semaphore, count)


class Reduce:
    def __init__(self, k, w, n, d, sizes, tp=True):
        self.k, self.w, self.n, self.d, self.sizes, self.tp = k, w, n, d, sizes, tp
        fsdp, ctx, tps = sizes
        self.rows, self.part = d // fsdp, d // fsdp // ctx
        self.count = 16 if tp else 15

    def scratch(self):
        k, w, n, d = self.k, self.w, self.n, self.d
        fsdp, ctx, tps = self.sizes
        dma = pltpu.SemaphoreType.DMA
        shapes = [
            pltpu.VMEM((n, k, d, w), BF16),
            pltpu.VMEM((n, fsdp - 1, k, self.rows, w), BF16),
            pltpu.VMEM((n, k, self.rows, w), F32),
            pltpu.VMEM((n, k, self.rows, w), BF16),
            pltpu.VMEM((n, ctx - 1, k, self.part, w), BF16),
            pltpu.VMEM((n, k, self.rows, w), BF16),
            dma((n, fsdp - 1)),
            dma((n, fsdp - 1)),
            dma((n, ctx - 1)),
            dma((n, ctx - 1)),
            dma((n, ctx - 1)),
            dma((n, ctx - 1)),
        ]
        if self.tp:
            shapes += [
                pltpu.VMEM((tps - 1, n, k, d, w), BF16),
                pltpu.VMEM((tps - 1, n, k, d, w), BF16),
                dma((tps - 1, n)),
                dma((tps - 1, n)),
            ]
        else:
            shapes += [pltpu.VMEM((tps, k, self.rows, w), F32), dma((tps - 1,)), dma((tps - 1,))]
        return shapes

    def bind(self, place, refs):
        self.place = place
        self.s2, self.r2, self.own, self.s3, self.r3, self.fin = refs[:6]
        self.m2, self.m3, self.m4 = refs[6:8], refs[8:10], refs[10:12]
        if self.tp:
            self.s1, self.r1 = refs[12:14]
            self.m1 = refs[14:16]
        else:
            self.all, self.m1 = refs[12], refs[13:15]

    def d1(self, o, c):
        p = self.place
        to = {"tp": lax.rem(p.t + o, p.tp)}
        if self.tp:
            return remote(
                self.s1.at[o - 1, c], self.r1.at[o - 1, c], self.m1[0].at[o - 1, c], self.m1[1].at[o - 1, c], to
            )
        return remote(self.all.at[p.t], self.all.at[p.t], self.m1[0].at[o - 1], self.m1[1].at[o - 1], to)

    def d2(self, r, c):
        p = self.place
        to = lax.rem(p.f + r, p.fsdp)
        rows = pl.ds(pl.multiple_of(to * self.rows, self.rows), self.rows)
        return remote(
            self.s2.at[c, :, rows, :],
            self.r2.at[c, r - 1],
            self.m2[0].at[c, r - 1],
            self.m2[1].at[c, r - 1],
            {"fsdp": to},
        )

    def spot(self, x):
        return pl.ds(pl.multiple_of(x * self.part, self.part), self.part)

    def d3(self, q, c):
        p = self.place
        to = lax.rem(p.x + q, p.ctx)
        return remote(
            self.s3.at[c, :, self.spot(to), :],
            self.r3.at[c, q - 1],
            self.m3[0].at[c, q - 1],
            self.m3[1].at[c, q - 1],
            {"ctx": to},
        )

    def d4(self, q, c):
        p = self.place
        to = lax.rem(p.x + q, p.ctx)
        mine = self.fin.at[c, :, self.spot(p.x), :]
        return remote(mine, mine, self.m4[0].at[c, q - 1], self.m4[1].at[c, q - 1], {"ctx": to})

    def put(self, o, c, k, value):
        self.s1[o - 1, c, k] = value.astype(BF16)

    def give(self, o, c):
        self.d1(o, c).start()

    def take(self, c, acc):
        p, w = self.place, self.w
        if self.tp:
            for o in range(1, p.tp):
                self.d1(o, c).wait_recv()
            for k in range(self.k):
                total = acc[k, :, 0:w]
                for o in range(1, p.tp):
                    total = total + self.r1[o - 1, c, k].astype(F32)
                acc[k, :, 0:w] = total
        for k in range(self.k):
            self.s2[c, k] = acc[k, :, 0:w].astype(BF16)
        for r in range(1, p.fsdp):
            self.d2(r, c).start()
        for k in range(self.k):
            self.own[c, k] = acc[k, pl.ds(pl.multiple_of(p.f * self.rows, self.rows), self.rows), 0:w]

    def fold(self, c):
        p = self.place
        for r in range(1, p.fsdp):
            self.d2(r, c).wait_recv()
        for k in range(self.k):
            total = self.own[c, k]
            for r in range(1, p.fsdp):
                total = total + self.r2[c, r - 1, k].astype(F32)
            if self.tp:
                self.own[c, k] = total
                self.s3[c, k] = total.astype(BF16)
            else:
                self.all[p.t, k] = total
        if self.tp:
            for q in range(1, p.ctx):
                self.d3(q, c).start()
        else:
            for o in range(1, p.tp):
                self.d1(o, c).start()

    def share(self, c):
        p = self.place
        for o in range(1, p.tp):
            self.d1(o, c).wait_recv()
        for k in range(self.k):
            total = self.all[0, k]
            for o in range(1, p.tp):
                total = total + self.all[o, k]
            self.own[c, k] = total
            self.s3[c, k] = total.astype(BF16)
        for q in range(1, p.ctx):
            self.d3(q, c).start()

    def finish(self, c):
        p = self.place
        for q in range(1, p.ctx):
            self.d3(q, c).wait_recv()
        for k in range(self.k):
            total = self.own[c, k, self.spot(p.x), :]
            for q in range(1, p.ctx):
                total = total + self.r3[c, q - 1, k].astype(F32)
            self.fin[c, k, self.spot(p.x), :] = total.astype(BF16)
        for q in range(1, p.ctx):
            self.d4(q, c).start()

    def close(self):
        p = self.place

        @pl.loop(0, self.n)
        def _(c):
            for q in range(1, p.ctx):
                self.d4(q, c).wait()
                self.d3(q, c).wait_send()
            for r in range(1, p.fsdp):
                self.d2(r, c).wait_send()
            for o in range(1, p.tp):
                self.d1(o, c).wait_send()


class Everywhere:
    def __init__(self, shape, sizes):
        self.shape, self.sizes, self.count = shape, sizes, 9

    def scratch(self):
        dma = pltpu.SemaphoreType.DMA
        shapes = []
        for size in self.sizes:
            shapes += [pltpu.VMEM((size,) + self.shape, F32), dma((size - 1,)), dma((size - 1,))]
        return shapes

    def bind(self, place, refs):
        self.place, self.refs = place, refs

    def copy(self, stage, r):
        p = self.place
        axis, size, me = (
            ("fsdp", p.fsdp, p.f),
            ("ctx", p.ctx, p.x),
            ("tp", p.tp, p.t),
        )[stage]
        buf, send, recv = self.refs[3 * stage : 3 * stage + 3]
        return remote(
            buf.at[me], buf.at[me], send.at[r - 1], recv.at[r - 1], {axis: lax.rem(me + r, size)}
        )

    def start(self, stage, value):
        p = self.place
        me = (p.f, p.x, p.t)[stage]
        self.refs[3 * stage][me] = value
        for r in range(1, self.sizes[stage]):
            self.copy(stage, r).start()

    def total(self, stage):
        buf = self.refs[3 * stage]
        for r in range(1, self.sizes[stage]):
            self.copy(stage, r).wait()
        total = buf[0]
        for r in range(1, self.sizes[stage]):
            total = total + buf[r]
        return total


def norm_back(grad, normed, inverse, gain):
    scaled = grad * gain
    inner = (
        scaled
        - jnp.mean(scaled, axis=-1, keepdims=True)
        - normed * jnp.mean(scaled * normed, axis=-1, keepdims=True)
    )
    return inner * inverse


def half_lanes(rows):
    return lax.broadcasted_iota(jnp.int32, (rows, 128), 1)


def both_halves(values, upper):
    low = half_lanes(values.shape[0]) < 64
    turned = pltpu.roll(values, 64, 1)
    return jnp.where(low, turned, values) if upper else jnp.where(low, values, turned)


def back_kernel(dims, *refs):
    (sizes, sequences, tokens, width, hidden_units, experts, pics, length, reducers) = dims
    fsdp, ctx, tps = sizes
    r_ud, r_wo, r_wq, r_kr, r_vec, r_bias = reducers
    place = Place(sizes, sequences)
    tiles = tokens // TQ
    cw, chunks = r_ud.w, r_ud.n
    rows_t = min(512, tokens)
    big = min(BIG, tokens)
    (
        pic_ref,
        tok,
        ups,
        meta,
        hid1,
        q_ref,
        kv_in,
        att,
        logt,
        wq,
        wkv,
        router,
        wo,
        up,
        down,
        up_bias,
        rows_in,
        out_hbm,
        grad_hbm,
        ud_out,
        wo_out,
        wq_out,
        kr_out,
        vec_out,
        bias_out,
        kv,
        wide,
        proj,
        normed2,
        hid2,
        out_acc,
        mid,
        inv2,
        gacc,
        woacc,
        pg,
        da,
        delta,
        lgp,
        dqt,
        dkv,
        dkv_send,
        dkv_recv,
        dqw,
        pairg,
        vec,
        bias_acc,
        res_low,
        grad_low,
        dkv_ssem,
        dkv_rsem,
        near_buf,
        near_send,
        near_ssem,
        near_rsem,
        loc_sem,
        out_ssem,
        out_rsem,
        *rest,
    ) = refs
    for reducer in reducers:
        reducer.bind(place, rest[: reducer.count])
        rest = rest[reducer.count :]

    place.barrier()
    gain1, gain2, bias2, down_bias = (rows_in[k : k + 1, :] for k in range(4))
    q_base = place.block * tokens
    starts = picture_starts(pic_ref, pics)
    lanes = half_lanes(TQ)

    def tile_rows(i):
        return pl.ds(pl.multiple_of(i * TQ, TQ), TQ)

    def gates(rows):
        return [meta[rows, k : k + 1] for k in range(4)]

    def expert_of(c):
        return 2 * c + jnp.where(lanes >= 64, 1, 0)

    vec[...] = jnp.zeros_like(vec)
    bias_acc[...] = jnp.zeros_like(bias_acc)
    woacc[...] = jnp.zeros_like(woacc)
    kv[pl.ds(0, length), :] = kv_in[...]
    kv[pl.ds(length, TQ), :] = jnp.zeros((TQ, 128), BF16)

    @pl.loop(0, tiles)
    def _(i):
        rows = tile_rows(i)
        g0, g1, r0, r1 = gates(rows)
        after = tok[rows, :].astype(F32)
        for s, (g, r) in enumerate(((g0, r0), (g1, r1))):
            twice = both_halves(att[s, rows, :], True)
            expert = r.astype(jnp.int32)
            for c in range(experts // 2):
                wide[s, rows, c * 128 : (c + 1) * 128] = jnp.where(expert == expert_of(c), twice, 0.0).astype(BF16)
            projected = dot(wide[s, rows, :], wo[...])
            proj[s, rows, :] = projected
            after = after + g * projected
        center = after - jnp.mean(after, axis=-1, keepdims=True)
        inverse = lax.rsqrt(jnp.mean(center * center, axis=-1, keepdims=True) + TINY)
        normed = center * inverse
        normed2[rows, :] = normed
        inv2[rows, :] = inverse
        hid2[rows, :] = (normed * gain2 + bias2).astype(BF16)
        out_acc[rows, :] = after + down_bias
        mid[rows, :] = jnp.zeros_like(after)

    def feed(t, c):
        cols = pl.ds(pl.multiple_of(c * cw, cw), cw)
        gacc[...] = jnp.zeros_like(gacc)

        @pl.loop(0, tokens // rows_t)
        def _(i):
            rows = pl.ds(pl.multiple_of(i * rows_t, rows_t), rows_t)
            h2, u = hid2[rows, :], ups[rows, :]
            pre = dot(h2, up[t, :, cols]) + up_bias[t, :, cols]
            sig = 1.0 / (1.0 + jnp.exp(-pre))
            active = (pre * sig).astype(BF16)
            out_acc[rows, :] += dot(active, down[t, cols, :])
            gacc[1] += dot_tn(u, active)
            slope = sig * (1.0 + pre * (1.0 - sig))
            grad = dot_nt(u, down[t, cols, :]) * slope
            low = grad.astype(BF16)
            bias_acc[t * chunks + c] += jnp.sum(low.astype(F32), axis=0, keepdims=True)
            gacc[0] += dot_tn(h2, low)
            mid[rows, :] += dot_nt(low, up[t, :, cols])

    for o in range(1, tps):

        @pl.loop(0, chunks)
        def _(c):
            feed(lax.rem(place.t + o, tps), c)
            for k in range(2):
                r_ud.put(o, c, k, gacc[k])
            r_ud.give(o, c)

    @pl.loop(0, chunks)
    def _(c):
        feed(place.t, c)
        r_ud.take(c, gacc)

    def local_out(low, hbm, slot):
        spot = hbm.at[place.seq, pl.ds(place.sub * tokens, tokens), :]
        copies = [
            remote(low, spot, out_ssem.at[slot, o - 1], out_rsem.at[slot, o - 1], {"tp": lax.rem(place.t + o, tps)})
            for o in range(1, tps)
        ]
        return pltpu.make_async_copy(low, spot, loc_sem.at[slot]), copies

    def add_row(k, value):
        vec[k : k + 1, :] += jnp.sum(value, axis=0, keepdims=True)

    @pl.loop(0, tiles)
    def _(i):
        rows = tile_rows(i)
        g0, g1, r0, r1 = gates(rows)
        res_low[rows, :] = out_acc[rows, :].astype(BF16)
        upstream = ups[rows, :].astype(F32)
        grad, normed = mid[rows, :], normed2[rows, :]
        resid = upstream + norm_back(grad, normed, inv2[rows, :], gain2)
        mid[rows, :] = resid
        add_row(2, grad * normed)
        add_row(3, grad)
        add_row(4, upstream)
        d0 = jnp.sum(proj[0, rows, :] * resid, axis=-1, keepdims=True)
        d1 = jnp.sum(proj[1, rows, :] * resid, axis=-1, keepdims=True)
        mean = g0 * d0 + g1 * d1
        for s, (g, r) in enumerate(((g0, r0), (g1, r1))):
            low = (g * resid).astype(BF16)
            woacc[0] += dot_tn(low, wide[s, rows, :])
            full = dot_nt(low, wo[...])
            expert = r.astype(jnp.int32)
            chosen = jnp.zeros((TQ, 128), F32)
            for c in range(experts // 2):
                chosen = jnp.where(expert == expert_of(c), full[:, c * 128 : (c + 1) * 128], chosen)
            chosen = jnp.where(lanes >= 64, chosen + pltpu.roll(chosen, 64, 1), 0.0).astype(BF16)
            da[s, rows, :] = chosen
            product = chosen.astype(F32) * jnp.where(lanes >= 64, att[s, rows, :], 0.0)
            delta[i, :, s * TQ : (s + 1) * TQ] = jnp.sum(product.T, axis=0, keepdims=True)
        lane_expert = lax.rem(lanes, experts)
        lg = jnp.where(lane_expert == r0.astype(jnp.int32), g0 * (d0 - mean), 0.0)
        lg = lg + jnp.where(lane_expert == r1.astype(jnp.int32), g1 * (d1 - mean), 0.0)
        high = lg.astype(BF16)
        rest_of = (lg - high.astype(F32)).astype(BF16)
        lgp[rows, :] = jnp.where(
            lanes < experts, high.astype(F32), jnp.where(lanes < 2 * experts, rest_of.astype(F32), 0.0)
        ).astype(BF16)

    own_copy, out_copies = local_out(res_low, out_hbm, 0)
    own_copy.start()
    for copy in out_copies:
        copy.start()

    def hand_out(reducer, acc):
        w = reducer.w
        for t in range(tps):

            @pl.when(t != place.t)
            def _():
                o = lax.rem(t - place.t + tps, tps)
                reducer.s1[o - 1, 0, 0] = acc[0, :, t * w : (t + 1) * w].astype(BF16)
                reducer.give(o, 0)

    def take_own(reducer, acc):
        w = reducer.w
        for t in range(tps):

            @pl.when(t == place.t)
            def _():
                gacc[0, :, 0:w] = acc[0, :, t * w : (t + 1) * w]

        reducer.take(0, gacc)

    hand_out(r_wo, woacc)

    dqt[...] = jnp.zeros_like(dqt)
    dkv[...] = jnp.zeros_like(dkv)

    def attend(i, k0, size, masked):
        rows = tile_rows(i)
        keys = pl.ds(pl.multiple_of(k0, TK), size)
        q = jnp.concatenate([q_ref[0, rows, :], q_ref[1, rows, :]], axis=0)
        d_att = jnp.concatenate([da[0, rows, :], da[1, rows, :]], axis=0)
        pair = kv[keys, :]
        scores = dot_nt(pair, q)
        if masked:
            scores = jnp.where(mask_of(q_base + i * TQ, k0, size, TQ, starts), scores, NEG)
        probs = jnp.exp(scores - logt[i])
        prob_grad = dot_nt(pair, d_att)
        score_grad = (probs * (prob_grad - delta[i])).astype(BF16)
        dkv[keys, :] += dot(score_grad, q) + dot(probs.astype(BF16), d_att)
        dqt[i] += dot_tn(pair, score_grad)

    def dkv_copy(block):
        slot = place.block - block - 1
        return remote(
            dkv_send.at[block],
            dkv_recv.at[slot],
            dkv_ssem.at[slot],
            dkv_rsem.at[slot],
            place.owner(block),
        )

    @pl.loop(0, place.blocks - 1)
    def _(j):
        @pl.when(j < place.block)
        def _():
            @pl.loop(0, tokens // big)
            def _(k):
                @pl.loop(0, tiles)
                def _(i):
                    attend(i, j * tokens + k * big, big, False)

            dkv_send[j] = dkv[pl.ds(pl.multiple_of(j * tokens, tokens), tokens), :].astype(BF16)
            dkv_copy(j).start()

        @pl.when(j < chunks)
        def _():
            r_ud.fold(j)

        if place.blocks > 2:

            @pl.when((j > 0) & (j < chunks + 1))
            def _():
                r_ud.finish(j - 1)

    done = place.blocks - 1
    take_own(r_wo, woacc)

    @pl.loop(0, tiles)
    def _(i):
        @pl.loop(0, i)
        def _(k):
            attend(i, q_base + k * TK, TK, False)

        attend(i, q_base + i * TK, TK, True)
        attend(i, q_base + (i + 1) * TK, TK, True)

    def near_copy():
        return remote(
            near_send, near_buf, near_ssem, near_rsem, place.owner(lax.rem(place.block + 1, place.blocks))
        )

    @pl.when(place.block + 1 < place.blocks)
    def _():
        near_send[...] = dkv[pl.ds(pl.multiple_of((place.block + 1) * tokens, TQ), TQ), :].astype(BF16)
        near_copy().start()

    for c in range(min(done, chunks), chunks):
        r_ud.fold(c)
    for c in range(max(min(done, chunks + 1) - 1, 0), chunks):
        r_ud.finish(c)
    r_wo.fold(0)

    @pl.loop(0, tiles)
    def _(i):
        rows = tile_rows(i)
        _, _, r0, r1 = gates(rows)
        dq = (dqt[i] * 0.125).T
        first, second = both_halves(dq[:TQ], False), both_halves(dq[TQ:], False)
        for c in range(experts // 2):
            column = jnp.where(r0.astype(jnp.int32) == expert_of(c), first, 0.0)
            column = jnp.where(r1.astype(jnp.int32) == expert_of(c), second, column)
            dqw[rows, c * 128 : (c + 1) * 128] = column.astype(BF16)

    woacc[0] = dot_tn(hid1[...], dqw[...])
    hand_out(r_wq, woacc)
    take_own(r_wq, woacc)
    r_wo.finish(0)

    own_rows = pl.ds(pl.multiple_of(q_base, tokens), tokens)

    @pl.loop(0, place.blocks - 1 - place.block)
    def _(slot):
        remote(
            dkv_send.at[0], dkv_recv.at[slot], dkv_ssem.at[slot], dkv_rsem.at[slot], place.owner(place.block)
        ).wait_recv()
        dkv[own_rows, :] += dkv_recv[slot].astype(F32)

    @pl.when(place.block > 0)
    def _():
        near_copy().wait_recv()
        dkv[pl.ds(pl.multiple_of(q_base, tokens), TQ), :] += near_buf[...].astype(F32)

    pairg[:, 0:128] = dkv[own_rows, :].astype(BF16)
    pairg[:, 128:256] = lgp[...]
    gacc[0, :, 0:256] = dot_tn(hid1[...], pairg[...])
    r_kr.take(0, gacc)
    r_wq.fold(0)

    @pl.loop(0, tiles)
    def _(i):
        rows = tile_rows(i)
        x = tok[rows, :].astype(F32)
        center = x - jnp.mean(x, axis=-1, keepdims=True)
        inverse = lax.rsqrt(jnp.mean(center * center, axis=-1, keepdims=True) + TINY)
        normed = center * inverse
        grad = (
            dot_nt(dqw[rows, :], wq[...])
            + dot_nt(pairg[rows, 0:128], wkv[...])
            + dot_nt(pairg[rows, 128:256], router[...])
        )
        add_row(0, grad * normed)
        add_row(1, grad)
        grad_low[rows, :] = (mid[rows, :] + norm_back(grad, normed, inverse, gain1)).astype(BF16)

    own_grad, grad_copies = local_out(grad_low, grad_hbm, 1)
    own_grad.start()
    for copy in grad_copies:
        copy.start()
    r_vec.start(2, vec[...])
    r_bias.start(2, bias_acc[...])
    r_kr.fold(0)
    r_wq.finish(0)
    r_vec.start(0, r_vec.total(2))
    r_bias.start(0, r_bias.total(2))
    r_kr.share(0)
    r_vec.start(1, r_vec.total(0))
    r_bias.start(1, r_bias.total(0))
    r_kr.finish(0)
    vec_out[...] = r_vec.total(1)
    bias_out[...] = r_bias.total(1)
    for reducer, out in ((r_ud, ud_out), (r_wo, wo_out), (r_wq, wq_out), (r_kr, kr_out)):
        reducer.close()
        out[...] = reducer.fin[...]

    @pl.loop(0, place.block)
    def _(j):
        dkv_copy(j).wait_send()

    @pl.when(place.block + 1 < place.blocks)
    def _():
        near_copy().wait_send()

    own_copy.wait()
    own_grad.wait()
    for copy in out_copies + grad_copies:
        copy.wait()


def run_back(sizes, sequences, shape, experts, hidden_units, pictures, arrays):
    tokens, width = arrays[0].shape
    length = arrays[5].shape[0]
    fsdp, ctx, tps = sizes
    subs = tps // sequences
    blocks = ctx * subs
    tiles = tokens // TQ
    cw = min(256, hidden_units // tps)
    chunks = hidden_units // tps // cw
    w = width // tps
    reducers = (
        Reduce(2, cw, chunks, width, sizes),
        Reduce(1, w, 1, width, sizes),
        Reduce(1, w, 1, width, sizes),
        Reduce(1, 256, 1, width, sizes, tp=False),
        Everywhere((8, width), sizes),
        Everywhere((tps * chunks, 1, cw), sizes),
    )
    dims = (sizes, sequences, tokens, width, hidden_units, experts, pictures.shape[1], length, reducers)
    rows = width // fsdp
    dma = pltpu.SemaphoreType.DMA
    scratch = [
        pltpu.VMEM((length + TQ, 128), BF16),
        pltpu.VMEM((2, tokens, width), BF16),
        pltpu.VMEM((2, tokens, width), F32),
        pltpu.VMEM((tokens, width), F32),
        pltpu.VMEM((tokens, width), BF16),
        pltpu.VMEM((tokens, width), F32),
        pltpu.VMEM((tokens, width), F32),
        pltpu.VMEM((tokens, 1), F32),
        pltpu.VMEM((2, width, max(cw, 256)), F32),
        pltpu.VMEM((1, width, width), F32),
        pltpu.VMEM((8, 128), F32),
        pltpu.VMEM((2, tokens, 128), BF16),
        pltpu.VMEM((tiles, 1, 2 * TQ), F32),
        pltpu.VMEM((tokens, 128), BF16),
        pltpu.VMEM((tiles, 128, 2 * TQ), F32),
        pltpu.VMEM((length + TQ, 128), F32),
        pltpu.VMEM((blocks - 1, tokens, 128), BF16),
        pltpu.VMEM((blocks - 1, tokens, 128), BF16),
        pltpu.VMEM((tokens, width), BF16),
        pltpu.VMEM((tokens, 256), BF16),
        pltpu.VMEM((8, width), F32),
        pltpu.VMEM((tps * chunks, 1, cw), F32),
        pltpu.VMEM((tokens, width), BF16),
        pltpu.VMEM((tokens, width), BF16),
        dma((blocks - 1,)),
        dma((blocks - 1,)),
        pltpu.VMEM((TQ, 128), BF16),
        pltpu.VMEM((TQ, 128), BF16),
        dma(()),
        dma(()),
        dma((2,)),
        dma((2, tps - 1)),
        dma((2, tps - 1)),
    ]
    for reducer in reducers:
        scratch += reducer.scratch()
    return pl.pallas_call(
        functools.partial(back_kernel, dims),
        in_specs=[SMEM] + [VMEM] * len(arrays),
        out_specs=[ANY, ANY] + [VMEM] * 6,
        out_shape=[
            jax.ShapeDtypeStruct(shape, BF16),
            jax.ShapeDtypeStruct(shape, BF16),
            jax.ShapeDtypeStruct((chunks, 2, rows, cw), BF16),
            jax.ShapeDtypeStruct((1, 1, rows, w), BF16),
            jax.ShapeDtypeStruct((1, 1, rows, w), BF16),
            jax.ShapeDtypeStruct((1, 1, rows, 256), BF16),
            jax.ShapeDtypeStruct((8, width), F32),
            jax.ShapeDtypeStruct((tps * chunks, 1, cw), F32),
        ],
        scratch_shapes=scratch,
        compiler_params=pltpu.CompilerParams(
            vmem_limit_bytes=62 << 20, collective_id=1, has_side_effects=True
        ),
        name="back",
    )(pictures, *arrays)


def pick(wide, route, experts):
    parts = wide.reshape(wide.shape[0], experts, -1)
    hot = route[:, None] == jnp.arange(experts, dtype=jnp.int32)
    return jnp.sum(jnp.where(hot[..., None], parts, 0), axis=1)


def gather2(shard, rows=0):
    part = lax.all_gather(shard, "fsdp", axis=rows, tiled=True)
    return lax.all_gather(part, "tp", axis=1 - rows, tiled=True)


def per_device(
    mesh_sizes,
    tokens,
    expert_routes,
    picture_start,
    picture_mode,
    norm1_gain,
    norm1_bias,
    router_weight,
    query_weight,
    output_weight,
    key_value_weight,
    norm2_gain,
    norm2_bias,
    up_weight,
    up_bias,
    down_weight,
    down_bias,
    upstream_tokens,
):
    sequences, block, width = tokens.shape
    tp_size = lax.axis_size("tp")
    subs = tp_size // sequences
    own = block // subs
    tp_rank = lax.axis_index("tp")
    sequence, sub = tp_rank // subs, tp_rank % subs
    position = lax.axis_index("ctx") * block + sub * own
    local_experts, rows_d, head = query_weight.shape
    experts = local_experts * tp_size

    def mine(array):
        return lax.dynamic_slice(
            array, (sequence, sub * own, 0), (1, own, array.shape[2])
        )[0]

    pictures = jnp.stack([picture_start, picture_mode])
    pictures = lax.dynamic_slice(
        pictures, (0, sequence, 0), (2, 1, pictures.shape[2])
    )[:, 0]
    low_inputs = mine(tokens)
    inputs = low_inputs.astype(F32)
    routes = mine(expert_routes)

    wq = gather2(jnp.transpose(query_weight, (1, 0, 2)).reshape(rows_d, -1))
    shared = lax.all_gather(
        jnp.concatenate([key_value_weight, router_weight], axis=1), "fsdp", axis=0, tiled=True
    )
    wkv, router = shared[:, : 2 * head], shared[:, 2 * head :]
    wo = gather2(output_weight.reshape(local_experts * head, -1), 1)
    up = lax.all_gather(lax.all_gather(up_weight, "fsdp", axis=0, tiled=True), "tp", axis=0)
    down = lax.all_gather(lax.all_gather(down_weight, "fsdp", axis=1, tiled=True), "tp", axis=0)
    up_shift = lax.all_gather(up_bias.astype(F32)[None], "tp", axis=0)

    gain_one = norm1_gain.astype(F32)
    center = inputs - jnp.mean(inputs, axis=-1, keepdims=True)
    inverse = lax.rsqrt(jnp.mean(center * center, axis=-1, keepdims=True) + TINY)
    hidden1 = (center * inverse * gain_one + norm1_bias.astype(F32)).astype(BF16)
    kv = dot(hidden1, wkv).astype(BF16)
    if subs > 1:
        by_tp = lax.all_gather(kv, "tp", axis=0, tiled=False)
        kv = lax.dynamic_slice_in_dim(by_tp, sequence * subs, subs, 0).reshape(block, -1)
    kv = lax.all_gather(kv, "ctx", axis=0, tiled=True)

    logits = dot(hidden1, router)
    r0, r1 = routes[:, 0], routes[:, 1]
    l0, l1 = pick(logits, r0, experts)[:, 0], pick(logits, r1, experts)[:, 0]
    top = jnp.maximum(l0, l1)
    e0, e1 = jnp.exp(l0 - top), jnp.exp(l1 - top)
    g0, g1 = e0 / (e0 + e1), e1 / (e0 + e1)

    queries = dot(hidden1, wq).astype(BF16)
    q = jnp.stack([pick(queries, r0, experts), pick(queries, r1, experts)])
    q_pad = jnp.pad(q * 0.125, ((0, 0), (0, 0), (0, head)))
    att, log_total = attention_forward(position[None], pictures, q_pad, kv)
    meta = jnp.stack([g0, g1, r0.astype(F32), r1.astype(F32)] * 2, axis=1)
    router_twice = jnp.pad(
        jnp.concatenate([router, router], axis=1), ((0, 0), (0, 128 - 2 * experts))
    )
    rows_in = jnp.stack([norm1_gain, norm2_gain, norm2_bias, down_bias] * 2).astype(F32)
    result, input_grad, ud, wo_grad, wq_grad, kr, vec, bias = run_back(
        mesh_sizes,
        sequences,
        tokens.shape,
        experts,
        up.shape[0] * up.shape[2],
        pictures,
        (
            low_inputs,
            mine(upstream_tokens),
            meta,
            hidden1,
            q_pad,
            kv,
            att,
            log_total,
            wq,
            wkv,
            router_twice,
            wo,
            up,
            down,
            up_shift,
            rows_in,
        ),
    )
    up_out = ud[:, 0].transpose(1, 0, 2).reshape(rows_d, -1).astype(F32)
    down_out = ud[:, 1].transpose(0, 2, 1).reshape(-1, rows_d).astype(F32)
    output_out = wo_grad[0, 0].astype(F32).T.reshape(output_weight.shape)
    query_out = wq_grad[0, 0].astype(F32).reshape(rows_d, local_experts, head).transpose(1, 0, 2)
    kr = kr[0, 0].astype(F32)
    pair_out = kr[:, : 2 * head]
    router_out = kr[:, 128 : 128 + experts] + kr[:, 128 + experts : 128 + 2 * experts]
    bias_sum = lax.dynamic_slice_in_dim(bias.reshape(-1), tp_rank * up_bias.shape[0], up_bias.shape[0], 0)
    return (
        result,
        input_grad,
        vec[0],
        vec[1],
        router_out,
        query_out,
        output_out,
        pair_out,
        vec[2],
        vec[3],
        up_out,
        bias_sum,
        down_out,
        vec[4],
    )


def solution(mesh):
    rows = P("fsdp", "ctx", None)
    placed = (
        rows,
        rows,
        P("fsdp", None),
        P("fsdp", None),
        P(),
        P(),
        P("fsdp", None),
        P("tp", "fsdp", None),
        P("tp", None, "fsdp"),
        P("fsdp", None),
        P(),
        P(),
        P("fsdp", "tp"),
        P("tp"),
        P("tp", "fsdp"),
        P(),
        rows,
    )
    sizes = tuple(mesh.shape[axis] for axis in ("fsdp", "ctx", "tp"))
    return jax.shard_map(
        functools.partial(per_device, sizes),
        mesh=mesh,
        in_specs=placed,
        out_specs=(
            rows,
            rows,
            P(),
            P(),
            P("fsdp", None),
            P("tp", "fsdp", None),
            P("tp", None, "fsdp"),
            P("fsdp", None),
            P(),
            P(),
            P("fsdp", "tp"),
            P("tp"),
            P("tp", "fsdp"),
            P(),
        ),
        check_vma=False,
    )
```

```python
import functools
import types

import jax
import jax.numpy as jnp
from jax import lax
from jax.experimental import pallas as pl
from jax.experimental.pallas import tpu as pltpu
from jax.sharding import PartitionSpec as P

PIC = 256
TINY = 1e-05
NEG = -1e30
F32 = jnp.float32
BF16 = jnp.bfloat16
TQ = 256
TK = 256
BIG = 1024
NT = (((1,), (1,)), ((), ()))
TN = (((0,), (0,)), ((), ()))


def dot(a, b):
    return jnp.dot(a, b, preferred_element_type=F32)


def dot_nt(a, b):
    return lax.dot_general(a, b, NT, preferred_element_type=F32)


def dot_tn(a, b):
    return lax.dot_general(a, b, TN, preferred_element_type=F32)


def picture_starts(start_ref, mode_ref, sequence, pics):
    return [jnp.where(mode_ref[sequence, k] == 1, start_ref[sequence, k], -(1 << 20)) for k in range(pics)]


def mask_of(q0, k0, keys, queries, starts):
    key_pos = k0 + lax.broadcasted_iota(jnp.int32, (keys, 1), 0)
    query_pos = q0 + lax.broadcasted_iota(jnp.int32, (1, queries), 1)
    key_id = jnp.full((keys, 1), -2, jnp.int32)
    query_id = jnp.full((1, queries), -1, jnp.int32)
    for k, start in enumerate(starts):
        key_id = jnp.where((key_pos >= start) & (key_pos < start + PIC), k, key_id)
        query_id = jnp.where((query_pos >= start) & (query_pos < start + PIC), k, query_id)
    allowed = (key_pos <= query_pos) | (key_id == query_id)
    return jnp.concatenate([allowed, allowed], axis=1)


SMEM = pl.BlockSpec(memory_space=pltpu.SMEM)
VMEM = pl.BlockSpec(memory_space=pltpu.VMEM)
ANY = pl.BlockSpec(memory_space=pl.ANY)
MESH = pl.DeviceIdType.MESH


def remote(src, dst, send, recv, to):
    return pltpu.make_async_remote_copy(
        src_ref=src, dst_ref=dst, send_sem=send, recv_sem=recv, device_id=to, device_id_type=MESH
    )


class Place:
    def __init__(self, sizes, sequences):
        self.fsdp, self.ctx, self.tp = sizes
        self.subs = self.tp // sequences
        self.blocks = self.ctx * self.subs
        self.f, self.x, self.t = (lax.axis_index(a) for a in ("fsdp", "ctx", "tp"))
        self.seq, self.sub = self.t // self.subs, self.t % self.subs
        self.block = self.x * self.subs + self.sub

    def owner(self, block):
        return {"ctx": block // self.subs, "tp": self.seq * self.subs + block % self.subs}

    def barrier(self):
        semaphore = pltpu.get_barrier_semaphore()
        count = 0
        for axis, size, me in (("fsdp", self.fsdp, self.f), ("ctx", self.ctx, self.x), ("tp", self.tp, self.t)):
            for r in range(1, size):
                pl.semaphore_signal(
                    semaphore, inc=1, device_id={axis: lax.rem(me + r, size)}, device_id_type=MESH
                )
                count += 1
        if self.subs > 1:
            for r in range(1, self.blocks):
                pl.semaphore_signal(
                    semaphore,
                    inc=1,
                    device_id=self.owner(lax.rem(self.block + r, self.blocks)),
                    device_id_type=MESH,
                )
                count += 1
        pl.semaphore_wait(semaphore, count)


class Reduce:
    def __init__(self, k, w, n, d, sizes, tp=True):
        self.k, self.w, self.n, self.d, self.sizes, self.tp = k, w, n, d, sizes, tp
        fsdp, ctx, tps = sizes
        self.rows, self.part = d // fsdp, d // fsdp // ctx
        self.count = 16 if tp else 15

    def scratch(self):
        k, w, n, d = self.k, self.w, self.n, self.d
        fsdp, ctx, tps = self.sizes
        dma = pltpu.SemaphoreType.DMA
        shapes = [
            pltpu.VMEM((n, k, d, w), BF16),
            pltpu.VMEM((n, fsdp - 1, k, self.rows, w), BF16),
            pltpu.VMEM((n, k, self.rows, w), F32),
            pltpu.VMEM((n, k, self.rows, w), BF16),
            pltpu.VMEM((n, ctx - 1, k, self.part, w), BF16),
            pltpu.VMEM((n, k, self.rows, w), BF16),
            dma((n, fsdp - 1)),
            dma((n, fsdp - 1)),
            dma((n, ctx - 1)),
            dma((n, ctx - 1)),
            dma((n, ctx - 1)),
            dma((n, ctx - 1)),
        ]
        if self.tp:
            shapes += [
                pltpu.VMEM((tps - 1, n, k, d, w), BF16),
                pltpu.VMEM((tps - 1, n, k, d, w), BF16),
                dma((tps - 1, n)),
                dma((tps - 1, n)),
            ]
        else:
            shapes += [pltpu.VMEM((tps, k, self.rows, w), F32), dma((tps - 1,)), dma((tps - 1,))]
        return shapes

    def bind(self, place, refs):
        self.place = place
        self.s2, self.r2, self.own, self.s3, self.r3, self.fin = refs[:6]
        self.m2, self.m3, self.m4 = refs[6:8], refs[8:10], refs[10:12]
        if self.tp:
            self.s1, self.r1 = refs[12:14]
            self.m1 = refs[14:16]
        else:
            self.all, self.m1 = refs[12], refs[13:15]

    def d1(self, o, c):
        p = self.place
        to = {"tp": lax.rem(p.t + o, p.tp)}
        if self.tp:
            return remote(
                self.s1.at[o - 1, c], self.r1.at[o - 1, c], self.m1[0].at[o - 1, c], self.m1[1].at[o - 1, c], to
            )
        return remote(self.all.at[p.t], self.all.at[p.t], self.m1[0].at[o - 1], self.m1[1].at[o - 1], to)

    def d2(self, r, c):
        p = self.place
        to = lax.rem(p.f + r, p.fsdp)
        rows = pl.ds(pl.multiple_of(to * self.rows, self.rows), self.rows)
        return remote(
            self.s2.at[c, :, rows, :],
            self.r2.at[c, r - 1],
            self.m2[0].at[c, r - 1],
            self.m2[1].at[c, r - 1],
            {"fsdp": to},
        )

    def spot(self, x):
        return pl.ds(pl.multiple_of(x * self.part, self.part), self.part)

    def d3(self, q, c):
        p = self.place
        to = lax.rem(p.x + q, p.ctx)
        return remote(
            self.s3.at[c, :, self.spot(to), :],
            self.r3.at[c, q - 1],
            self.m3[0].at[c, q - 1],
            self.m3[1].at[c, q - 1],
            {"ctx": to},
        )

    def d4(self, q, c):
        p = self.place
        to = lax.rem(p.x + q, p.ctx)
        mine = self.fin.at[c, :, self.spot(p.x), :]
        return remote(mine, mine, self.m4[0].at[c, q - 1], self.m4[1].at[c, q - 1], {"ctx": to})

    def put(self, o, c, k, value):
        self.s1[o - 1, c, k] = value.astype(BF16)

    def give(self, o, c):
        self.d1(o, c).start()

    def take(self, c, acc):
        p, w = self.place, self.w
        if self.tp:
            for o in range(1, p.tp):
                self.d1(o, c).wait_recv()
            for k in range(self.k):
                total = acc[k, :, 0:w]
                for o in range(1, p.tp):
                    total = total + self.r1[o - 1, c, k].astype(F32)
                acc[k, :, 0:w] = total
        for k in range(self.k):
            self.s2[c, k] = acc[k, :, 0:w].astype(BF16)
        for r in range(1, p.fsdp):
            self.d2(r, c).start()
        for k in range(self.k):
            self.own[c, k] = acc[k, pl.ds(pl.multiple_of(p.f * self.rows, self.rows), self.rows), 0:w]

    def fold(self, c):
        p = self.place
        for r in range(1, p.fsdp):
            self.d2(r, c).wait_recv()
        for k in range(self.k):
            total = self.own[c, k]
            for r in range(1, p.fsdp):
                total = total + self.r2[c, r - 1, k].astype(F32)
            if self.tp:
                self.own[c, k] = total
                self.s3[c, k] = total.astype(BF16)
            else:
                self.all[p.t, k] = total
        if self.tp:
            for q in range(1, p.ctx):
                self.d3(q, c).start()
        else:
            for o in range(1, p.tp):
                self.d1(o, c).start()

    def share(self, c):
        p = self.place
        for o in range(1, p.tp):
            self.d1(o, c).wait_recv()
        for k in range(self.k):
            total = self.all[0, k]
            for o in range(1, p.tp):
                total = total + self.all[o, k]
            self.own[c, k] = total
            self.s3[c, k] = total.astype(BF16)
        for q in range(1, p.ctx):
            self.d3(q, c).start()

    def finish(self, c):
        p = self.place
        for q in range(1, p.ctx):
            self.d3(q, c).wait_recv()
        for k in range(self.k):
            total = self.own[c, k, self.spot(p.x), :]
            for q in range(1, p.ctx):
                total = total + self.r3[c, q - 1, k].astype(F32)
            self.fin[c, k, self.spot(p.x), :] = total.astype(BF16)
        for q in range(1, p.ctx):
            self.d4(q, c).start()

    def close(self):
        p = self.place

        @pl.loop(0, self.n)
        def _(c):
            for q in range(1, p.ctx):
                self.d4(q, c).wait()
                self.d3(q, c).wait_send()
            for r in range(1, p.fsdp):
                self.d2(r, c).wait_send()
            for o in range(1, p.tp):
                self.d1(o, c).wait_send()


class Everywhere:
    def __init__(self, shape, sizes):
        self.shape, self.sizes, self.count = shape, sizes, 9

    def scratch(self):
        dma = pltpu.SemaphoreType.DMA
        shapes = []
        for size in self.sizes:
            shapes += [pltpu.VMEM((size,) + self.shape, F32), dma((size - 1,)), dma((size - 1,))]
        return shapes

    def bind(self, place, refs):
        self.place, self.refs = place, refs

    def copy(self, stage, r):
        p = self.place
        axis, size, me = (
            ("fsdp", p.fsdp, p.f),
            ("ctx", p.ctx, p.x),
            ("tp", p.tp, p.t),
        )[stage]
        buf, send, recv = self.refs[3 * stage : 3 * stage + 3]
        return remote(
            buf.at[me], buf.at[me], send.at[r - 1], recv.at[r - 1], {axis: lax.rem(me + r, size)}
        )

    def start(self, stage, value):
        p = self.place
        me = (p.f, p.x, p.t)[stage]
        self.refs[3 * stage][me] = value
        for r in range(1, self.sizes[stage]):
            self.copy(stage, r).start()

    def total(self, stage):
        buf = self.refs[3 * stage]
        for r in range(1, self.sizes[stage]):
            self.copy(stage, r).wait()
        total = buf[0]
        for r in range(1, self.sizes[stage]):
            total = total + buf[r]
        return total


def norm_back(grad, normed, inverse, gain):
    scaled = grad * gain
    inner = (
        scaled
        - jnp.mean(scaled, axis=-1, keepdims=True)
        - normed * jnp.mean(scaled * normed, axis=-1, keepdims=True)
    )
    return inner * inverse


def half_lanes(rows):
    return lax.broadcasted_iota(jnp.int32, (rows, 128), 1)


def both_halves(values, upper):
    low = half_lanes(values.shape[0]) < 64
    turned = pltpu.roll(values, 64, 1)
    return jnp.where(low, turned, values) if upper else jnp.where(low, values, turned)


class Gather:
    def __init__(self, place, shard, spot, to_tp, refs):
        self.place, self.shard, self.spot, self.to_tp = place, shard, spot, to_tp
        self.fsend, self.frecv, self.tsend, self.trecv, self.local = refs

    def keep(self):
        p = self.place
        return pltpu.make_async_copy(self.shard, self.spot(p.t, p.f), self.local.at[0])

    def across(self, r):
        p = self.place
        return remote(
            self.shard,
            self.spot(p.t, p.f),
            self.fsend.at[r - 1],
            self.frecv.at[r - 1],
            {"fsdp": lax.rem(p.f + r, p.fsdp)},
        )

    def beside(self, o, r):
        p = self.place
        spot = self.spot(p.t, lax.rem(p.f - r + p.fsdp, p.fsdp))
        return remote(
            self.shard if r == 0 else spot,
            spot,
            self.tsend.at[o - 1, r],
            self.trecv.at[o - 1, r],
            {"tp": lax.rem(p.t + o, p.tp)},
        )

    def begin(self):
        p = self.place
        for r in range(1, p.fsdp):
            self.across(r).start()
        if self.to_tp:
            for o in range(1, p.tp):
                self.beside(o, 0).start()
        self.keep().start()

    def forward(self):
        p = self.place
        for r in range(1, p.fsdp):
            self.across(r).wait_recv()
            if self.to_tp:
                for o in range(1, p.tp):
                    self.beside(o, r).start()
        self.keep().wait()

    def arrive(self):
        p = self.place
        if self.to_tp:
            for o in range(1, p.tp):
                for r in range(p.fsdp):
                    self.beside(o, r).wait_recv()

    def close(self):
        p = self.place
        for r in range(1, p.fsdp):
            self.across(r).wait_send()
        if self.to_tp:
            for o in range(1, p.tp):
                for r in range(p.fsdp):
                    self.beside(o, r).wait_send()


INPUTS = ["pic_start", "pic_mode", "tokens", "routes", "upstream"]
INPUTS += ["kv_shard", "wq_shard", "wo_shard", "up_shard", "down_shard"]
INPUTS += ["router_in", "bias_in", "gain1_in", "bias1_in", "gain2_in", "bias2_in", "down_bias_in"]
OUTPUTS = ["out_hbm", "grad_hbm", "ud_out", "wo_out", "wq_out", "kr_out", "vec_out", "bias_out"]
WEIGHTS = ["kv", "rt", "wq", "wo", "up", "down"]
FSDP_ONLY = ["kv", "rt"]


def layer_kernel(dims, names, *refs):
    sizes, sequences, tokens, width, experts, pics, length, reducers = dims
    fsdp, ctx, tps = sizes
    named = INPUTS + OUTPUTS + names
    a = types.SimpleNamespace(**dict(zip(named, refs[: len(named)])))
    rest = refs[len(named) :]
    r_ud, r_wo, r_wq, r_kr, r_vec, r_bias = reducers
    place = Place(sizes, sequences)
    for reducer in reducers:
        reducer.bind(place, rest[: reducer.count])
        rest = rest[reducer.count :]
    tiles = tokens // TQ
    cw, chunks = r_ud.w, r_ud.n
    rows_t = min(1024, tokens)
    big = min(BIG, tokens)
    shard_rows = width // fsdp

    def span(index, size):
        return pl.ds(pl.multiple_of(index * size, size), size)

    spots = dict(
        kv=lambda t, f: a.wkv.at[span(f, shard_rows), :],
        rt=lambda t, f: a.rpad.at[0:16, span(f, shard_rows)],
        wq=lambda t, f: a.wq.at[t, :, span(f, shard_rows)],
        wo=lambda t, f: a.wo.at[t, :, span(f, shard_rows)],
        up=lambda t, f: a.up.at[t, span(f, shard_rows), :],
        down=lambda t, f: a.down.at[t, :, span(f, shard_rows)],
    )
    weights = {}
    for name in WEIGHTS:
        weights[name] = Gather(place, getattr(a, name + "_shard"), spots[name], name not in FSDP_ONLY, rest[:5])
        rest = rest[5:]

    own_slice = (place.seq, pl.ds(pl.multiple_of(place.sub * tokens, tokens), tokens))
    loads = [
        pltpu.make_async_copy(source.at[own_slice[0], own_slice[1], :], target, a.load_sem.at[k])
        for k, (source, target) in enumerate(
            ((a.tokens, a.tok), (a.upstream, a.ups))
        )
    ]
    loads.append(
        pltpu.make_async_copy(
            a.routes.at[place.seq, :, pl.ds(pl.multiple_of(place.sub * tokens, tokens), tokens)], a.rt, a.load_sem.at[2]
        )
    )
    for load in loads:
        load.start()

    router = a.router_in[...].astype(F32)
    a.rt_shard[...] = jnp.concatenate([router, router], axis=0).astype(BF16)
    a.rpad[16:, :] = jnp.zeros((112, width), BF16)
    a.bias_shard[...] = a.bias_in[...].astype(F32)
    a.bias_raw[place.t] = a.bias_shard[...]
    place.barrier()
    for name in WEIGHTS[:3]:
        weights[name].begin()

    def bias_copy(o):
        spot = a.bias_raw.at[place.t]
        return remote(
            a.bias_shard, spot, a.bias_sem.at[0, o - 1], a.bias_sem.at[1, o - 1], {"tp": lax.rem(place.t + o, tps)}
        )

    for o in range(1, tps):
        bias_copy(o).start()

    def row(ref):
        values = ref[...].astype(F32)
        return jnp.concatenate([values[k : k + 1, :] for k in range(values.shape[0])], axis=1)

    gain1, bias1 = row(a.gain1_in), row(a.bias1_in)
    q_base = place.block * tokens
    starts = picture_starts(a.pic_start, a.pic_mode, place.seq, pics)
    lanes = half_lanes(TQ)
    own_rows = pl.ds(pl.multiple_of(q_base, tokens), tokens)

    def tile_rows(i):
        return span(i, TQ)

    def gates(rows):
        return [a.meta[rows, k : k + 1] for k in range(4)]

    def expert_of(c):
        return 2 * c + jnp.where(lanes >= 64, 1, 0)

    def normalise(x):
        center = x - jnp.mean(x, axis=-1, keepdims=True)
        inverse = lax.rsqrt(jnp.mean(center * center, axis=-1, keepdims=True) + TINY)
        return center * inverse, inverse

    def choose(full, r):
        expert = r.astype(jnp.int32)
        chosen = jnp.zeros((TQ, 128), F32)
        for c in range(experts // 2):
            chosen = jnp.where(expert == expert_of(c), full[:, c * 128 : (c + 1) * 128], chosen)
        return chosen + pltpu.roll(chosen, 64, 1)

    loads[0].wait()
    loads[2].wait()

    @pl.loop(0, tiles)
    def _(i):
        rows = tile_rows(i)
        normed, _ = normalise(a.tok[rows, :].astype(F32))
        a.hid1[rows, :] = (normed * gain1 + bias1).astype(BF16)

    a.kv[pl.ds(length, TQ), :] = jnp.zeros((TQ, 128), BF16)
    weights["kv"].forward()

    @pl.loop(0, tiles)
    def _(i):
        rows = tile_rows(i)
        pair = dot(a.hid1[rows, :], a.wkv[...])
        a.kv[pl.ds(pl.multiple_of(q_base + i * TQ, TQ), TQ), :] = pair.astype(BF16)

    after_me, before_me = place.block + 1 < place.blocks, place.block > 0

    def pass_on(d):
        keys = pl.ds(pl.multiple_of((place.block - d) * tokens, tokens), tokens)
        to = place.owner(lax.rem(place.block + 1, place.blocks))
        return remote(a.kv.at[keys, :], a.kv.at[keys, :], a.kv_sem.at[0, d], a.kv_sem.at[1, d], to)

    def reach_back():
        keys = pl.ds(pl.multiple_of(q_base, TQ), TQ)
        to = place.owner(lax.rem(place.block + place.blocks - 1, place.blocks))
        return remote(a.kv.at[keys, :], a.kv.at[keys, :], a.near_sem.at[2], a.near_sem.at[3], to)

    @pl.when(after_me)
    def _():
        pass_on(0).start()

    @pl.when(before_me)
    def _():
        reach_back().start()

    weights["rt"].forward()

    @pl.loop(0, tiles)
    def _(i):
        rows = tile_rows(i)
        logits = dot_nt(a.hid1[rows, :], a.rpad[...])
        pairs = jnp.concatenate([a.rt[:, rows].astype(F32)] * 4, axis=0).T
        r0, r1 = pairs[:, 0:1].astype(jnp.int32), pairs[:, 1:2].astype(jnp.int32)
        l0 = jnp.sum(jnp.where(lanes == r0, logits, 0.0), axis=-1, keepdims=True)
        l1 = jnp.sum(jnp.where(lanes == r1, logits, 0.0), axis=-1, keepdims=True)
        top = jnp.maximum(l0, l1)
        e0, e1 = jnp.exp(l0 - top), jnp.exp(l1 - top)
        a.meta[rows, 0:1] = e0 / (e0 + e1)
        a.meta[rows, 1:2] = e1 / (e0 + e1)
        a.meta[rows, 2:3] = r0.astype(F32)
        a.meta[rows, 3:4] = r1.astype(F32)

    weights["wq"].forward()
    for name in WEIGHTS[3:]:
        weights[name].begin()
    weights["wq"].arrive()

    @pl.loop(0, tiles)
    def _(i):
        rows = tile_rows(i)
        _, _, r0, r1 = gates(rows)
        full = dot_nt(a.hid1[rows, :], a.wq[...].reshape(width, width))
        for s, r in enumerate((r0, r1)):
            a.q[s, rows, :] = jnp.where(lanes < 64, choose(full, r) * 0.125, 0.0).astype(BF16)

    @pl.loop(0, tiles)
    def _(i):
        a.top[i] = jnp.full((1, 2 * TQ), NEG, F32)
        a.total[i] = jnp.zeros((1, 2 * TQ), F32)
    a.dqt[...] = jnp.zeros_like(a.dqt)

    def look(i, k0, size, masked):
        rows = tile_rows(i)
        keys = pl.ds(pl.multiple_of(k0, TK), size)
        q = jnp.concatenate([a.q[0, rows, :], a.q[1, rows, :]], axis=0)
        pair = a.kv[keys, :]
        scores = dot_nt(pair, q)
        if masked:
            scores = jnp.where(mask_of(q_base + i * TQ, k0, size, TQ, starts), scores, NEG)
        before = a.top[i]
        now = jnp.maximum(before, jnp.max(scores, axis=0, keepdims=True))
        probs = jnp.exp(scores - now)
        scale = jnp.exp(before - now)
        a.top[i] = now
        a.total[i] = a.total[i] * scale + jnp.sum(probs, axis=0, keepdims=True)
        a.dqt[i] = a.dqt[i] * scale + dot_tn(pair, probs.astype(BF16))

    @pl.when(after_me)
    def _():
        reach_back().wait_recv()

    @pl.loop(0, tiles)
    def _(i):
        look(i, q_base + i * TK, 2 * TK, True)

    for i in range(1, tiles):
        look(i, q_base, i * TK, False)

    later = ["wo", "up", "down"]

    @pl.loop(0, place.blocks - 1)
    def _(j):
        @pl.when(j < place.block)
        def _():
            pass_on(j).wait_recv()

            @pl.when(after_me)
            def _():
                pass_on(j + 1).start()

            @pl.loop(0, tokens // big)
            def _(k):
                @pl.loop(0, tiles)
                def _(i):
                    look(i, (place.block - 1 - j) * tokens + k * big, big, False)

        for k, name in enumerate(later):
            if k < place.blocks - 1:

                @pl.when(j == k)
                def _():
                    weights[name].forward()

    for name in later[place.blocks - 1 :]:
        weights[name].forward()

    @pl.loop(0, tiles)
    def _(i):
        rows = tile_rows(i)
        both = (a.dqt[i] / a.total[i]).T
        a.att[0, rows, :] = both[:TQ]
        a.att[1, rows, :] = both[TQ:]
        a.logt[i] = a.top[i] + jnp.log(a.total[i])

    gain2, bias2, down_bias = row(a.gain2_in), row(a.bias2_in), row(a.down_bias_in)
    a.vec[...] = jnp.zeros_like(a.vec)
    a.bias_acc[...] = jnp.zeros_like(a.bias_acc)
    a.woacc[...] = jnp.zeros_like(a.woacc)
    weights["wo"].arrive()

    @pl.loop(0, tiles)
    def _(i):
        rows = tile_rows(i)
        g0, g1, r0, r1 = gates(rows)
        after = a.tok[rows, :].astype(F32)
        out_w = a.wo[...].reshape(width, width)
        for s, (g, r) in enumerate(((g0, r0), (g1, r1))):
            twice = both_halves(a.att[s, rows, :], True)
            expert = r.astype(jnp.int32)
            for c in range(experts // 2):
                a.wide[s, rows, c * 128 : (c + 1) * 128] = jnp.where(expert == expert_of(c), twice, 0.0).astype(BF16)
            projected = dot(a.wide[s, rows, :], out_w)
            a.proj[s, rows, :] = projected
            after = after + g * projected
        normed, inverse = normalise(after)
        a.normed2[rows, :] = normed
        a.inv2[rows, :] = inverse
        a.hid2[rows, :] = (normed * gain2 + bias2).astype(BF16)
        a.out_acc[rows, :] = after + down_bias
        a.mid[rows, :] = jnp.zeros_like(after)

    loads[1].wait()
    weights["up"].arrive()
    weights["down"].arrive()
    for o in range(1, tps):
        bias_copy(o).wait_recv()
    lines = cw // 128
    for t in range(tps):
        for c in range(chunks):
            a.up_bias[t * chunks + c] = jnp.concatenate(
                [a.bias_raw[t, c * lines + k : c * lines + k + 1, :] for k in range(lines)], axis=1
            )

    def feed(t, c):
        cols = span(c, cw)
        whole = tokens == rows_t
        if not whole:
            a.gacc[...] = jnp.zeros_like(a.gacc)

        @pl.loop(0, tokens // rows_t)
        def _(i):
            rows = span(i, rows_t)
            h2, u = a.hid2[rows, :], a.ups[rows, :]
            pre = dot(h2, a.up[t, :, cols]) + a.up_bias[t * chunks + c]
            sig = 1.0 / (1.0 + jnp.exp(-pre))
            active = (pre * sig).astype(BF16)
            a.out_acc[rows, :] += dot(active, a.down[t, cols, :])
            down_part = dot_tn(u, active)
            a.gacc[1, :, 0:cw] = down_part if whole else a.gacc[1, :, 0:cw] + down_part
            slope = sig * (1.0 + pre * (1.0 - sig))
            grad = dot_nt(u, a.down[t, cols, :]) * slope
            low = grad.astype(BF16)
            a.bias_acc[t * chunks + c] += jnp.sum(low.astype(F32), axis=0, keepdims=True)
            up_part = dot_tn(h2, low)
            a.gacc[0, :, 0:cw] = up_part if whole else a.gacc[0, :, 0:cw] + up_part
            a.mid[rows, :] += dot_nt(low, a.up[t, :, cols])

    for o in range(1, tps):

        @pl.loop(0, chunks)
        def _(c):
            feed(lax.rem(place.t + o, tps), c)
            for k in range(2):
                r_ud.put(o, c, k, a.gacc[k, :, 0:cw])
            r_ud.give(o, c)

    @pl.loop(0, chunks)
    def _(c):
        feed(place.t, c)
        r_ud.take(c, a.gacc)

    r_bias.start(2, a.bias_acc[...])

    def share_out(low, hbm, slot):
        spot = hbm.at[own_slice[0], own_slice[1], :]
        copies = [
            remote(
                low, spot, a.out_sem.at[0, slot, o - 1], a.out_sem.at[1, slot, o - 1], {"tp": lax.rem(place.t + o, tps)}
            )
            for o in range(1, tps)
        ]
        copies.append(pltpu.make_async_copy(low, spot, a.loc_sem.at[slot]))
        for copy in copies:
            copy.start()
        return copies

    def add_row(k, value):
        a.vec[k : k + 1, :] += jnp.sum(value, axis=0, keepdims=True)

    @pl.loop(0, tiles)
    def _(i):
        rows = tile_rows(i)
        g0, g1, r0, r1 = gates(rows)
        out_w = a.wo[...].reshape(width, width)
        a.res_low[rows, :] = a.out_acc[rows, :].astype(BF16)
        upstream = a.ups[rows, :].astype(F32)
        grad, normed = a.mid[rows, :], a.normed2[rows, :]
        resid = upstream + norm_back(grad, normed, a.inv2[rows, :], gain2)
        a.mid[rows, :] = resid
        add_row(2, grad * normed)
        add_row(3, grad)
        add_row(4, upstream)
        d0 = jnp.sum(a.proj[0, rows, :] * resid, axis=-1, keepdims=True)
        d1 = jnp.sum(a.proj[1, rows, :] * resid, axis=-1, keepdims=True)
        mean = g0 * d0 + g1 * d1
        for s, (g, r) in enumerate(((g0, r0), (g1, r1))):
            low = (g * resid).astype(BF16)
            a.woacc[0] += dot_tn(low, a.wide[s, rows, :])
            chosen = jnp.where(lanes >= 64, choose(dot_nt(low, out_w), r), 0.0).astype(BF16)
            a.da[s, rows, :] = chosen
            product = chosen.astype(F32) * jnp.where(lanes >= 64, a.att[s, rows, :], 0.0)
            a.delta[i, :, s * TQ : (s + 1) * TQ] = jnp.sum(product.T, axis=0, keepdims=True)
        lane_expert = lax.rem(lanes, experts)
        lg = jnp.where(lane_expert == r0.astype(jnp.int32), g0 * (d0 - mean), 0.0)
        lg = lg + jnp.where(lane_expert == r1.astype(jnp.int32), g1 * (d1 - mean), 0.0)
        high = lg.astype(BF16).astype(F32)
        a.lgp[rows, :] = jnp.where(
            lanes < experts, high, jnp.where(lanes < 2 * experts, lg - high, 0.0)
        ).astype(BF16)

    out_copies = share_out(a.res_low, a.out_hbm, 0)

    def hand_out(reducer, acc):
        w = reducer.w
        for t in range(tps):

            @pl.when(t != place.t)
            def _():
                o = lax.rem(t - place.t + tps, tps)
                reducer.s1[o - 1, 0, 0] = acc[0, :, t * w : (t + 1) * w].astype(BF16)
                reducer.give(o, 0)

    def take_own(reducer, acc):
        w = reducer.w
        for t in range(tps):

            @pl.when(t == place.t)
            def _():
                a.gacc[0, :, 0:w] = acc[0, :, t * w : (t + 1) * w]

        reducer.take(0, a.gacc)

    hand_out(r_wo, a.woacc)
    r_bias.start(0, r_bias.total(2))

    a.dqt[...] = jnp.zeros_like(a.dqt)
    a.dkv[...] = jnp.zeros_like(a.dkv)

    def attend(i, k0, size, masked):
        rows = tile_rows(i)
        keys = pl.ds(pl.multiple_of(k0, TK), size)
        q = jnp.concatenate([a.q[0, rows, :], a.q[1, rows, :]], axis=0)
        d_att = jnp.concatenate([a.da[0, rows, :], a.da[1, rows, :]], axis=0)
        pair = a.kv[keys, :]
        scores = dot_nt(pair, q)
        if masked:
            scores = jnp.where(mask_of(q_base + i * TQ, k0, size, TQ, starts), scores, NEG)
        probs = jnp.exp(scores - a.logt[i])
        prob_grad = dot_nt(pair, d_att)
        score_grad = (probs * (prob_grad - a.delta[i])).astype(BF16)
        a.dkv[keys, :] += dot(score_grad, q) + dot(probs.astype(BF16), d_att)
        a.dqt[i] += dot_tn(pair, score_grad)

    def dkv_copy(block):
        slot = place.block - block - 1
        return remote(
            a.dkv_send.at[block],
            a.dkv_recv.at[slot],
            a.dkv_sem.at[0, slot],
            a.dkv_sem.at[1, slot],
            place.owner(block),
        )

    @pl.loop(0, place.blocks - 1)
    def _(j):
        @pl.when(j < place.block)
        def _():
            @pl.loop(0, tokens // big)
            def _(k):
                @pl.loop(0, tiles)
                def _(i):
                    attend(i, j * tokens + k * big, big, False)

            a.dkv_send[j] = a.dkv[span(j, tokens), :].astype(BF16)
            dkv_copy(j).start()

        @pl.when(j < chunks)
        def _():
            r_ud.fold(j)

        if place.blocks > 2:

            @pl.when((j > 0) & (j < chunks + 1))
            def _():
                r_ud.finish(j - 1)

    done = place.blocks - 1
    take_own(r_wo, a.woacc)
    r_bias.start(1, r_bias.total(0))

    @pl.loop(0, tiles)
    def _(i):
        attend(i, q_base + i * TK, 2 * TK, True)

    for i in range(1, tiles):
        attend(i, q_base, i * TK, False)

    def near_copy():
        return remote(
            a.near_send,
            a.near_buf,
            a.near_sem.at[0],
            a.near_sem.at[1],
            place.owner(lax.rem(place.block + 1, place.blocks)),
        )

    @pl.when(after_me)
    def _():
        a.near_send[...] = a.dkv[pl.ds(pl.multiple_of((place.block + 1) * tokens, TQ), TQ), :].astype(BF16)
        near_copy().start()

    for c in range(min(done, chunks), chunks):
        r_ud.fold(c)
    for c in range(max(min(done, chunks + 1) - 1, 0), chunks):
        r_ud.finish(c)
    r_wo.fold(0)

    @pl.loop(0, tiles)
    def _(i):
        rows = tile_rows(i)
        _, _, r0, r1 = gates(rows)
        dq = (a.dqt[i] * 0.125).T
        first, second = both_halves(dq[:TQ], False), both_halves(dq[TQ:], False)
        for c in range(experts // 2):
            column = jnp.where(r0.astype(jnp.int32) == expert_of(c), first, 0.0)
            column = jnp.where(r1.astype(jnp.int32) == expert_of(c), second, column)
            a.dqw[rows, c * 128 : (c + 1) * 128] = column.astype(BF16)

    a.woacc[0] = dot_tn(a.hid1[...], a.dqw[...])
    hand_out(r_wq, a.woacc)

    def dkv_from(slot):
        return remote(
            a.dkv_send.at[0], a.dkv_recv.at[slot], a.dkv_sem.at[0, slot], a.dkv_sem.at[1, slot], place.owner(place.block)
        )

    @pl.loop(0, place.blocks - 1 - place.block)
    def _(slot):
        dkv_from(slot).wait_recv()
        a.dkv[own_rows, :] += a.dkv_recv[slot].astype(F32)

    @pl.when(before_me)
    def _():
        near_copy().wait_recv()
        a.dkv[pl.ds(pl.multiple_of(q_base, TQ), TQ), :] += a.near_buf[...].astype(F32)

    a.pairg[:, 0:128] = a.dkv[own_rows, :].astype(BF16)
    a.pairg[:, 128:256] = a.lgp[...]
    a.gacc[0, :, 0:256] = dot_tn(a.hid1[...], a.pairg[...])
    r_kr.take(0, a.gacc)
    take_own(r_wq, a.woacc)
    r_wo.finish(0)

    @pl.loop(0, tiles)
    def _(i):
        rows = tile_rows(i)
        normed, inverse = normalise(a.tok[rows, :].astype(F32))
        grad = dot(a.dqw[rows, :], a.wq[...].reshape(width, width))
        grad = grad + dot_nt(a.pairg[rows, 0:128], a.wkv[...]) + dot(a.lgp[rows, :], a.rpad[...])
        add_row(0, grad * normed)
        add_row(1, grad)
        a.grad_low[rows, :] = (a.mid[rows, :] + norm_back(grad, normed, inverse, gain1)).astype(BF16)

    grad_copies = share_out(a.grad_low, a.grad_hbm, 1)
    r_vec.start(2, a.vec[...])
    r_kr.fold(0)
    r_wq.fold(0)
    r_vec.start(0, r_vec.total(2))
    r_kr.share(0)
    r_vec.start(1, r_vec.total(0))
    r_wq.finish(0)
    r_kr.finish(0)
    a.vec_out[...] = r_vec.total(1)
    a.bias_out[...] = r_bias.total(1)
    for reducer, out in ((r_ud, a.ud_out), (r_wo, a.wo_out), (r_wq, a.wq_out), (r_kr, a.kr_out)):
        reducer.close()
        out[...] = reducer.fin[...]

    @pl.loop(0, place.block)
    def _(j):
        dkv_copy(j).wait_send()

    @pl.when(after_me)
    def _():
        near_copy().wait_send()

        @pl.loop(0, place.block + 1)
        def _(d):
            pass_on(d).wait_send()

    @pl.when(before_me)
    def _():
        reach_back().wait_send()

    for name in WEIGHTS:
        weights[name].close()
    for o in range(1, tps):
        bias_copy(o).wait_send()
    for copy in out_copies + grad_copies:
        copy.wait()


def run_layer(sizes, sequences, shape, experts, arrays):
    fsdp, ctx, tps = sizes
    subs = tps // sequences
    width = shape[2]
    tokens = shape[1] // subs
    length = shape[1] * ctx
    blocks = ctx * subs
    tiles = tokens // TQ
    local_hidden = arrays[8].shape[1]
    cw = min(512, local_hidden)
    chunks = local_hidden // cw
    w = width // tps
    reducers = (
        Reduce(2, cw, chunks, width, sizes),
        Reduce(1, w, 1, width, sizes),
        Reduce(1, w, 1, width, sizes),
        Reduce(1, 256, 1, width, sizes, tp=False),
        Everywhere((8, width), sizes),
        Everywhere((tps * chunks, 1, cw), sizes),
    )
    dims = (sizes, sequences, tokens, width, experts, arrays[0].shape[1], length, reducers)
    rows = width // fsdp
    dma = pltpu.SemaphoreType.DMA
    vmem = pltpu.VMEM
    scratch = dict(
        tok=vmem((tokens, width), BF16),
        rt=vmem((2, tokens), jnp.int32),
        ups=vmem((tokens, width), BF16),
        load_sem=dma((3,)),
        wkv=vmem((width, 128), BF16),
        rt_shard=vmem((16, rows), BF16),
        rpad=vmem((128, width), BF16),
        wq=vmem((tps, w, width), BF16),
        wo=vmem((tps, w, width), BF16),
        up=vmem((tps, width, local_hidden), BF16),
        down=vmem((tps, local_hidden, width), BF16),
        bias_shard=vmem((local_hidden // 128, 128), F32),
        bias_raw=vmem((tps, local_hidden // 128, 128), F32),
        up_bias=vmem((tps * chunks, 1, cw), F32),
        bias_sem=dma((2, tps - 1)),
        meta=vmem((tokens, 8), F32),
        hid1=vmem((tokens, width), BF16),
        q=vmem((2, tokens, 128), BF16),
        kv=vmem((length + TQ, 128), BF16),
        kv_sem=dma((2, blocks)),
        near_sem=dma((4,)),
        top=vmem((tiles, 1, 2 * TQ), F32),
        total=vmem((tiles, 1, 2 * TQ), F32),
        att=vmem((2, tokens, 128), F32),
        logt=vmem((tiles, 1, 2 * TQ), F32),
        wide=vmem((2, tokens, width), BF16),
        proj=vmem((2, tokens, width), F32),
        normed2=vmem((tokens, width), F32),
        hid2=vmem((tokens, width), BF16),
        out_acc=vmem((tokens, width), F32),
        mid=vmem((tokens, width), F32),
        inv2=vmem((tokens, 1), F32),
        gacc=vmem((2, width, max(cw, 256)), F32),
        woacc=vmem((1, width, width), F32),
        da=vmem((2, tokens, 128), BF16),
        delta=vmem((tiles, 1, 2 * TQ), F32),
        lgp=vmem((tokens, 128), BF16),
        dqt=vmem((tiles, 128, 2 * TQ), F32),
        dkv=vmem((length + TQ, 128), F32),
        dkv_send=vmem((blocks - 1, tokens, 128), BF16),
        dkv_recv=vmem((blocks - 1, tokens, 128), BF16),
        dkv_sem=dma((2, blocks - 1)),
        dqw=vmem((tokens, width), BF16),
        pairg=vmem((tokens, 256), BF16),
        vec=vmem((8, width), F32),
        bias_acc=vmem((tps * chunks, 1, cw), F32),
        res_low=vmem((tokens, width), BF16),
        grad_low=vmem((tokens, width), BF16),
        near_buf=vmem((TQ, 128), BF16),
        near_send=vmem((TQ, 128), BF16),
        loc_sem=dma((2,)),
        out_sem=dma((2, 2, tps - 1)),
    )
    shapes = list(scratch.values())
    for reducer in reducers:
        shapes += reducer.scratch()
    for _ in WEIGHTS:
        shapes += [dma((fsdp - 1,)), dma((fsdp - 1,)), dma((tps - 1, fsdp)), dma((tps - 1, fsdp)), dma((1,))]
    return pl.pallas_call(
        functools.partial(layer_kernel, dims, list(scratch)),
        in_specs=[SMEM, SMEM] + [ANY] * 8 + [VMEM] * 7,
        out_specs=[ANY, ANY] + [VMEM] * 6,
        out_shape=[
            jax.ShapeDtypeStruct(shape, BF16),
            jax.ShapeDtypeStruct(shape, BF16),
            jax.ShapeDtypeStruct((chunks, 2, rows, cw), BF16),
            jax.ShapeDtypeStruct((1, 1, rows, w), BF16),
            jax.ShapeDtypeStruct((1, 1, rows, w), BF16),
            jax.ShapeDtypeStruct((1, 1, rows, 256), BF16),
            jax.ShapeDtypeStruct((8, width), F32),
            jax.ShapeDtypeStruct((tps * chunks, 1, cw), F32),
        ],
        scratch_shapes=shapes,
        compiler_params=pltpu.CompilerParams(
            vmem_limit_bytes=63 << 20, collective_id=1, has_side_effects=True
        ),
        name="layer",
    )(*arrays)


def settle_kernel(experts, *refs):
    given, made, held, sem = refs[:8], refs[8:22], refs[22:30], refs[30]
    out_to, grad_to, up_to, down_to, wo_to, wq_to, pair_to, router_to, bias_to, *vectors = made
    loads = [pltpu.make_async_copy(given[k], held[k], sem.at[k]) for k in range(8)]
    for load in loads:
        load.start()
    copies = [pltpu.make_async_copy(held[k], made[k], sem.at[8 + k]) for k in range(2)]
    for load in loads[2:]:
        load.wait()
    for load, copy in zip(loads, copies):
        load.wait()
        copy.start()
    ud, wo, wq, kr, vec, bias = held[2:]
    chunks, _, rows, cw = ud.shape
    for c in range(chunks):
        up_to[:, c * cw : (c + 1) * cw] = ud[c, 0].astype(F32)
        down_to[c * cw : (c + 1) * cw, :] = ud[c, 1].astype(F32).T
        bias_to[:, c * cw : (c + 1) * cw] = bias[lax.axis_index("tp") * chunks + c]
    wo_to[...] = wo[0, 0].astype(F32).T
    wq_to[...] = wq[0, 0].astype(F32).T
    pair_to[...] = kr[0, 0, :, 0:128].astype(F32)
    router = kr[0, 0, :, 128:256].astype(F32).T
    router_to[...] = router[0:experts] + router[experts : 2 * experts]
    for k, to in enumerate(vectors):
        to[...] = vec[k : k + 1, :]
    for copy in copies:
        copy.wait()


def run_settle(tps, experts, results):
    out, grad, ud, wo, wq, kr, vec, bias = results
    chunks, _, rows, cw = ud.shape
    w, width = wo.shape[3], vec.shape[1]

    def f32(*shape):
        return jax.ShapeDtypeStruct(shape, F32)

    return pl.pallas_call(
        functools.partial(settle_kernel, experts),
        in_specs=[ANY] * 8,
        out_specs=[ANY, ANY] + [VMEM] * 12,
        out_shape=[
            jax.ShapeDtypeStruct(out.shape, BF16),
            jax.ShapeDtypeStruct(out.shape, BF16),
            f32(rows, chunks * cw),
            f32(chunks * cw, rows),
            f32(w, rows),
            f32(w, rows),
            f32(rows, 128),
            f32(experts, rows),
            f32(1, chunks * cw),
        ]
        + [f32(1, width)] * 5,
        scratch_shapes=[pltpu.VMEM(r.shape, r.dtype) for r in results] + [pltpu.SemaphoreType.DMA((10,))],
        compiler_params=pltpu.CompilerParams(vmem_limit_bytes=60 << 20),
        name="settle",
    )(*results)


def per_device(
    mesh_sizes,
    tokens,
    expert_routes,
    picture_start,
    picture_mode,
    norm1_gain,
    norm1_bias,
    router_weight,
    query_weight,
    output_weight,
    key_value_weight,
    norm2_gain,
    norm2_bias,
    up_weight,
    up_bias,
    down_weight,
    down_bias,
    upstream_tokens,
):
    local_experts, rows_d, head = query_weight.shape
    experts = local_experts * mesh_sizes[2]
    width = tokens.shape[2]
    heads = local_experts * head

    def lines(vector):
        return vector.reshape(-1, 128)

    results = run_layer(
        mesh_sizes,
        tokens.shape[0],
        tokens.shape,
        experts,
        (
            picture_start,
            picture_mode,
            tokens,
            jnp.transpose(expert_routes, (0, 2, 1)),
            upstream_tokens,
            key_value_weight,
            jnp.transpose(query_weight, (0, 2, 1)).reshape(heads, rows_d),
            output_weight.reshape(heads, rows_d),
            up_weight,
            down_weight,
            router_weight.T,
            lines(up_bias),
            lines(norm1_gain),
            lines(norm1_bias),
            lines(norm2_gain),
            lines(norm2_bias),
            lines(down_bias),
        ),
    )
    outs = run_settle(mesh_sizes[2], experts, results)
    result, input_grad, up_out, down_out, wo_out, wq_out, pair_out, router_out, bias_out, *vectors = outs
    gain1, bias1, gain2, bias2, down_bias_sum = (v.reshape(width) for v in vectors)
    return (
        result,
        input_grad,
        gain1,
        bias1,
        router_out.T,
        jnp.transpose(wq_out.reshape(local_experts, head, rows_d), (0, 2, 1)),
        wo_out.reshape(output_weight.shape),
        pair_out,
        gain2,
        bias2,
        up_out,
        bias_out.reshape(-1),
        down_out,
        down_bias_sum,
    )


def solution(mesh):
    rows = P("fsdp", "ctx", None)
    placed = (
        rows,
        rows,
        P("fsdp", None),
        P("fsdp", None),
        P(),
        P(),
        P("fsdp", None),
        P("tp", "fsdp", None),
        P("tp", None, "fsdp"),
        P("fsdp", None),
        P(),
        P(),
        P("fsdp", "tp"),
        P("tp"),
        P("tp", "fsdp"),
        P(),
        rows,
    )
    sizes = tuple(mesh.shape[axis] for axis in ("fsdp", "ctx", "tp"))
    return jax.shard_map(
        functools.partial(per_device, sizes),
        mesh=mesh,
        in_specs=placed,
        out_specs=(
            rows,
            rows,
            P(),
            P(),
            P("fsdp", None),
            P("tp", "fsdp", None),
            P("tp", None, "fsdp"),
            P("fsdp", None),
            P(),
            P(),
            P("fsdp", "tp"),
            P("tp"),
            P("tp", "fsdp"),
            P(),
        ),
        check_vma=False,
    )
```

```python
import functools
import types

import jax
import jax.numpy as jnp
from jax import lax
from jax.experimental import pallas as pl
from jax.experimental.pallas import tpu as pltpu
from jax.sharding import PartitionSpec as P

PIC = 256
TINY = 1e-05
NEG = -1e30
F32 = jnp.float32
BF16 = jnp.bfloat16
TQ = 256
TK = 256
BIG = 1024
NT = (((1,), (1,)), ((), ()))
TN = (((0,), (0,)), ((), ()))


def dot(a, b):
    return jnp.dot(a, b, preferred_element_type=F32)


def dot_nt(a, b):
    return lax.dot_general(a, b, NT, preferred_element_type=F32)


def dot_tn(a, b):
    return lax.dot_general(a, b, TN, preferred_element_type=F32)


def picture_starts(start_ref, mode_ref, sequence, pics):
    return [jnp.where(mode_ref[sequence, k] == 1, start_ref[sequence, k], -(1 << 20)) for k in range(pics)]


def mask_of(q0, k0, keys, queries, starts):
    key_pos = k0 + lax.broadcasted_iota(jnp.int32, (keys, 1), 0)
    query_pos = q0 + lax.broadcasted_iota(jnp.int32, (1, queries), 1)
    key_id = jnp.full((keys, 1), -2, jnp.int32)
    query_id = jnp.full((1, queries), -1, jnp.int32)
    for k, start in enumerate(starts):
        key_id = jnp.where((key_pos >= start) & (key_pos < start + PIC), k, key_id)
        query_id = jnp.where((query_pos >= start) & (query_pos < start + PIC), k, query_id)
    allowed = (key_pos <= query_pos) | (key_id == query_id)
    return jnp.concatenate([allowed, allowed], axis=1)


SMEM = pl.BlockSpec(memory_space=pltpu.SMEM)
VMEM = pl.BlockSpec(memory_space=pltpu.VMEM)
ANY = pl.BlockSpec(memory_space=pl.ANY)
MESH = pl.DeviceIdType.MESH


def remote(src, dst, send, recv, to):
    return pltpu.make_async_remote_copy(
        src_ref=src, dst_ref=dst, send_sem=send, recv_sem=recv, device_id=to, device_id_type=MESH
    )


class Place:
    def __init__(self, sizes, sequences):
        self.fsdp, self.ctx, self.tp = sizes
        self.subs = self.tp // sequences
        self.blocks = self.ctx * self.subs
        self.f, self.x, self.t = (lax.axis_index(a) for a in ("fsdp", "ctx", "tp"))
        self.seq, self.sub = self.t // self.subs, self.t % self.subs
        self.block = self.x * self.subs + self.sub

    def owner(self, block):
        return {"ctx": block // self.subs, "tp": self.seq * self.subs + block % self.subs}

    def barrier(self):
        semaphore = pltpu.get_barrier_semaphore()
        count = 0
        for axis, size, me in (("fsdp", self.fsdp, self.f), ("ctx", self.ctx, self.x), ("tp", self.tp, self.t)):
            for r in range(1, size):
                pl.semaphore_signal(
                    semaphore, inc=1, device_id={axis: lax.rem(me + r, size)}, device_id_type=MESH
                )
                count += 1
        if self.subs > 1:
            for r in range(1, self.blocks):
                pl.semaphore_signal(
                    semaphore,
                    inc=1,
                    device_id=self.owner(lax.rem(self.block + r, self.blocks)),
                    device_id_type=MESH,
                )
                count += 1
        pl.semaphore_wait(semaphore, count)


class Reduce:
    def __init__(self, k, w, n, d, sizes, tp=True):
        self.k, self.w, self.n, self.d, self.sizes, self.tp = k, w, n, d, sizes, tp
        fsdp, ctx, tps = sizes
        self.rows, self.part = d // fsdp, d // fsdp // ctx
        self.count = 16 if tp else 15

    def scratch(self):
        k, w, n, d = self.k, self.w, self.n, self.d
        fsdp, ctx, tps = self.sizes
        dma = pltpu.SemaphoreType.DMA
        shapes = [
            pltpu.VMEM((n, k, d, w), BF16),
            pltpu.VMEM((n, fsdp - 1, k, self.rows, w), BF16),
            pltpu.VMEM((n, k, self.rows, w), F32),
            pltpu.VMEM((n, k, self.rows, w), BF16),
            pltpu.VMEM((n, ctx - 1, k, self.part, w), BF16),
            pltpu.VMEM((n, k, self.rows, w), BF16),
            dma((n, fsdp - 1)),
            dma((n, fsdp - 1)),
            dma((n, ctx - 1)),
            dma((n, ctx - 1)),
            dma((n, ctx - 1)),
            dma((n, ctx - 1)),
        ]
        if self.tp:
            shapes += [
                pltpu.VMEM((tps - 1, n, k, d, w), BF16),
                pltpu.VMEM((tps - 1, n, k, d, w), BF16),
                dma((tps - 1, n)),
                dma((tps - 1, n)),
            ]
        else:
            shapes += [pltpu.VMEM((tps, k, self.rows, w), F32), dma((tps - 1,)), dma((tps - 1,))]
        return shapes

    def bind(self, place, refs):
        self.place = place
        self.s2, self.r2, self.own, self.s3, self.r3, self.fin = refs[:6]
        self.m2, self.m3, self.m4 = refs[6:8], refs[8:10], refs[10:12]
        if self.tp:
            self.s1, self.r1 = refs[12:14]
            self.m1 = refs[14:16]
        else:
            self.all, self.m1 = refs[12], refs[13:15]

    def d1(self, o, c):
        p = self.place
        to = {"tp": lax.rem(p.t + o, p.tp)}
        if self.tp:
            return remote(
                self.s1.at[o - 1, c], self.r1.at[o - 1, c], self.m1[0].at[o - 1, c], self.m1[1].at[o - 1, c], to
            )
        return remote(self.all.at[p.t], self.all.at[p.t], self.m1[0].at[o - 1], self.m1[1].at[o - 1], to)

    def d2(self, r, c):
        p = self.place
        to = lax.rem(p.f + r, p.fsdp)
        rows = pl.ds(pl.multiple_of(to * self.rows, self.rows), self.rows)
        return remote(
            self.s2.at[c, :, rows, :],
            self.r2.at[c, r - 1],
            self.m2[0].at[c, r - 1],
            self.m2[1].at[c, r - 1],
            {"fsdp": to},
        )

    def spot(self, x):
        return pl.ds(pl.multiple_of(x * self.part, self.part), self.part)

    def d3(self, q, c):
        p = self.place
        to = lax.rem(p.x + q, p.ctx)
        return remote(
            self.s3.at[c, :, self.spot(to), :],
            self.r3.at[c, q - 1],
            self.m3[0].at[c, q - 1],
            self.m3[1].at[c, q - 1],
            {"ctx": to},
        )

    def d4(self, q, c):
        p = self.place
        to = lax.rem(p.x + q, p.ctx)
        mine = self.fin.at[c, :, self.spot(p.x), :]
        return remote(mine, mine, self.m4[0].at[c, q - 1], self.m4[1].at[c, q - 1], {"ctx": to})

    def put(self, o, c, k, value):
        self.s1[o - 1, c, k] = value.astype(BF16)

    def give(self, o, c):
        self.d1(o, c).start()

    def take(self, c, acc):
        p, w = self.place, self.w
        if self.tp:
            for o in range(1, p.tp):
                self.d1(o, c).wait_recv()
            for k in range(self.k):
                total = acc[k, :, 0:w]
                for o in range(1, p.tp):
                    total = total + self.r1[o - 1, c, k].astype(F32)
                acc[k, :, 0:w] = total
        for k in range(self.k):
            self.s2[c, k] = acc[k, :, 0:w].astype(BF16)
        for r in range(1, p.fsdp):
            self.d2(r, c).start()
        for k in range(self.k):
            self.own[c, k] = acc[k, pl.ds(pl.multiple_of(p.f * self.rows, self.rows), self.rows), 0:w]

    def fold(self, c):
        p = self.place
        for r in range(1, p.fsdp):
            self.d2(r, c).wait_recv()
        for k in range(self.k):
            total = self.own[c, k]
            for r in range(1, p.fsdp):
                total = total + self.r2[c, r - 1, k].astype(F32)
            if self.tp:
                self.own[c, k] = total
                self.s3[c, k] = total.astype(BF16)
            else:
                self.all[p.t, k] = total
        if self.tp:
            for q in range(1, p.ctx):
                self.d3(q, c).start()
        else:
            for o in range(1, p.tp):
                self.d1(o, c).start()

    def share(self, c):
        p = self.place
        for o in range(1, p.tp):
            self.d1(o, c).wait_recv()
        for k in range(self.k):
            total = self.all[0, k]
            for o in range(1, p.tp):
                total = total + self.all[o, k]
            self.own[c, k] = total
            self.s3[c, k] = total.astype(BF16)
        for q in range(1, p.ctx):
            self.d3(q, c).start()

    def finish(self, c):
        p = self.place
        for q in range(1, p.ctx):
            self.d3(q, c).wait_recv()
        for k in range(self.k):
            total = self.own[c, k, self.spot(p.x), :]
            for q in range(1, p.ctx):
                total = total + self.r3[c, q - 1, k].astype(F32)
            self.fin[c, k, self.spot(p.x), :] = total.astype(BF16)
        for q in range(1, p.ctx):
            self.d4(q, c).start()

    def close(self):
        p = self.place

        @pl.loop(0, self.n)
        def _(c):
            for q in range(1, p.ctx):
                self.d4(q, c).wait()
                self.d3(q, c).wait_send()
            for r in range(1, p.fsdp):
                self.d2(r, c).wait_send()
            for o in range(1, p.tp):
                self.d1(o, c).wait_send()


class Everywhere:
    def __init__(self, shape, sizes):
        self.shape, self.sizes, self.count = shape, sizes, 9

    def scratch(self):
        dma = pltpu.SemaphoreType.DMA
        shapes = []
        for size in self.sizes:
            shapes += [pltpu.VMEM((size,) + self.shape, F32), dma((size - 1,)), dma((size - 1,))]
        return shapes

    def bind(self, place, refs):
        self.place, self.refs = place, refs

    def copy(self, stage, r):
        p = self.place
        axis, size, me = (
            ("fsdp", p.fsdp, p.f),
            ("ctx", p.ctx, p.x),
            ("tp", p.tp, p.t),
        )[stage]
        buf, send, recv = self.refs[3 * stage : 3 * stage + 3]
        return remote(
            buf.at[me], buf.at[me], send.at[r - 1], recv.at[r - 1], {axis: lax.rem(me + r, size)}
        )

    def start(self, stage, value):
        p = self.place
        me = (p.f, p.x, p.t)[stage]
        self.refs[3 * stage][me] = value
        for r in range(1, self.sizes[stage]):
            self.copy(stage, r).start()

    def total(self, stage):
        buf = self.refs[3 * stage]
        for r in range(1, self.sizes[stage]):
            self.copy(stage, r).wait()
        total = buf[0]
        for r in range(1, self.sizes[stage]):
            total = total + buf[r]
        return total


def norm_back(grad, normed, inverse, gain):
    scaled = grad * gain
    inner = (
        scaled
        - jnp.mean(scaled, axis=-1, keepdims=True)
        - normed * jnp.mean(scaled * normed, axis=-1, keepdims=True)
    )
    return inner * inverse


def half_lanes(rows):
    return lax.broadcasted_iota(jnp.int32, (rows, 128), 1)


def both_halves(values, upper):
    low = half_lanes(values.shape[0]) < 64
    turned = pltpu.roll(values, 64, 1)
    return jnp.where(low, turned, values) if upper else jnp.where(low, values, turned)


class Gather:
    def __init__(self, place, shard, spot, to_tp, refs):
        self.place, self.shard, self.spot, self.to_tp = place, shard, spot, to_tp
        self.fsend, self.frecv, self.tsend, self.trecv, self.local = refs

    def keep(self):
        p = self.place
        return pltpu.make_async_copy(self.shard, self.spot(p.t, p.f), self.local.at[0])

    def across(self, r):
        p = self.place
        return remote(
            self.shard,
            self.spot(p.t, p.f),
            self.fsend.at[r - 1],
            self.frecv.at[r - 1],
            {"fsdp": lax.rem(p.f + r, p.fsdp)},
        )

    def beside(self, o, r):
        p = self.place
        spot = self.spot(p.t, lax.rem(p.f - r + p.fsdp, p.fsdp))
        return remote(
            self.shard if r == 0 else spot,
            spot,
            self.tsend.at[o - 1, r],
            self.trecv.at[o - 1, r],
            {"tp": lax.rem(p.t + o, p.tp)},
        )

    def begin(self):
        p = self.place
        for r in range(1, p.fsdp):
            self.across(r).start()
        if self.to_tp:
            for o in range(1, p.tp):
                self.beside(o, 0).start()
        self.keep().start()

    def forward(self):
        p = self.place
        for r in range(1, p.fsdp):
            self.across(r).wait_recv()
            if self.to_tp:
                for o in range(1, p.tp):
                    self.beside(o, r).start()
        self.keep().wait()

    def arrive(self):
        p = self.place
        if self.to_tp:
            for o in range(1, p.tp):
                for r in range(p.fsdp):
                    self.beside(o, r).wait_recv()

    def close(self):
        p = self.place
        for r in range(1, p.fsdp):
            self.across(r).wait_send()
        if self.to_tp:
            for o in range(1, p.tp):
                for r in range(p.fsdp):
                    self.beside(o, r).wait_send()


INPUTS = ["pic_start", "pic_mode", "tokens", "routes", "upstream"]
INPUTS += ["kv_shard", "wq_shard", "wo_shard", "up_shard", "down_shard"]
INPUTS += ["router_in", "bias_in", "gain1_in", "bias1_in", "gain2_in", "bias2_in", "down_bias_in"]
OUTPUTS = ["out_hbm", "grad_hbm", "ud_out", "wo_out", "wq_out", "kr_out", "vec_out", "bias_out"]
FIRST = ["kv", "rt", "wq"]
FSDP_ONLY = ["kv", "rt"]


def layer_kernel(dims, names, *refs):
    sizes, sequences, tokens, width, experts, pics, length, reducers = dims
    fsdp, ctx, tps = sizes
    named = INPUTS + OUTPUTS + names
    a = types.SimpleNamespace(**dict(zip(named, refs[: len(named)])))
    rest = refs[len(named) :]
    r_ud, r_wo, r_wq, r_kr, r_vec, r_bias = reducers
    place = Place(sizes, sequences)
    for reducer in reducers:
        reducer.bind(place, rest[: reducer.count])
        rest = rest[reducer.count :]
    tiles = tokens // TQ
    cw, chunks = r_ud.w, r_ud.n
    rows_t = min(1024, tokens)
    big = min(BIG, tokens)
    shard_rows = width // fsdp

    def span(index, size):
        return pl.ds(pl.multiple_of(index * size, size), size)

    spots = dict(
        kv=lambda t, f: a.wkv.at[span(f, shard_rows), :],
        rt=lambda t, f: a.rpad.at[0:16, span(f, shard_rows)],
        wq=lambda t, f: a.wq.at[t, :, span(f, shard_rows)],
        wo=lambda t, f: a.wo.at[t, :, span(f, shard_rows)],
    )
    shards = dict(kv=a.kv_shard, rt=a.rt_shard, wq=a.wq_shard, wo=a.wo_shard)
    later = ["wo"]
    for c in range(chunks):
        cut = slice(c * cw, (c + 1) * cw)
        up, down = "up%d" % c, "down%d" % c
        later += [up, down]
        shards[up], shards[down] = a.up_shard.at[:, cut], a.down_shard.at[cut, :]
        spots[up] = lambda t, f, cut=cut: a.up.at[t, span(f, shard_rows), cut]
        spots[down] = lambda t, f, cut=cut: a.down.at[t, cut, span(f, shard_rows)]
    weights = {}
    for name in FIRST + later:
        weights[name] = Gather(place, shards[name], spots[name], name not in FSDP_ONLY, rest[:5])
        rest = rest[5:]

    own_slice = (place.seq, pl.ds(pl.multiple_of(place.sub * tokens, tokens), tokens))
    loads = [
        pltpu.make_async_copy(source.at[own_slice[0], own_slice[1], :], target, a.load_sem.at[k])
        for k, (source, target) in enumerate(
            ((a.tokens, a.tok), (a.upstream, a.ups))
        )
    ]
    loads.append(
        pltpu.make_async_copy(
            a.routes.at[place.seq, :, pl.ds(pl.multiple_of(place.sub * tokens, tokens), tokens)], a.rt, a.load_sem.at[2]
        )
    )
    for load in loads:
        load.start()

    router = a.router_in[...].astype(F32)
    a.rt_shard[...] = jnp.concatenate([router, router], axis=0).astype(BF16)
    a.rpad[16:, :] = jnp.zeros((112, width), BF16)
    a.bias_shard[...] = a.bias_in[...].astype(F32)
    a.bias_raw[place.t] = a.bias_shard[...]
    place.barrier()
    for name in FIRST:
        weights[name].begin()

    def bias_copy(o):
        spot = a.bias_raw.at[place.t]
        return remote(
            a.bias_shard, spot, a.bias_sem.at[0, o - 1], a.bias_sem.at[1, o - 1], {"tp": lax.rem(place.t + o, tps)}
        )

    for o in range(1, tps):
        bias_copy(o).start()

    def row(ref):
        values = ref[...].astype(F32)
        return jnp.concatenate([values[k : k + 1, :] for k in range(values.shape[0])], axis=1)

    gain1, bias1 = row(a.gain1_in), row(a.bias1_in)
    q_base = place.block * tokens
    starts = picture_starts(a.pic_start, a.pic_mode, place.seq, pics)
    lanes = half_lanes(TQ)
    own_rows = pl.ds(pl.multiple_of(q_base, tokens), tokens)

    def tile_rows(i):
        return span(i, TQ)

    def gates(rows):
        return [a.meta[rows, k : k + 1] for k in range(4)]

    def expert_of(c):
        return 2 * c + jnp.where(lanes >= 64, 1, 0)

    def normalise(x):
        center = x - jnp.mean(x, axis=-1, keepdims=True)
        inverse = lax.rsqrt(jnp.mean(center * center, axis=-1, keepdims=True) + TINY)
        return center * inverse, inverse

    def choose(full, r):
        expert = r.astype(jnp.int32)
        chosen = jnp.zeros((TQ, 128), F32)
        for c in range(experts // 2):
            chosen = jnp.where(expert == expert_of(c), full[:, c * 128 : (c + 1) * 128], chosen)
        return chosen + pltpu.roll(chosen, 64, 1)

    loads[0].wait()
    loads[2].wait()

    @pl.loop(0, tiles)
    def _(i):
        rows = tile_rows(i)
        normed, _ = normalise(a.tok[rows, :].astype(F32))
        a.hid1[rows, :] = (normed * gain1 + bias1).astype(BF16)

    a.kv[pl.ds(length, TQ), :] = jnp.zeros((TQ, 128), BF16)
    weights["kv"].forward()

    @pl.loop(0, tiles)
    def _(i):
        rows = tile_rows(i)
        pair = dot(a.hid1[rows, :], a.wkv[...])
        a.kv[pl.ds(pl.multiple_of(q_base + i * TQ, TQ), TQ), :] = pair.astype(BF16)

    after_me, before_me = place.block + 1 < place.blocks, place.block > 0

    def pass_on(d):
        keys = pl.ds(pl.multiple_of((place.block - d) * tokens, tokens), tokens)
        to = place.owner(lax.rem(place.block + 1, place.blocks))
        return remote(a.kv.at[keys, :], a.kv.at[keys, :], a.kv_sem.at[0, d], a.kv_sem.at[1, d], to)

    def reach_back():
        keys = pl.ds(pl.multiple_of(q_base, TQ), TQ)
        to = place.owner(lax.rem(place.block + place.blocks - 1, place.blocks))
        return remote(a.kv.at[keys, :], a.kv.at[keys, :], a.near_sem.at[2], a.near_sem.at[3], to)

    @pl.when(after_me)
    def _():
        pass_on(0).start()

    @pl.when(before_me)
    def _():
        reach_back().start()

    weights["rt"].forward()

    @pl.loop(0, tiles)
    def _(i):
        rows = tile_rows(i)
        logits = dot_nt(a.hid1[rows, :], a.rpad[...])
        pairs = jnp.concatenate([a.rt[:, rows].astype(F32)] * 4, axis=0).T
        r0, r1 = pairs[:, 0:1].astype(jnp.int32), pairs[:, 1:2].astype(jnp.int32)
        l0 = jnp.sum(jnp.where(lanes == r0, logits, 0.0), axis=-1, keepdims=True)
        l1 = jnp.sum(jnp.where(lanes == r1, logits, 0.0), axis=-1, keepdims=True)
        top = jnp.maximum(l0, l1)
        e0, e1 = jnp.exp(l0 - top), jnp.exp(l1 - top)
        a.meta[rows, 0:1] = e0 / (e0 + e1)
        a.meta[rows, 1:2] = e1 / (e0 + e1)
        a.meta[rows, 2:3] = r0.astype(F32)
        a.meta[rows, 3:4] = r1.astype(F32)

    weights["wq"].forward()
    for name in later:
        weights[name].begin()
    weights["wq"].arrive()

    @pl.loop(0, tiles)
    def _(i):
        rows = tile_rows(i)
        _, _, r0, r1 = gates(rows)
        full = dot_nt(a.hid1[rows, :], a.wq[...].reshape(width, width))
        for s, r in enumerate((r0, r1)):
            a.q[s, rows, :] = jnp.where(lanes < 64, choose(full, r) * 0.125, 0.0).astype(BF16)

    @pl.loop(0, tiles)
    def _(i):
        a.top[i] = jnp.full((1, 2 * TQ), NEG, F32)
        a.total[i] = jnp.zeros((1, 2 * TQ), F32)
    a.dqt[...] = jnp.zeros_like(a.dqt)

    def look(i, k0, size, masked):
        rows = tile_rows(i)
        keys = pl.ds(pl.multiple_of(k0, TK), size)
        q = jnp.concatenate([a.q[0, rows, :], a.q[1, rows, :]], axis=0)
        pair = a.kv[keys, :]
        scores = dot_nt(pair, q)
        if masked:
            scores = jnp.where(mask_of(q_base + i * TQ, k0, size, TQ, starts), scores, NEG)
        before = a.top[i]
        now = jnp.maximum(before, jnp.max(scores, axis=0, keepdims=True))
        probs = jnp.exp(scores - now)
        scale = jnp.exp(before - now)
        a.top[i] = now
        a.total[i] = a.total[i] * scale + jnp.sum(probs, axis=0, keepdims=True)
        a.dqt[i] = a.dqt[i] * scale + dot_tn(pair, probs.astype(BF16))

    @pl.when(after_me)
    def _():
        reach_back().wait_recv()

    @pl.loop(0, tiles)
    def _(i):
        look(i, q_base + i * TK, 2 * TK, True)

    for i in range(1, tiles):
        look(i, q_base, i * TK, False)

    @pl.loop(0, place.blocks - 1)
    def _(j):
        @pl.when(j < place.block)
        def _():
            pass_on(j).wait_recv()

            @pl.when(after_me)
            def _():
                pass_on(j + 1).start()

            @pl.loop(0, tokens // big)
            def _(k):
                @pl.loop(0, tiles)
                def _(i):
                    look(i, (place.block - 1 - j) * tokens + k * big, big, False)

        @pl.when(j == place.blocks - 2)
        def _():
            weights["wo"].forward()

    weights["up0"].forward()
    weights["down0"].forward()

    @pl.loop(0, tiles)
    def _(i):
        rows = tile_rows(i)
        both = (a.dqt[i] / a.total[i]).T
        a.att[0, rows, :] = both[:TQ]
        a.att[1, rows, :] = both[TQ:]
        a.logt[i] = a.top[i] + jnp.log(a.total[i])

    gain2, bias2, down_bias = row(a.gain2_in), row(a.bias2_in), row(a.down_bias_in)
    a.vec[...] = jnp.zeros_like(a.vec)
    a.bias_acc[...] = jnp.zeros_like(a.bias_acc)
    a.woacc[...] = jnp.zeros_like(a.woacc)
    weights["wo"].arrive()

    @pl.loop(0, tiles)
    def _(i):
        rows = tile_rows(i)
        g0, g1, r0, r1 = gates(rows)
        after = a.tok[rows, :].astype(F32)
        out_w = a.wo[...].reshape(width, width)
        for s, (g, r) in enumerate(((g0, r0), (g1, r1))):
            twice = both_halves(a.att[s, rows, :], True)
            expert = r.astype(jnp.int32)
            for c in range(experts // 2):
                a.wide[s, rows, c * 128 : (c + 1) * 128] = jnp.where(expert == expert_of(c), twice, 0.0).astype(BF16)
            projected = dot(a.wide[s, rows, :], out_w)
            a.proj[s, rows, :] = projected
            after = after + g * projected
        normed, inverse = normalise(after)
        a.normed2[rows, :] = normed
        a.inv2[rows, :] = inverse
        a.hid2[rows, :] = (normed * gain2 + bias2).astype(BF16)
        a.out_acc[rows, :] = after + down_bias
        a.mid[rows, :] = jnp.zeros_like(after)

    loads[1].wait()
    for o in range(1, tps):
        bias_copy(o).wait_recv()
    lines = cw // 128
    for t in range(tps):
        for c in range(chunks):
            a.up_bias[t * chunks + c] = jnp.concatenate(
                [a.bias_raw[t, c * lines + k : c * lines + k + 1, :] for k in range(lines)], axis=1
            )

    def feed(t, c):
        cols = span(c, cw)
        whole = tokens == rows_t
        if not whole:
            a.gacc[...] = jnp.zeros_like(a.gacc)

        @pl.loop(0, tokens // rows_t)
        def _(i):
            rows = span(i, rows_t)
            h2, u = a.hid2[rows, :], a.ups[rows, :]
            pre = dot(h2, a.up[t, :, cols]) + a.up_bias[t * chunks + c]
            sig = 1.0 / (1.0 + jnp.exp(-pre))
            active = (pre * sig).astype(BF16)
            a.out_acc[rows, :] += dot(active, a.down[t, cols, :])
            down_part = dot_tn(u, active)
            a.gacc[1, :, 0:cw] = down_part if whole else a.gacc[1, :, 0:cw] + down_part
            slope = sig * (1.0 + pre * (1.0 - sig))
            grad = dot_nt(u, a.down[t, cols, :]) * slope
            low = grad.astype(BF16)
            a.bias_acc[t * chunks + c] += jnp.sum(low.astype(F32), axis=0, keepdims=True)
            up_part = dot_tn(h2, low)
            a.gacc[0, :, 0:cw] = up_part if whole else a.gacc[0, :, 0:cw] + up_part
            a.mid[rows, :] += dot_nt(low, a.up[t, :, cols])

    @pl.loop(0, chunks)
    def _(c):
        for k in range(chunks):

            @pl.when(c == k)
            def _():
                weights["up%d" % k].arrive()
                weights["down%d" % k].arrive()

        for o in range(1, tps):
            feed(lax.rem(place.t + o, tps), c)
            for k in range(2):
                r_ud.put(o, c, k, a.gacc[k, :, 0:cw])
            r_ud.give(o, c)
        for k in range(1, chunks):

            @pl.when(c + 1 == k)
            def _():
                weights["up%d" % k].forward()
                weights["down%d" % k].forward()

        feed(place.t, c)
        r_ud.take(c, a.gacc)

    r_bias.start(2, a.bias_acc[...])

    def share_out(low, hbm, slot):
        spot = hbm.at[own_slice[0], own_slice[1], :]
        copies = [
            remote(
                low, spot, a.out_sem.at[0, slot, o - 1], a.out_sem.at[1, slot, o - 1], {"tp": lax.rem(place.t + o, tps)}
            )
            for o in range(1, tps)
        ]
        copies.append(pltpu.make_async_copy(low, spot, a.loc_sem.at[slot]))
        for copy in copies:
            copy.start()
        return copies

    def add_row(k, value):
        a.vec[k : k + 1, :] += jnp.sum(value, axis=0, keepdims=True)

    @pl.loop(0, tiles)
    def _(i):
        rows = tile_rows(i)
        g0, g1, r0, r1 = gates(rows)
        out_w = a.wo[...].reshape(width, width)
        a.res_low[rows, :] = a.out_acc[rows, :].astype(BF16)
        upstream = a.ups[rows, :].astype(F32)
        grad, normed = a.mid[rows, :], a.normed2[rows, :]
        resid = upstream + norm_back(grad, normed, a.inv2[rows, :], gain2)
        a.mid[rows, :] = resid
        add_row(2, grad * normed)
        add_row(3, grad)
        add_row(4, upstream)
        d0 = jnp.sum(a.proj[0, rows, :] * resid, axis=-1, keepdims=True)
        d1 = jnp.sum(a.proj[1, rows, :] * resid, axis=-1, keepdims=True)
        mean = g0 * d0 + g1 * d1
        for s, (g, r) in enumerate(((g0, r0), (g1, r1))):
            low = (g * resid).astype(BF16)
            a.woacc[0] += dot_tn(low, a.wide[s, rows, :])
            chosen = jnp.where(lanes >= 64, choose(dot_nt(low, out_w), r), 0.0).astype(BF16)
            a.da[s, rows, :] = chosen
            product = chosen.astype(F32) * jnp.where(lanes >= 64, a.att[s, rows, :], 0.0)
            a.delta[i, :, s * TQ : (s + 1) * TQ] = jnp.sum(product.T, axis=0, keepdims=True)
        lane_expert = lax.rem(lanes, experts)
        lg = jnp.where(lane_expert == r0.astype(jnp.int32), g0 * (d0 - mean), 0.0)
        lg = lg + jnp.where(lane_expert == r1.astype(jnp.int32), g1 * (d1 - mean), 0.0)
        high = lg.astype(BF16).astype(F32)
        a.lgp[rows, :] = jnp.where(
            lanes < experts, high, jnp.where(lanes < 2 * experts, lg - high, 0.0)
        ).astype(BF16)

    out_copies = share_out(a.res_low, a.out_hbm, 0)

    def hand_out(reducer, acc):
        w = reducer.w
        for t in range(tps):

            @pl.when(t != place.t)
            def _():
                o = lax.rem(t - place.t + tps, tps)
                reducer.s1[o - 1, 0, 0] = acc[0, :, t * w : (t + 1) * w].astype(BF16)
                reducer.give(o, 0)

    def take_own(reducer, acc):
        w = reducer.w
        for t in range(tps):

            @pl.when(t == place.t)
            def _():
                a.gacc[0, :, 0:w] = acc[0, :, t * w : (t + 1) * w]

        reducer.take(0, a.gacc)

    hand_out(r_wo, a.woacc)
    r_bias.start(0, r_bias.total(2))

    a.dqt[...] = jnp.zeros_like(a.dqt)
    a.dkv[...] = jnp.zeros_like(a.dkv)

    def attend(i, k0, size, masked):
        rows = tile_rows(i)
        keys = pl.ds(pl.multiple_of(k0, TK), size)
        q = jnp.concatenate([a.q[0, rows, :], a.q[1, rows, :]], axis=0)
        d_att = jnp.concatenate([a.da[0, rows, :], a.da[1, rows, :]], axis=0)
        pair = a.kv[keys, :]
        scores = dot_nt(pair, q)
        if masked:
            scores = jnp.where(mask_of(q_base + i * TQ, k0, size, TQ, starts), scores, NEG)
        probs = jnp.exp(scores - a.logt[i])
        prob_grad = dot_nt(pair, d_att)
        score_grad = (probs * (prob_grad - a.delta[i])).astype(BF16)
        a.dkv[keys, :] += dot(score_grad, q) + dot(probs.astype(BF16), d_att)
        a.dqt[i] += dot_tn(pair, score_grad)

    def dkv_copy(block):
        return remote(
            a.dkv_send.at[block],
            a.dkv_recv.at[block],
            a.dkv_sem.at[0, block],
            a.dkv_sem.at[1, block],
            place.owner(lax.rem(place.block + place.blocks - 1, place.blocks)),
        )

    def hand_down(block):
        keys = span(block, tokens)

        @pl.when(after_me)
        def _():
            dkv_copy(block).wait_recv()
            a.dkv[keys, :] += a.dkv_recv[block].astype(F32)

        a.dkv_send[block] = a.dkv[keys, :].astype(BF16)
        dkv_copy(block).start()

    @pl.loop(0, place.blocks - 1)
    def _(j):
        @pl.when(j < place.block)
        def _():
            @pl.loop(0, tokens // big)
            def _(k):
                @pl.loop(0, tiles)
                def _(i):
                    attend(i, j * tokens + k * big, big, False)

            ready = j - jnp.where(after_me, 1, 0)

            @pl.when(ready >= 0)
            def _():
                hand_down(ready)

    take_own(r_wo, a.woacc)
    r_bias.start(1, r_bias.total(0))

    @pl.loop(0, tiles)
    def _(i):
        attend(i, q_base + i * TK, 2 * TK, True)

    for i in range(1, tiles):
        attend(i, q_base, i * TK, False)

    @pl.when(after_me & before_me)
    def _():
        hand_down(place.block - 1)

    def near_copy():
        return remote(
            a.near_send,
            a.near_buf,
            a.near_sem.at[0],
            a.near_sem.at[1],
            place.owner(lax.rem(place.block + 1, place.blocks)),
        )

    @pl.when(after_me)
    def _():
        a.near_send[...] = a.dkv[pl.ds(pl.multiple_of((place.block + 1) * tokens, TQ), TQ), :].astype(BF16)
        near_copy().start()

    r_ud.fold(0)
    r_wo.fold(0)

    @pl.loop(0, tiles)
    def _(i):
        rows = tile_rows(i)
        _, _, r0, r1 = gates(rows)
        dq = (a.dqt[i] * 0.125).T
        first, second = both_halves(dq[:TQ], False), both_halves(dq[TQ:], False)
        for c in range(experts // 2):
            column = jnp.where(r0.astype(jnp.int32) == expert_of(c), first, 0.0)
            column = jnp.where(r1.astype(jnp.int32) == expert_of(c), second, column)
            a.dqw[rows, c * 128 : (c + 1) * 128] = column.astype(BF16)

    a.woacc[0] = dot_tn(a.hid1[...], a.dqw[...])
    hand_out(r_wq, a.woacc)

    for c in range(1, chunks):
        r_ud.fold(c)

    @pl.when(after_me)
    def _():
        dkv_copy(place.block).wait_recv()
        a.dkv[own_rows, :] += a.dkv_recv[place.block].astype(F32)

    @pl.when(before_me)
    def _():
        near_copy().wait_recv()
        a.dkv[pl.ds(pl.multiple_of(q_base, TQ), TQ), :] += a.near_buf[...].astype(F32)

    a.pairg[:, 0:128] = a.dkv[own_rows, :].astype(BF16)
    a.pairg[:, 128:256] = a.lgp[...]
    a.gacc[0, :, 0:256] = dot_tn(a.hid1[...], a.pairg[...])
    r_kr.take(0, a.gacc)
    take_own(r_wq, a.woacc)
    r_ud.finish(0)
    r_wo.finish(0)

    @pl.loop(0, tiles)
    def _(i):
        rows = tile_rows(i)
        normed, inverse = normalise(a.tok[rows, :].astype(F32))
        grad = dot(a.dqw[rows, :], a.wq[...].reshape(width, width))
        grad = grad + dot_nt(a.pairg[rows, 0:128], a.wkv[...]) + dot(a.lgp[rows, :], a.rpad[...])
        add_row(0, grad * normed)
        add_row(1, grad)
        a.grad_low[rows, :] = (a.mid[rows, :] + norm_back(grad, normed, inverse, gain1)).astype(BF16)

    grad_copies = share_out(a.grad_low, a.grad_hbm, 1)
    r_vec.start(2, a.vec[...])
    r_kr.fold(0)
    r_wq.fold(0)
    r_vec.start(0, r_vec.total(2))
    r_kr.share(0)
    for c in range(1, chunks):
        r_ud.finish(c)
    r_vec.start(1, r_vec.total(0))
    r_wq.finish(0)
    r_kr.finish(0)
    a.vec_out[...] = r_vec.total(1)
    a.bias_out[...] = r_bias.total(1)
    for reducer, out in ((r_ud, a.ud_out), (r_wo, a.wo_out), (r_wq, a.wq_out), (r_kr, a.kr_out)):
        reducer.close()
        out[...] = reducer.fin[...]

    @pl.loop(0, place.block)
    def _(j):
        dkv_copy(j).wait_send()

    @pl.when(after_me)
    def _():
        near_copy().wait_send()

        @pl.loop(0, place.block + 1)
        def _(d):
            pass_on(d).wait_send()

    @pl.when(before_me)
    def _():
        reach_back().wait_send()

    for name in FIRST + later:
        weights[name].close()
    for o in range(1, tps):
        bias_copy(o).wait_send()
    for copy in out_copies + grad_copies:
        copy.wait()


def run_layer(sizes, sequences, shape, experts, arrays):
    fsdp, ctx, tps = sizes
    subs = tps // sequences
    width = shape[2]
    tokens = shape[1] // subs
    length = shape[1] * ctx
    blocks = ctx * subs
    tiles = tokens // TQ
    local_hidden = arrays[8].shape[1]
    cw = min(512, local_hidden)
    chunks = local_hidden // cw
    w = width // tps
    reducers = (
        Reduce(2, cw, chunks, width, sizes),
        Reduce(1, w, 1, width, sizes),
        Reduce(1, w, 1, width, sizes),
        Reduce(1, 256, 1, width, sizes, tp=False),
        Everywhere((8, width), sizes),
        Everywhere((tps * chunks, 1, cw), sizes),
    )
    dims = (sizes, sequences, tokens, width, experts, arrays[0].shape[1], length, reducers)
    rows = width // fsdp
    dma = pltpu.SemaphoreType.DMA
    vmem = pltpu.VMEM
    scratch = dict(
        tok=vmem((tokens, width), BF16),
        rt=vmem((2, tokens), jnp.int32),
        ups=vmem((tokens, width), BF16),
        load_sem=dma((3,)),
        wkv=vmem((width, 128), BF16),
        rt_shard=vmem((16, rows), BF16),
        rpad=vmem((128, width), BF16),
        wq=vmem((tps, w, width), BF16),
        wo=vmem((tps, w, width), BF16),
        up=vmem((tps, width, local_hidden), BF16),
        down=vmem((tps, local_hidden, width), BF16),
        bias_shard=vmem((local_hidden // 128, 128), F32),
        bias_raw=vmem((tps, local_hidden // 128, 128), F32),
        up_bias=vmem((tps * chunks, 1, cw), F32),
        bias_sem=dma((2, tps - 1)),
        meta=vmem((tokens, 8), F32),
        hid1=vmem((tokens, width), BF16),
        q=vmem((2, tokens, 128), BF16),
        kv=vmem((length + TQ, 128), BF16),
        kv_sem=dma((2, blocks)),
        near_sem=dma((4,)),
        top=vmem((tiles, 1, 2 * TQ), F32),
        total=vmem((tiles, 1, 2 * TQ), F32),
        att=vmem((2, tokens, 128), F32),
        logt=vmem((tiles, 1, 2 * TQ), F32),
        wide=vmem((2, tokens, width), BF16),
        proj=vmem((2, tokens, width), F32),
        normed2=vmem((tokens, width), F32),
        hid2=vmem((tokens, width), BF16),
        out_acc=vmem((tokens, width), F32),
        mid=vmem((tokens, width), F32),
        inv2=vmem((tokens, 1), F32),
        gacc=vmem((2, width, max(cw, 256)), F32),
        woacc=vmem((1, width, width), F32),
        da=vmem((2, tokens, 128), BF16),
        delta=vmem((tiles, 1, 2 * TQ), F32),
        lgp=vmem((tokens, 128), BF16),
        dqt=vmem((tiles, 128, 2 * TQ), F32),
        dkv=vmem((length + TQ, 128), F32),
        dkv_send=vmem((blocks - 1, tokens, 128), BF16),
        dkv_recv=vmem((blocks - 1, tokens, 128), BF16),
        dkv_sem=dma((2, blocks - 1)),
        dqw=vmem((tokens, width), BF16),
        pairg=vmem((tokens, 256), BF16),
        vec=vmem((8, width), F32),
        bias_acc=vmem((tps * chunks, 1, cw), F32),
        res_low=vmem((tokens, width), BF16),
        grad_low=vmem((tokens, width), BF16),
        near_buf=vmem((TQ, 128), BF16),
        near_send=vmem((TQ, 128), BF16),
        loc_sem=dma((2,)),
        out_sem=dma((2, 2, tps - 1)),
    )
    shapes = list(scratch.values())
    for reducer in reducers:
        shapes += reducer.scratch()
    for _ in range(len(FIRST) + 1 + 2 * chunks):
        shapes += [dma((fsdp - 1,)), dma((fsdp - 1,)), dma((tps - 1, fsdp)), dma((tps - 1, fsdp)), dma((1,))]
    return pl.pallas_call(
        functools.partial(layer_kernel, dims, list(scratch)),
        in_specs=[SMEM, SMEM] + [ANY] * 8 + [VMEM] * 7,
        out_specs=[ANY, ANY] + [VMEM] * 6,
        out_shape=[
            jax.ShapeDtypeStruct(shape, BF16),
            jax.ShapeDtypeStruct(shape, BF16),
            jax.ShapeDtypeStruct((chunks, 2, rows, cw), BF16),
            jax.ShapeDtypeStruct((1, 1, rows, w), BF16),
            jax.ShapeDtypeStruct((1, 1, rows, w), BF16),
            jax.ShapeDtypeStruct((1, 1, rows, 256), BF16),
            jax.ShapeDtypeStruct((8, width), F32),
            jax.ShapeDtypeStruct((tps * chunks, 1, cw), F32),
        ],
        scratch_shapes=shapes,
        compiler_params=pltpu.CompilerParams(
            vmem_limit_bytes=63 << 20, collective_id=1, has_side_effects=True
        ),
        name="layer",
    )(*arrays)


def settle_kernel(experts, *refs):
    given, made, held, sem = refs[:8], refs[8:22], refs[22:30], refs[30]
    out_to, grad_to, up_to, down_to, wo_to, wq_to, pair_to, router_to, bias_to, *vectors = made
    loads = [pltpu.make_async_copy(given[k], held[k], sem.at[k]) for k in range(8)]
    for load in loads:
        load.start()
    copies = [pltpu.make_async_copy(held[k], made[k], sem.at[8 + k]) for k in range(2)]
    for load in loads[2:]:
        load.wait()
    for load, copy in zip(loads, copies):
        load.wait()
        copy.start()
    ud, wo, wq, kr, vec, bias = held[2:]
    chunks, _, rows, cw = ud.shape
    for c in range(chunks):
        up_to[:, c * cw : (c + 1) * cw] = ud[c, 0].astype(F32)
        down_to[c * cw : (c + 1) * cw, :] = ud[c, 1].astype(F32).T
        bias_to[:, c * cw : (c + 1) * cw] = bias[lax.axis_index("tp") * chunks + c]
    wo_to[...] = wo[0, 0].astype(F32).T
    wq_to[...] = wq[0, 0].astype(F32).T
    pair_to[...] = kr[0, 0, :, 0:128].astype(F32)
    router = kr[0, 0, :, 128:256].astype(F32).T
    router_to[...] = router[0:experts] + router[experts : 2 * experts]
    for k, to in enumerate(vectors):
        to[...] = vec[k : k + 1, :]
    for copy in copies:
        copy.wait()


def run_settle(tps, experts, results):
    out, grad, ud, wo, wq, kr, vec, bias = results
    chunks, _, rows, cw = ud.shape
    w, width = wo.shape[3], vec.shape[1]

    def f32(*shape):
        return jax.ShapeDtypeStruct(shape, F32)

    return pl.pallas_call(
        functools.partial(settle_kernel, experts),
        in_specs=[ANY] * 8,
        out_specs=[ANY, ANY] + [VMEM] * 12,
        out_shape=[
            jax.ShapeDtypeStruct(out.shape, BF16),
            jax.ShapeDtypeStruct(out.shape, BF16),
            f32(rows, chunks * cw),
            f32(chunks * cw, rows),
            f32(w, rows),
            f32(w, rows),
            f32(rows, 128),
            f32(experts, rows),
            f32(1, chunks * cw),
        ]
        + [f32(1, width)] * 5,
        scratch_shapes=[pltpu.VMEM(r.shape, r.dtype) for r in results] + [pltpu.SemaphoreType.DMA((10,))],
        compiler_params=pltpu.CompilerParams(vmem_limit_bytes=60 << 20),
        name="settle",
    )(*results)


def per_device(
    mesh_sizes,
    tokens,
    expert_routes,
    picture_start,
    picture_mode,
    norm1_gain,
    norm1_bias,
    router_weight,
    query_weight,
    output_weight,
    key_value_weight,
    norm2_gain,
    norm2_bias,
    up_weight,
    up_bias,
    down_weight,
    down_bias,
    upstream_tokens,
):
    local_experts, rows_d, head = query_weight.shape
    experts = local_experts * mesh_sizes[2]
    width = tokens.shape[2]
    heads = local_experts * head

    def lines(vector):
        return vector.reshape(-1, 128)

    results = run_layer(
        mesh_sizes,
        tokens.shape[0],
        tokens.shape,
        experts,
        (
            picture_start,
            picture_mode,
            tokens,
            jnp.transpose(expert_routes, (0, 2, 1)),
            upstream_tokens,
            key_value_weight,
            jnp.transpose(query_weight, (0, 2, 1)).reshape(heads, rows_d),
            output_weight.reshape(heads, rows_d),
            up_weight,
            down_weight,
            router_weight.T,
            lines(up_bias),
            lines(norm1_gain),
            lines(norm1_bias),
            lines(norm2_gain),
            lines(norm2_bias),
            lines(down_bias),
        ),
    )
    outs = run_settle(mesh_sizes[2], experts, results)
    result, input_grad, up_out, down_out, wo_out, wq_out, pair_out, router_out, bias_out, *vectors = outs
    gain1, bias1, gain2, bias2, down_bias_sum = (v.reshape(width) for v in vectors)
    return (
        result,
        input_grad,
        gain1,
        bias1,
        router_out.T,
        jnp.transpose(wq_out.reshape(local_experts, head, rows_d), (0, 2, 1)),
        wo_out.reshape(output_weight.shape),
        pair_out,
        gain2,
        bias2,
        up_out,
        bias_out.reshape(-1),
        down_out,
        down_bias_sum,
    )


def solution(mesh):
    rows = P("fsdp", "ctx", None)
    placed = (
        rows,
        rows,
        P("fsdp", None),
        P("fsdp", None),
        P(),
        P(),
        P("fsdp", None),
        P("tp", "fsdp", None),
        P("tp", None, "fsdp"),
        P("fsdp", None),
        P(),
        P(),
        P("fsdp", "tp"),
        P("tp"),
        P("tp", "fsdp"),
        P(),
        rows,
    )
    sizes = tuple(mesh.shape[axis] for axis in ("fsdp", "ctx", "tp"))
    return jax.shard_map(
        functools.partial(per_device, sizes),
        mesh=mesh,
        in_specs=placed,
        out_specs=(
            rows,
            rows,
            P(),
            P(),
            P("fsdp", None),
            P("tp", "fsdp", None),
            P("tp", None, "fsdp"),
            P("fsdp", None),
            P(),
            P(),
            P("fsdp", "tp"),
            P("tp"),
            P("tp", "fsdp"),
            P(),
        ),
        check_vma=False,
    )
```

```python
import functools
import types

import jax
import jax.numpy as jnp
from jax import lax
from jax.experimental import pallas as pl
from jax.experimental.pallas import tpu as pltpu
from jax.sharding import PartitionSpec as P

PIC = 256
TINY = 1e-05
NEG = -1e30
F32 = jnp.float32
BF16 = jnp.bfloat16
TQ = 256
TK = 256
BIG = 1024
NT = (((1,), (1,)), ((), ()))
TN = (((0,), (0,)), ((), ()))


def dot(a, b):
    return jnp.dot(a, b, preferred_element_type=F32)


def dot_nt(a, b):
    return lax.dot_general(a, b, NT, preferred_element_type=F32)


def dot_tn(a, b):
    return lax.dot_general(a, b, TN, preferred_element_type=F32)


def picture_starts(start_ref, mode_ref, sequence, pics):
    return [jnp.where(mode_ref[sequence, k] == 1, start_ref[sequence, k], -(1 << 20)) for k in range(pics)]


def mask_of(q0, k0, keys, queries, starts):
    key_pos = k0 + lax.broadcasted_iota(jnp.int32, (keys, 1), 0)
    query_pos = q0 + lax.broadcasted_iota(jnp.int32, (1, queries), 1)
    key_id = jnp.full((keys, 1), -2, jnp.int32)
    query_id = jnp.full((1, queries), -1, jnp.int32)
    for k, start in enumerate(starts):
        key_id = jnp.where((key_pos >= start) & (key_pos < start + PIC), k, key_id)
        query_id = jnp.where((query_pos >= start) & (query_pos < start + PIC), k, query_id)
    allowed = (key_pos <= query_pos) | (key_id == query_id)
    return jnp.concatenate([allowed, allowed], axis=1)


SMEM = pl.BlockSpec(memory_space=pltpu.SMEM)
VMEM = pl.BlockSpec(memory_space=pltpu.VMEM)
ANY = pl.BlockSpec(memory_space=pl.ANY)
MESH = pl.DeviceIdType.MESH


def remote(src, dst, send, recv, to):
    return pltpu.make_async_remote_copy(
        src_ref=src, dst_ref=dst, send_sem=send, recv_sem=recv, device_id=to, device_id_type=MESH
    )


class Place:
    def __init__(self, sizes, sequences):
        self.fsdp, self.ctx, self.tp = sizes
        self.subs = self.tp // sequences
        self.blocks = self.ctx * self.subs
        self.f, self.x, self.t = (lax.axis_index(a) for a in ("fsdp", "ctx", "tp"))
        self.seq, self.sub = self.t // self.subs, self.t % self.subs
        self.block = self.x * self.subs + self.sub

    def owner(self, block):
        return {"ctx": block // self.subs, "tp": self.seq * self.subs + block % self.subs}

    def barrier(self):
        semaphore = pltpu.get_barrier_semaphore()
        count = 0
        for axis, size, me in (("fsdp", self.fsdp, self.f), ("ctx", self.ctx, self.x), ("tp", self.tp, self.t)):
            for r in range(1, size):
                pl.semaphore_signal(
                    semaphore, inc=1, device_id={axis: lax.rem(me + r, size)}, device_id_type=MESH
                )
                count += 1
        if self.subs > 1:
            for r in range(1, self.blocks):
                pl.semaphore_signal(
                    semaphore,
                    inc=1,
                    device_id=self.owner(lax.rem(self.block + r, self.blocks)),
                    device_id_type=MESH,
                )
                count += 1
        pl.semaphore_wait(semaphore, count)


class Reduce:
    def __init__(self, k, w, n, d, sizes, tp=True):
        self.k, self.w, self.n, self.d, self.sizes, self.tp = k, w, n, d, sizes, tp
        fsdp, ctx, tps = sizes
        self.rows, self.part = d // fsdp, d // fsdp // ctx
        self.count = 16 if tp else 15

    def scratch(self):
        k, w, n, d = self.k, self.w, self.n, self.d
        fsdp, ctx, tps = self.sizes
        dma = pltpu.SemaphoreType.DMA
        shapes = [
            pltpu.VMEM((n, k, d, w), BF16),
            pltpu.VMEM((n, fsdp - 1, k, self.rows, w), BF16),
            pltpu.VMEM((n, k, self.rows, w), F32),
            pltpu.VMEM((n, k, self.rows, w), BF16),
            pltpu.VMEM((n, ctx - 1, k, self.part, w), BF16),
            pltpu.VMEM((n, k, self.rows, w), BF16),
            dma((n, fsdp - 1)),
            dma((n, fsdp - 1)),
            dma((n, ctx - 1)),
            dma((n, ctx - 1)),
            dma((n, ctx - 1)),
            dma((n, ctx - 1)),
        ]
        if self.tp:
            shapes += [
                pltpu.VMEM((tps - 1, n, k, d, w), BF16),
                pltpu.VMEM((tps - 1, n, k, d, w), BF16),
                dma((tps - 1, n)),
                dma((tps - 1, n)),
            ]
        else:
            shapes += [pltpu.VMEM((tps, k, self.rows, w), F32), dma((tps - 1,)), dma((tps - 1,))]
        return shapes

    def bind(self, place, refs):
        self.place = place
        self.s2, self.r2, self.own, self.s3, self.r3, self.fin = refs[:6]
        self.m2, self.m3, self.m4 = refs[6:8], refs[8:10], refs[10:12]
        if self.tp:
            self.s1, self.r1 = refs[12:14]
            self.m1 = refs[14:16]
        else:
            self.all, self.m1 = refs[12], refs[13:15]

    def d1(self, o, c):
        p = self.place
        to = {"tp": lax.rem(p.t + o, p.tp)}
        if self.tp:
            return remote(
                self.s1.at[o - 1, c], self.r1.at[o - 1, c], self.m1[0].at[o - 1, c], self.m1[1].at[o - 1, c], to
            )
        return remote(self.all.at[p.t], self.all.at[p.t], self.m1[0].at[o - 1], self.m1[1].at[o - 1], to)

    def d2(self, r, c):
        p = self.place
        to = lax.rem(p.f + r, p.fsdp)
        rows = pl.ds(pl.multiple_of(to * self.rows, self.rows), self.rows)
        return remote(
            self.s2.at[c, :, rows, :],
            self.r2.at[c, r - 1],
            self.m2[0].at[c, r - 1],
            self.m2[1].at[c, r - 1],
            {"fsdp": to},
        )

    def spot(self, x):
        return pl.ds(pl.multiple_of(x * self.part, self.part), self.part)

    def d3(self, q, c):
        p = self.place
        to = lax.rem(p.x + q, p.ctx)
        return remote(
            self.s3.at[c, :, self.spot(to), :],
            self.r3.at[c, q - 1],
            self.m3[0].at[c, q - 1],
            self.m3[1].at[c, q - 1],
            {"ctx": to},
        )

    def d4(self, q, c):
        p = self.place
        to = lax.rem(p.x + q, p.ctx)
        mine = self.fin.at[c, :, self.spot(p.x), :]
        return remote(mine, mine, self.m4[0].at[c, q - 1], self.m4[1].at[c, q - 1], {"ctx": to})

    def put(self, o, c, k, value):
        self.s1[o - 1, c, k] = value.astype(BF16)

    def give(self, o, c):
        self.d1(o, c).start()

    def take(self, c, acc):
        p, w = self.place, self.w
        if self.tp:
            for o in range(1, p.tp):
                self.d1(o, c).wait_recv()
            for k in range(self.k):
                total = acc[k, :, 0:w]
                for o in range(1, p.tp):
                    total = total + self.r1[o - 1, c, k].astype(F32)
                acc[k, :, 0:w] = total
        for k in range(self.k):
            self.s2[c, k] = acc[k, :, 0:w].astype(BF16)
        for r in range(1, p.fsdp):
            self.d2(r, c).start()
        for k in range(self.k):
            self.own[c, k] = acc[k, pl.ds(pl.multiple_of(p.f * self.rows, self.rows), self.rows), 0:w]

    def fold(self, c):
        p = self.place
        for r in range(1, p.fsdp):
            self.d2(r, c).wait_recv()
        for k in range(self.k):
            total = self.own[c, k]
            for r in range(1, p.fsdp):
                total = total + self.r2[c, r - 1, k].astype(F32)
            if self.tp:
                self.own[c, k] = total
                self.s3[c, k] = total.astype(BF16)
            else:
                self.all[p.t, k] = total
        if self.tp:
            for q in range(1, p.ctx):
                self.d3(q, c).start()
        else:
            for o in range(1, p.tp):
                self.d1(o, c).start()

    def share(self, c):
        p = self.place
        for o in range(1, p.tp):
            self.d1(o, c).wait_recv()
        for k in range(self.k):
            total = self.all[0, k]
            for o in range(1, p.tp):
                total = total + self.all[o, k]
            self.own[c, k] = total
            self.s3[c, k] = total.astype(BF16)
        for q in range(1, p.ctx):
            self.d3(q, c).start()

    def finish(self, c):
        p = self.place
        for q in range(1, p.ctx):
            self.d3(q, c).wait_recv()
        for k in range(self.k):
            total = self.own[c, k, self.spot(p.x), :]
            for q in range(1, p.ctx):
                total = total + self.r3[c, q - 1, k].astype(F32)
            self.fin[c, k, self.spot(p.x), :] = total.astype(BF16)
        for q in range(1, p.ctx):
            self.d4(q, c).start()

    def close(self):
        p = self.place

        @pl.loop(0, self.n)
        def _(c):
            for q in range(1, p.ctx):
                self.d4(q, c).wait()
                self.d3(q, c).wait_send()
            for r in range(1, p.fsdp):
                self.d2(r, c).wait_send()
            for o in range(1, p.tp):
                self.d1(o, c).wait_send()


class Everywhere:
    def __init__(self, shape, sizes):
        self.shape, self.sizes, self.count = shape, sizes, 9

    def scratch(self):
        dma = pltpu.SemaphoreType.DMA
        shapes = []
        for size in self.sizes:
            shapes += [pltpu.VMEM((size,) + self.shape, F32), dma((size - 1,)), dma((size - 1,))]
        return shapes

    def bind(self, place, refs):
        self.place, self.refs = place, refs

    def copy(self, stage, r):
        p = self.place
        axis, size, me = (
            ("fsdp", p.fsdp, p.f),
            ("ctx", p.ctx, p.x),
            ("tp", p.tp, p.t),
        )[stage]
        buf, send, recv = self.refs[3 * stage : 3 * stage + 3]
        return remote(
            buf.at[me], buf.at[me], send.at[r - 1], recv.at[r - 1], {axis: lax.rem(me + r, size)}
        )

    def start(self, stage, value):
        p = self.place
        me = (p.f, p.x, p.t)[stage]
        self.refs[3 * stage][me] = value
        for r in range(1, self.sizes[stage]):
            self.copy(stage, r).start()

    def total(self, stage):
        buf = self.refs[3 * stage]
        for r in range(1, self.sizes[stage]):
            self.copy(stage, r).wait()
        total = buf[0]
        for r in range(1, self.sizes[stage]):
            total = total + buf[r]
        return total


def norm_back(grad, normed, inverse, gain):
    scaled = grad * gain
    inner = (
        scaled
        - jnp.mean(scaled, axis=-1, keepdims=True)
        - normed * jnp.mean(scaled * normed, axis=-1, keepdims=True)
    )
    return inner * inverse


def half_lanes(rows):
    return lax.broadcasted_iota(jnp.int32, (rows, 128), 1)


def both_halves(values, upper):
    low = half_lanes(values.shape[0]) < 64
    turned = pltpu.roll(values, 64, 1)
    return jnp.where(low, turned, values) if upper else jnp.where(low, values, turned)


class Gather:
    def __init__(self, place, shard, spot, to_tp, refs):
        self.place, self.shard, self.spot, self.to_tp = place, shard, spot, to_tp
        self.fsend, self.frecv, self.tsend, self.trecv, self.local = refs

    def keep(self):
        p = self.place
        return pltpu.make_async_copy(self.shard, self.spot(p.t, p.f), self.local.at[0])

    def across(self, r):
        p = self.place
        return remote(
            self.shard,
            self.spot(p.t, p.f),
            self.fsend.at[r - 1],
            self.frecv.at[r - 1],
            {"fsdp": lax.rem(p.f + r, p.fsdp)},
        )

    def beside(self, o, r):
        p = self.place
        spot = self.spot(p.t, lax.rem(p.f - r + p.fsdp, p.fsdp))
        return remote(
            self.shard if r == 0 else spot,
            spot,
            self.tsend.at[o - 1, r],
            self.trecv.at[o - 1, r],
            {"tp": lax.rem(p.t + o, p.tp)},
        )

    def begin(self):
        p = self.place
        for r in range(1, p.fsdp):
            self.across(r).start()
        if self.to_tp:
            for o in range(1, p.tp):
                self.beside(o, 0).start()
        self.keep().start()

    def forward(self):
        p = self.place
        for r in range(1, p.fsdp):
            self.across(r).wait_recv()
            if self.to_tp:
                for o in range(1, p.tp):
                    self.beside(o, r).start()
        self.keep().wait()

    def arrive(self):
        p = self.place
        if self.to_tp:
            for o in range(1, p.tp):
                for r in range(p.fsdp):
                    self.beside(o, r).wait_recv()

    def close(self):
        p = self.place
        for r in range(1, p.fsdp):
            self.across(r).wait_send()
        if self.to_tp:
            for o in range(1, p.tp):
                for r in range(p.fsdp):
                    self.beside(o, r).wait_send()


INPUTS = ["pic_start", "pic_mode", "tokens", "routes", "upstream"]
INPUTS += ["kv_shard", "wq_shard", "wo_shard", "up_shard", "down_shard"]
INPUTS += ["router_in", "bias_in", "gain1_in", "bias1_in", "gain2_in", "bias2_in", "down_bias_in"]
OUTPUTS = ["out_hbm", "grad_hbm", "ud_out", "wo_out", "wq_out", "kr_out", "vec_out", "bias_out"]
FIRST = ["kv", "rt", "wq"]
FSDP_ONLY = ["kv", "rt"]


def layer_kernel(dims, names, *refs):
    sizes, sequences, tokens, width, experts, pics, length, reducers = dims
    fsdp, ctx, tps = sizes
    named = INPUTS + OUTPUTS + names
    a = types.SimpleNamespace(**dict(zip(named, refs[: len(named)])))
    rest = refs[len(named) :]
    r_ud, r_wo, r_wq, r_kr, r_vec, r_bias = reducers
    place = Place(sizes, sequences)
    for reducer in reducers:
        reducer.bind(place, rest[: reducer.count])
        rest = rest[reducer.count :]
    tiles = tokens // TQ
    cw, chunks = r_ud.w, r_ud.n
    rows_t = min(1024, tokens)
    big = min(BIG, tokens)
    shard_rows = width // fsdp

    def span(index, size):
        return pl.ds(pl.multiple_of(index * size, size), size)

    spots = dict(
        kv=lambda t, f: a.wkv.at[span(f, shard_rows), :],
        rt=lambda t, f: a.rpad.at[0:16, span(f, shard_rows)],
        wq=lambda t, f: a.wq.at[t, :, span(f, shard_rows)],
        wo=lambda t, f: a.wo.at[t, :, span(f, shard_rows)],
    )
    shards = dict(kv=a.kv_shard, rt=a.rt_shard, wq=a.wq_shard, wo=a.wo_shard)
    later = ["wo"]
    for c in range(chunks):
        cut = slice(c * cw, (c + 1) * cw)
        up, down = "up%d" % c, "down%d" % c
        later += [up, down]
        shards[up], shards[down] = a.up_shard.at[:, cut], a.down_shard.at[cut, :]
        spots[up] = lambda t, f, cut=cut: a.up.at[t, span(f, shard_rows), cut]
        spots[down] = lambda t, f, cut=cut: a.down.at[t, cut, span(f, shard_rows)]
    weights = {}
    for name in FIRST + later:
        weights[name] = Gather(place, shards[name], spots[name], name not in FSDP_ONLY, rest[:5])
        rest = rest[5:]

    own_slice = (place.seq, pl.ds(pl.multiple_of(place.sub * tokens, tokens), tokens))
    loads = [
        pltpu.make_async_copy(source.at[own_slice[0], own_slice[1], :], target, a.load_sem.at[k])
        for k, (source, target) in enumerate(
            ((a.tokens, a.tok), (a.upstream, a.ups))
        )
    ]
    loads.append(
        pltpu.make_async_copy(
            a.routes.at[place.seq, :, pl.ds(pl.multiple_of(place.sub * tokens, tokens), tokens)], a.rt, a.load_sem.at[2]
        )
    )
    for load in loads:
        load.start()

    router = a.router_in[...].astype(F32)
    a.rt_shard[...] = jnp.concatenate([router, router], axis=0).astype(BF16)
    a.rpad[16:, :] = jnp.zeros((112, width), BF16)
    a.bias_shard[...] = a.bias_in[...].astype(F32)
    a.bias_raw[place.t] = a.bias_shard[...]
    place.barrier()
    for name in FIRST:
        weights[name].begin()

    def bias_copy(o):
        spot = a.bias_raw.at[place.t]
        return remote(
            a.bias_shard, spot, a.bias_sem.at[0, o - 1], a.bias_sem.at[1, o - 1], {"tp": lax.rem(place.t + o, tps)}
        )

    for o in range(1, tps):
        bias_copy(o).start()

    def row(ref):
        values = ref[...].astype(F32)
        return jnp.concatenate([values[k : k + 1, :] for k in range(values.shape[0])], axis=1)

    gain1, bias1 = row(a.gain1_in), row(a.bias1_in)
    q_base = place.block * tokens
    starts = picture_starts(a.pic_start, a.pic_mode, place.seq, pics)
    lanes = half_lanes(TQ)
    own_rows = pl.ds(pl.multiple_of(q_base, tokens), tokens)

    def tile_rows(i):
        return span(i, TQ)

    def gates(rows):
        return [a.meta[rows, k : k + 1] for k in range(4)]

    def expert_of(c):
        return 2 * c + jnp.where(lanes >= 64, 1, 0)

    def normalise(x):
        center = x - jnp.mean(x, axis=-1, keepdims=True)
        inverse = lax.rsqrt(jnp.mean(center * center, axis=-1, keepdims=True) + TINY)
        return center * inverse, inverse

    def choose(full, r):
        expert = r.astype(jnp.int32)
        chosen = jnp.zeros((TQ, 128), F32)
        for c in range(experts // 2):
            chosen = jnp.where(expert == expert_of(c), full[:, c * 128 : (c + 1) * 128], chosen)
        return chosen + pltpu.roll(chosen, 64, 1)

    loads[0].wait()
    loads[2].wait()

    @pl.loop(0, tiles)
    def _(i):
        rows = tile_rows(i)
        normed, _ = normalise(a.tok[rows, :].astype(F32))
        a.hid1[rows, :] = (normed * gain1 + bias1).astype(BF16)

    a.kv[pl.ds(length, TQ), :] = jnp.zeros((TQ, 128), BF16)
    weights["kv"].forward()

    @pl.loop(0, tiles)
    def _(i):
        rows = tile_rows(i)
        pair = dot(a.hid1[rows, :], a.wkv[...])
        a.kv[pl.ds(pl.multiple_of(q_base + i * TQ, TQ), TQ), :] = pair.astype(BF16)

    after_me, before_me = place.block + 1 < place.blocks, place.block > 0

    def pass_on(d):
        keys = pl.ds(pl.multiple_of((place.block - d) * tokens, tokens), tokens)
        to = place.owner(lax.rem(place.block + 1, place.blocks))
        return remote(a.kv.at[keys, :], a.kv.at[keys, :], a.kv_sem.at[0, d], a.kv_sem.at[1, d], to)

    def reach_back():
        keys = pl.ds(pl.multiple_of(q_base, TQ), TQ)
        to = place.owner(lax.rem(place.block + place.blocks - 1, place.blocks))
        return remote(a.kv.at[keys, :], a.kv.at[keys, :], a.near_sem.at[2], a.near_sem.at[3], to)

    @pl.when(after_me)
    def _():
        pass_on(0).start()

    @pl.when(before_me)
    def _():
        reach_back().start()

    weights["rt"].forward()

    @pl.loop(0, tiles)
    def _(i):
        rows = tile_rows(i)
        logits = dot_nt(a.hid1[rows, :], a.rpad[...])
        pairs = jnp.concatenate([a.rt[:, rows].astype(F32)] * 4, axis=0).T
        r0, r1 = pairs[:, 0:1].astype(jnp.int32), pairs[:, 1:2].astype(jnp.int32)
        l0 = jnp.sum(jnp.where(lanes == r0, logits, 0.0), axis=-1, keepdims=True)
        l1 = jnp.sum(jnp.where(lanes == r1, logits, 0.0), axis=-1, keepdims=True)
        top = jnp.maximum(l0, l1)
        e0, e1 = jnp.exp(l0 - top), jnp.exp(l1 - top)
        a.meta[rows, 0:1] = e0 / (e0 + e1)
        a.meta[rows, 1:2] = e1 / (e0 + e1)
        a.meta[rows, 2:3] = r0.astype(F32)
        a.meta[rows, 3:4] = r1.astype(F32)

    weights["wq"].forward()
    for name in later:
        weights[name].begin()
    weights["wq"].arrive()

    @pl.loop(0, tiles)
    def _(i):
        rows = tile_rows(i)
        _, _, r0, r1 = gates(rows)
        full = dot_nt(a.hid1[rows, :], a.wq[...].reshape(width, width))
        for s, r in enumerate((r0, r1)):
            a.q[s, rows, :] = jnp.where(lanes < 64, choose(full, r) * 0.125, 0.0).astype(BF16)

    @pl.loop(0, tiles)
    def _(i):
        a.top[i] = jnp.full((1, 2 * TQ), NEG, F32)
        a.total[i] = jnp.zeros((1, 2 * TQ), F32)
    a.dqt[...] = jnp.zeros_like(a.dqt)

    def look(i, k0, size, masked):
        rows = tile_rows(i)
        keys = pl.ds(pl.multiple_of(k0, TK), size)
        q = jnp.concatenate([a.q[0, rows, :], a.q[1, rows, :]], axis=0)
        pair = a.kv[keys, :]
        scores = dot_nt(pair, q)
        if masked:
            scores = jnp.where(mask_of(q_base + i * TQ, k0, size, TQ, starts), scores, NEG)
        before = a.top[i]
        now = jnp.maximum(before, jnp.max(scores, axis=0, keepdims=True))
        probs = jnp.exp(scores - now)
        scale = jnp.exp(before - now)
        a.top[i] = now
        a.total[i] = a.total[i] * scale + jnp.sum(probs, axis=0, keepdims=True)
        a.dqt[i] = a.dqt[i] * scale + dot_tn(pair, probs.astype(BF16))

    @pl.when(after_me)
    def _():
        reach_back().wait_recv()

    @pl.loop(0, tiles)
    def _(i):
        look(i, q_base + i * TK, 2 * TK, True)

    for i in range(1, tiles):
        look(i, q_base, i * TK, False)

    @pl.loop(0, place.blocks - 1)
    def _(j):
        @pl.when(j < place.block)
        def _():
            pass_on(j).wait_recv()

            @pl.when(after_me)
            def _():
                pass_on(j + 1).start()

            @pl.loop(0, tokens // big)
            def _(k):
                @pl.loop(0, tiles)
                def _(i):
                    look(i, (place.block - 1 - j) * tokens + k * big, big, False)

        @pl.when(j == place.blocks - 2)
        def _():
            weights["wo"].forward()

    weights["up0"].forward()
    weights["down0"].forward()

    @pl.loop(0, tiles)
    def _(i):
        rows = tile_rows(i)
        both = (a.dqt[i] / a.total[i]).T
        a.att[0, rows, :] = both[:TQ]
        a.att[1, rows, :] = both[TQ:]
        a.logt[i] = a.top[i] + jnp.log(a.total[i])

    gain2, bias2, down_bias = row(a.gain2_in), row(a.bias2_in), row(a.down_bias_in)
    a.vec[...] = jnp.zeros_like(a.vec)
    a.bias_acc[...] = jnp.zeros_like(a.bias_acc)
    a.woacc[...] = jnp.zeros_like(a.woacc)
    weights["wo"].arrive()

    @pl.loop(0, tiles)
    def _(i):
        rows = tile_rows(i)
        g0, g1, r0, r1 = gates(rows)
        after = a.tok[rows, :].astype(F32)
        out_w = a.wo[...].reshape(width, width)
        for s, (g, r) in enumerate(((g0, r0), (g1, r1))):
            twice = both_halves(a.att[s, rows, :], True)
            expert = r.astype(jnp.int32)
            for c in range(experts // 2):
                a.wide[s, rows, c * 128 : (c + 1) * 128] = jnp.where(expert == expert_of(c), twice, 0.0).astype(BF16)
            projected = dot(a.wide[s, rows, :], out_w)
            a.proj[s, rows, :] = projected
            after = after + g * projected
        normed, inverse = normalise(after)
        a.normed2[rows, :] = normed
        a.inv2[rows, :] = inverse
        a.hid2[rows, :] = (normed * gain2 + bias2).astype(BF16)
        a.out_acc[rows, :] = after + down_bias
        a.mid[rows, :] = jnp.zeros_like(after)

    loads[1].wait()
    for o in range(1, tps):
        bias_copy(o).wait_recv()
    lines = cw // 128
    for t in range(tps):
        for c in range(chunks):
            a.up_bias[t * chunks + c] = jnp.concatenate(
                [a.bias_raw[t, c * lines + k : c * lines + k + 1, :] for k in range(lines)], axis=1
            )

    def feed(t, c):
        cols = span(c, cw)
        whole = tokens == rows_t
        if not whole:
            a.gacc[...] = jnp.zeros_like(a.gacc)

        @pl.loop(0, tokens // rows_t)
        def _(i):
            rows = span(i, rows_t)
            h2, u = a.hid2[rows, :], a.ups[rows, :]
            pre = dot(h2, a.up[t, :, cols]) + a.up_bias[t * chunks + c]
            sig = 1.0 / (1.0 + jnp.exp(-pre))
            active = (pre * sig).astype(BF16)
            a.out_acc[rows, :] += dot(active, a.down[t, cols, :])
            down_part = dot_tn(u, active)
            a.gacc[1, :, 0:cw] = down_part if whole else a.gacc[1, :, 0:cw] + down_part
            slope = sig * (1.0 + pre * (1.0 - sig))
            grad = dot_nt(u, a.down[t, cols, :]) * slope
            low = grad.astype(BF16)
            a.bias_acc[t * chunks + c] += jnp.sum(low.astype(F32), axis=0, keepdims=True)
            up_part = dot_tn(h2, low)
            a.gacc[0, :, 0:cw] = up_part if whole else a.gacc[0, :, 0:cw] + up_part
            a.mid[rows, :] += dot_nt(low, a.up[t, :, cols])

    @pl.loop(0, chunks)
    def _(c):
        for k in range(chunks):

            @pl.when(c == k)
            def _():
                weights["up%d" % k].arrive()
                weights["down%d" % k].arrive()

        for o in range(1, tps):
            feed(lax.rem(place.t + o, tps), c)
            for k in range(2):
                r_ud.put(o, c, k, a.gacc[k, :, 0:cw])
            r_ud.give(o, c)
        for k in range(1, chunks):

            @pl.when(c + 1 == k)
            def _():
                weights["up%d" % k].forward()
                weights["down%d" % k].forward()

        feed(place.t, c)
        r_ud.take(c, a.gacc)

    r_bias.start(2, a.bias_acc[...])

    def share_out(low, hbm, slot):
        spot = hbm.at[own_slice[0], own_slice[1], :]
        copies = [
            remote(
                low, spot, a.out_sem.at[0, slot, o - 1], a.out_sem.at[1, slot, o - 1], {"tp": lax.rem(place.t + o, tps)}
            )
            for o in range(1, tps)
        ]
        copies.append(pltpu.make_async_copy(low, spot, a.loc_sem.at[slot]))
        for copy in copies:
            copy.start()
        return copies

    def add_row(k, value):
        a.vec[k : k + 1, :] += jnp.sum(value, axis=0, keepdims=True)

    @pl.loop(0, tiles)
    def _(i):
        rows = tile_rows(i)
        g0, g1, r0, r1 = gates(rows)
        out_w = a.wo[...].reshape(width, width)
        a.res_low[rows, :] = a.out_acc[rows, :].astype(BF16)
        upstream = a.ups[rows, :].astype(F32)
        grad, normed = a.mid[rows, :], a.normed2[rows, :]
        resid = upstream + norm_back(grad, normed, a.inv2[rows, :], gain2)
        a.mid[rows, :] = resid
        add_row(2, grad * normed)
        add_row(3, grad)
        add_row(4, upstream)
        d0 = jnp.sum(a.proj[0, rows, :] * resid, axis=-1, keepdims=True)
        d1 = jnp.sum(a.proj[1, rows, :] * resid, axis=-1, keepdims=True)
        mean = g0 * d0 + g1 * d1
        for s, (g, r) in enumerate(((g0, r0), (g1, r1))):
            low = (g * resid).astype(BF16)
            a.woacc[0] += dot_tn(low, a.wide[s, rows, :])
            chosen = jnp.where(lanes >= 64, choose(dot_nt(low, out_w), r), 0.0).astype(BF16)
            a.da[s, rows, :] = chosen
            product = chosen.astype(F32) * jnp.where(lanes >= 64, a.att[s, rows, :], 0.0)
            a.delta[i, :, s * TQ : (s + 1) * TQ] = jnp.sum(product.T, axis=0, keepdims=True)
        lane_expert = lax.rem(lanes, experts)
        lg = jnp.where(lane_expert == r0.astype(jnp.int32), g0 * (d0 - mean), 0.0)
        lg = lg + jnp.where(lane_expert == r1.astype(jnp.int32), g1 * (d1 - mean), 0.0)
        high = lg.astype(BF16).astype(F32)
        a.lgp[rows, :] = jnp.where(
            lanes < experts, high, jnp.where(lanes < 2 * experts, lg - high, 0.0)
        ).astype(BF16)

    out_copies = share_out(a.res_low, a.out_hbm, 0)

    def hand_out(reducer, acc):
        w = reducer.w
        for t in range(tps):

            @pl.when(t != place.t)
            def _():
                o = lax.rem(t - place.t + tps, tps)
                reducer.s1[o - 1, 0, 0] = acc[0, :, t * w : (t + 1) * w].astype(BF16)
                reducer.give(o, 0)

    def take_own(reducer, acc):
        w = reducer.w
        for t in range(tps):

            @pl.when(t == place.t)
            def _():
                a.gacc[0, :, 0:w] = acc[0, :, t * w : (t + 1) * w]

        reducer.take(0, a.gacc)

    hand_out(r_wo, a.woacc)
    r_bias.start(0, r_bias.total(2))

    a.dqt[...] = jnp.zeros_like(a.dqt)
    a.dkv[...] = jnp.zeros_like(a.dkv)

    def attend(i, k0, size, masked):
        rows = tile_rows(i)
        keys = pl.ds(pl.multiple_of(k0, TK), size)
        q = jnp.concatenate([a.q[0, rows, :], a.q[1, rows, :]], axis=0)
        d_att = jnp.concatenate([a.da[0, rows, :], a.da[1, rows, :]], axis=0)
        pair = a.kv[keys, :]
        scores = dot_nt(pair, q)
        if masked:
            scores = jnp.where(mask_of(q_base + i * TQ, k0, size, TQ, starts), scores, NEG)
        probs = jnp.exp(scores - a.logt[i])
        prob_grad = dot_nt(pair, d_att)
        score_grad = (probs * (prob_grad - a.delta[i])).astype(BF16)
        a.dkv[keys, :] += dot(score_grad, q) + dot(probs.astype(BF16), d_att)
        a.dqt[i] += dot_tn(pair, score_grad)

    def dkv_copy(block):
        return remote(
            a.dkv_send.at[block],
            a.dkv_recv.at[block],
            a.dkv_sem.at[0, block],
            a.dkv_sem.at[1, block],
            place.owner(lax.rem(place.block + place.blocks - 1, place.blocks)),
        )

    def hand_down(block):
        keys = span(block, tokens)

        @pl.when(after_me)
        def _():
            dkv_copy(block).wait_recv()
            a.dkv[keys, :] += a.dkv_recv[block].astype(F32)

        a.dkv_send[block] = a.dkv[keys, :].astype(BF16)
        dkv_copy(block).start()

    r_ud.fold(0)

    @pl.loop(0, place.blocks - 1)
    def _(j):
        @pl.when(j < place.block)
        def _():
            @pl.loop(0, tokens // big)
            def _(k):
                @pl.loop(0, tiles)
                def _(i):
                    attend(i, j * tokens + k * big, big, False)

            ready = j - jnp.where(after_me, 1, 0)

            @pl.when(ready >= 0)
            def _():
                hand_down(ready)

        @pl.when(j == place.blocks - 2)
        def _():
            r_ud.finish(0)

    take_own(r_wo, a.woacc)
    r_bias.start(1, r_bias.total(0))

    @pl.loop(0, tiles)
    def _(i):
        attend(i, q_base + i * TK, 2 * TK, True)

    for i in range(1, tiles):
        attend(i, q_base, i * TK, False)

    @pl.when(after_me & before_me)
    def _():
        hand_down(place.block - 1)

    r_ud.fold(chunks - 1)
    r_wo.fold(0)

    def near_copy():
        return remote(
            a.near_send,
            a.near_buf,
            a.near_sem.at[0],
            a.near_sem.at[1],
            place.owner(lax.rem(place.block + 1, place.blocks)),
        )

    @pl.when(after_me)
    def _():
        a.near_send[...] = a.dkv[pl.ds(pl.multiple_of((place.block + 1) * tokens, TQ), TQ), :].astype(BF16)
        near_copy().start()

    @pl.loop(0, tiles)
    def _(i):
        rows = tile_rows(i)
        _, _, r0, r1 = gates(rows)
        dq = (a.dqt[i] * 0.125).T
        first, second = both_halves(dq[:TQ], False), both_halves(dq[TQ:], False)
        for c in range(experts // 2):
            column = jnp.where(r0.astype(jnp.int32) == expert_of(c), first, 0.0)
            column = jnp.where(r1.astype(jnp.int32) == expert_of(c), second, column)
            a.dqw[rows, c * 128 : (c + 1) * 128] = column.astype(BF16)

    a.woacc[0] = dot_tn(a.hid1[...], a.dqw[...])
    hand_out(r_wq, a.woacc)

    take_own(r_wq, a.woacc)

    @pl.when(after_me)
    def _():
        dkv_copy(place.block).wait_recv()
        a.dkv[own_rows, :] += a.dkv_recv[place.block].astype(F32)

    @pl.when(before_me)
    def _():
        near_copy().wait_recv()
        a.dkv[pl.ds(pl.multiple_of(q_base, TQ), TQ), :] += a.near_buf[...].astype(F32)

    a.pairg[:, 0:128] = a.dkv[own_rows, :].astype(BF16)
    a.pairg[:, 128:256] = a.lgp[...]
    a.gacc[0, :, 0:256] = dot_tn(a.hid1[...], a.pairg[...])
    r_kr.take(0, a.gacc)

    r_wq.fold(0)

    @pl.loop(0, tiles)
    def _(i):
        rows = tile_rows(i)
        normed, inverse = normalise(a.tok[rows, :].astype(F32))
        grad = dot(a.dqw[rows, :], a.wq[...].reshape(width, width))
        grad = grad + dot_nt(a.pairg[rows, 0:128], a.wkv[...]) + dot(a.lgp[rows, :], a.rpad[...])
        add_row(0, grad * normed)
        add_row(1, grad)
        a.grad_low[rows, :] = (a.mid[rows, :] + norm_back(grad, normed, inverse, gain1)).astype(BF16)

    grad_copies = share_out(a.grad_low, a.grad_hbm, 1)
    r_vec.start(2, a.vec[...])
    r_ud.finish(chunks - 1)
    r_wo.finish(0)
    r_kr.fold(0)
    r_vec.start(0, r_vec.total(2))
    r_kr.share(0)
    r_vec.start(1, r_vec.total(0))
    r_wq.finish(0)
    r_kr.finish(0)
    a.vec_out[...] = r_vec.total(1)
    a.bias_out[...] = r_bias.total(1)
    for reducer, out in ((r_ud, a.ud_out), (r_wo, a.wo_out), (r_wq, a.wq_out), (r_kr, a.kr_out)):
        reducer.close()
        out[...] = reducer.fin[...]

    @pl.loop(0, place.block)
    def _(j):
        dkv_copy(j).wait_send()

    @pl.when(after_me)
    def _():
        near_copy().wait_send()

        @pl.loop(0, place.block + 1)
        def _(d):
            pass_on(d).wait_send()

    @pl.when(before_me)
    def _():
        reach_back().wait_send()

    for name in FIRST + later:
        weights[name].close()
    for o in range(1, tps):
        bias_copy(o).wait_send()
    for copy in out_copies + grad_copies:
        copy.wait()


def run_layer(sizes, sequences, shape, experts, arrays):
    fsdp, ctx, tps = sizes
    subs = tps // sequences
    width = shape[2]
    tokens = shape[1] // subs
    length = shape[1] * ctx
    blocks = ctx * subs
    tiles = tokens // TQ
    local_hidden = arrays[8].shape[1]
    cw = min(512, local_hidden)
    chunks = local_hidden // cw
    w = width // tps
    reducers = (
        Reduce(2, cw, chunks, width, sizes),
        Reduce(1, w, 1, width, sizes),
        Reduce(1, w, 1, width, sizes),
        Reduce(1, 256, 1, width, sizes, tp=False),
        Everywhere((8, width), sizes),
        Everywhere((tps * chunks, 1, cw), sizes),
    )
    dims = (sizes, sequences, tokens, width, experts, arrays[0].shape[1], length, reducers)
    rows = width // fsdp
    dma = pltpu.SemaphoreType.DMA
    vmem = pltpu.VMEM
    scratch = dict(
        tok=vmem((tokens, width), BF16),
        rt=vmem((2, tokens), jnp.int32),
        ups=vmem((tokens, width), BF16),
        load_sem=dma((3,)),
        wkv=vmem((width, 128), BF16),
        rt_shard=vmem((16, rows), BF16),
        rpad=vmem((128, width), BF16),
        wq=vmem((tps, w, width), BF16),
        wo=vmem((tps, w, width), BF16),
        up=vmem((tps, width, local_hidden), BF16),
        down=vmem((tps, local_hidden, width), BF16),
        bias_shard=vmem((local_hidden // 128, 128), F32),
        bias_raw=vmem((tps, local_hidden // 128, 128), F32),
        up_bias=vmem((tps * chunks, 1, cw), F32),
        bias_sem=dma((2, tps - 1)),
        meta=vmem((tokens, 8), F32),
        hid1=vmem((tokens, width), BF16),
        q=vmem((2, tokens, 128), BF16),
        kv=vmem((length + TQ, 128), BF16),
        kv_sem=dma((2, blocks)),
        near_sem=dma((4,)),
        top=vmem((tiles, 1, 2 * TQ), F32),
        total=vmem((tiles, 1, 2 * TQ), F32),
        att=vmem((2, tokens, 128), F32),
        logt=vmem((tiles, 1, 2 * TQ), F32),
        wide=vmem((2, tokens, width), BF16),
        proj=vmem((2, tokens, width), F32),
        normed2=vmem((tokens, width), F32),
        hid2=vmem((tokens, width), BF16),
        out_acc=vmem((tokens, width), F32),
        mid=vmem((tokens, width), F32),
        inv2=vmem((tokens, 1), F32),
        gacc=vmem((2, width, max(cw, 256)), F32),
        woacc=vmem((1, width, width), F32),
        da=vmem((2, tokens, 128), BF16),
        delta=vmem((tiles, 1, 2 * TQ), F32),
        lgp=vmem((tokens, 128), BF16),
        dqt=vmem((tiles, 128, 2 * TQ), F32),
        dkv=vmem((length + TQ, 128), F32),
        dkv_send=vmem((blocks - 1, tokens, 128), BF16),
        dkv_recv=vmem((blocks - 1, tokens, 128), BF16),
        dkv_sem=dma((2, blocks - 1)),
        dqw=vmem((tokens, width), BF16),
        pairg=vmem((tokens, 256), BF16),
        vec=vmem((8, width), F32),
        bias_acc=vmem((tps * chunks, 1, cw), F32),
        res_low=vmem((tokens, width), BF16),
        grad_low=vmem((tokens, width), BF16),
        near_buf=vmem((TQ, 128), BF16),
        near_send=vmem((TQ, 128), BF16),
        loc_sem=dma((2,)),
        out_sem=dma((2, 2, tps - 1)),
    )
    shapes = list(scratch.values())
    for reducer in reducers:
        shapes += reducer.scratch()
    for _ in range(len(FIRST) + 1 + 2 * chunks):
        shapes += [dma((fsdp - 1,)), dma((fsdp - 1,)), dma((tps - 1, fsdp)), dma((tps - 1, fsdp)), dma((1,))]
    return pl.pallas_call(
        functools.partial(layer_kernel, dims, list(scratch)),
        in_specs=[SMEM, SMEM] + [ANY] * 8 + [VMEM] * 7,
        out_specs=[ANY, ANY] + [VMEM] * 6,
        out_shape=[
            jax.ShapeDtypeStruct(shape, BF16),
            jax.ShapeDtypeStruct(shape, BF16),
            jax.ShapeDtypeStruct((chunks, 2, rows, cw), BF16),
            jax.ShapeDtypeStruct((1, 1, rows, w), BF16),
            jax.ShapeDtypeStruct((1, 1, rows, w), BF16),
            jax.ShapeDtypeStruct((1, 1, rows, 256), BF16),
            jax.ShapeDtypeStruct((8, width), F32),
            jax.ShapeDtypeStruct((tps * chunks, 1, cw), F32),
        ],
        scratch_shapes=shapes,
        compiler_params=pltpu.CompilerParams(
            vmem_limit_bytes=63 << 20, collective_id=1, has_side_effects=True
        ),
        name="layer",
    )(*arrays)


def settle_kernel(experts, *refs):
    given, made, held, sem = refs[:8], refs[8:22], refs[22:30], refs[30]
    out_to, grad_to, up_to, down_to, wo_to, wq_to, pair_to, router_to, bias_to, *vectors = made
    small = [pltpu.make_async_copy(given[k], held[k], sem.at[k]) for k in range(2, 8)]
    rows = given[0].shape[1] // 4
    pieces = [(k, i, j) for i in range(given[0].shape[0]) for j in range(4) for k in range(2)]
    loads, copies = [], []
    for n, (k, i, j) in enumerate(pieces):
        spot = (i, slice(j * rows, (j + 1) * rows), slice(None))
        loads.append(pltpu.make_async_copy(given[k].at[spot], held[k].at[spot], sem.at[8 + n]))
        copies.append(pltpu.make_async_copy(held[k].at[spot], made[k].at[spot], sem.at[8 + len(pieces) + n]))
    for load in loads + small:
        load.start()
    for load, copy in zip(loads, copies):
        load.wait()
        copy.start()
    for load in small:
        load.wait()
    ud, wo, wq, kr, vec, bias = held[2:]
    chunks, _, rows, cw = ud.shape
    for c in range(chunks):
        up_to[:, c * cw : (c + 1) * cw] = ud[c, 0].astype(F32)
        down_to[c * cw : (c + 1) * cw, :] = ud[c, 1].astype(F32).T
        bias_to[:, c * cw : (c + 1) * cw] = bias[lax.axis_index("tp") * chunks + c]
    wo_to[...] = wo[0, 0].astype(F32).T
    wq_to[...] = wq[0, 0].astype(F32).T
    pair_to[...] = kr[0, 0, :, 0:128].astype(F32)
    router = kr[0, 0, :, 128:256].astype(F32).T
    router_to[...] = router[0:experts] + router[experts : 2 * experts]
    for k, to in enumerate(vectors):
        to[...] = vec[k : k + 1, :]
    for copy in copies:
        copy.wait()


def run_settle(tps, experts, results):
    out, grad, ud, wo, wq, kr, vec, bias = results
    chunks, _, rows, cw = ud.shape
    w, width = wo.shape[3], vec.shape[1]

    def f32(*shape):
        return jax.ShapeDtypeStruct(shape, F32)

    return pl.pallas_call(
        functools.partial(settle_kernel, experts),
        in_specs=[ANY] * 8,
        out_specs=[ANY, ANY] + [VMEM] * 12,
        out_shape=[
            jax.ShapeDtypeStruct(out.shape, BF16),
            jax.ShapeDtypeStruct(out.shape, BF16),
            f32(rows, chunks * cw),
            f32(chunks * cw, rows),
            f32(w, rows),
            f32(w, rows),
            f32(rows, 128),
            f32(experts, rows),
            f32(1, chunks * cw),
        ]
        + [f32(1, width)] * 5,
        scratch_shapes=[pltpu.VMEM(r.shape, r.dtype) for r in results] + [pltpu.SemaphoreType.DMA((8 + 16 * results[0].shape[0],))],
        compiler_params=pltpu.CompilerParams(vmem_limit_bytes=60 << 20),
        name="settle",
    )(*results)


def per_device(
    mesh_sizes,
    tokens,
    expert_routes,
    picture_start,
    picture_mode,
    norm1_gain,
    norm1_bias,
    router_weight,
    query_weight,
    output_weight,
    key_value_weight,
    norm2_gain,
    norm2_bias,
    up_weight,
    up_bias,
    down_weight,
    down_bias,
    upstream_tokens,
):
    local_experts, rows_d, head = query_weight.shape
    experts = local_experts * mesh_sizes[2]
    width = tokens.shape[2]
    heads = local_experts * head

    def lines(vector):
        return vector.reshape(-1, 128)

    results = run_layer(
        mesh_sizes,
        tokens.shape[0],
        tokens.shape,
        experts,
        (
            picture_start,
            picture_mode,
            tokens,
            jnp.transpose(expert_routes, (0, 2, 1)),
            upstream_tokens,
            key_value_weight,
            jnp.transpose(query_weight, (0, 2, 1)).reshape(heads, rows_d),
            output_weight.reshape(heads, rows_d),
            up_weight,
            down_weight,
            router_weight.T,
            lines(up_bias),
            lines(norm1_gain),
            lines(norm1_bias),
            lines(norm2_gain),
            lines(norm2_bias),
            lines(down_bias),
        ),
    )
    outs = run_settle(mesh_sizes[2], experts, results)
    result, input_grad, up_out, down_out, wo_out, wq_out, pair_out, router_out, bias_out, *vectors = outs
    gain1, bias1, gain2, bias2, down_bias_sum = (v.reshape(width) for v in vectors)
    return (
        result,
        input_grad,
        gain1,
        bias1,
        router_out.T,
        jnp.transpose(wq_out.reshape(local_experts, head, rows_d), (0, 2, 1)),
        wo_out.reshape(output_weight.shape),
        pair_out,
        gain2,
        bias2,
        up_out,
        bias_out.reshape(-1),
        down_out,
        down_bias_sum,
    )


def solution(mesh):
    rows = P("fsdp", "ctx", None)
    placed = (
        rows,
        rows,
        P("fsdp", None),
        P("fsdp", None),
        P(),
        P(),
        P("fsdp", None),
        P("tp", "fsdp", None),
        P("tp", None, "fsdp"),
        P("fsdp", None),
        P(),
        P(),
        P("fsdp", "tp"),
        P("tp"),
        P("tp", "fsdp"),
        P(),
        rows,
    )
    sizes = tuple(mesh.shape[axis] for axis in ("fsdp", "ctx", "tp"))
    return jax.shard_map(
        functools.partial(per_device, sizes),
        mesh=mesh,
        in_specs=placed,
        out_specs=(
            rows,
            rows,
            P(),
            P(),
            P("fsdp", None),
            P("tp", "fsdp", None),
            P("tp", None, "fsdp"),
            P("fsdp", None),
            P(),
            P(),
            P("fsdp", "tp"),
            P("tp"),
            P("tp", "fsdp"),
            P(),
        ),
        check_vma=False,
    )
```

```python
import functools
import types

import jax
import jax.numpy as jnp
from jax import lax
from jax.experimental import pallas as pl
from jax.experimental.pallas import tpu as pltpu
from jax.sharding import PartitionSpec as P

PIC = 256
TINY = 1e-05
NEG = -1e30
F32 = jnp.float32
BF16 = jnp.bfloat16
TQ = 256
TK = 256
BIG = 1024
NT = (((1,), (1,)), ((), ()))
TN = (((0,), (0,)), ((), ()))


def dot(a, b):
    return jnp.dot(a, b, preferred_element_type=F32)


def dot_nt(a, b):
    return lax.dot_general(a, b, NT, preferred_element_type=F32)


def dot_tn(a, b):
    return lax.dot_general(a, b, TN, preferred_element_type=F32)


def picture_starts(start_ref, mode_ref, sequence, pics):
    return [jnp.where(mode_ref[sequence, k] == 1, start_ref[sequence, k], -(1 << 20)) for k in range(pics)]


def mask_of(q0, k0, keys, queries, starts):
    key_pos = k0 + lax.broadcasted_iota(jnp.int32, (keys, 1), 0)
    query_pos = q0 + lax.broadcasted_iota(jnp.int32, (1, queries), 1)
    key_id = jnp.full((keys, 1), -2, jnp.int32)
    query_id = jnp.full((1, queries), -1, jnp.int32)
    for k, start in enumerate(starts):
        key_id = jnp.where((key_pos >= start) & (key_pos < start + PIC), k, key_id)
        query_id = jnp.where((query_pos >= start) & (query_pos < start + PIC), k, query_id)
    allowed = (key_pos <= query_pos) | (key_id == query_id)
    return jnp.concatenate([allowed, allowed], axis=1)


SMEM = pl.BlockSpec(memory_space=pltpu.SMEM)
VMEM = pl.BlockSpec(memory_space=pltpu.VMEM)
ANY = pl.BlockSpec(memory_space=pl.ANY)
MESH = pl.DeviceIdType.MESH


def remote(src, dst, send, recv, to):
    return pltpu.make_async_remote_copy(
        src_ref=src, dst_ref=dst, send_sem=send, recv_sem=recv, device_id=to, device_id_type=MESH
    )


class Place:
    def __init__(self, sizes, sequences):
        self.fsdp, self.ctx, self.tp = sizes
        self.subs = self.tp // sequences
        self.blocks = self.ctx * self.subs
        self.f, self.x, self.t = (lax.axis_index(a) for a in ("fsdp", "ctx", "tp"))
        self.seq, self.sub = self.t // self.subs, self.t % self.subs
        self.block = self.x * self.subs + self.sub

    def owner(self, block):
        return {"ctx": block // self.subs, "tp": self.seq * self.subs + block % self.subs}

    def barrier(self):
        semaphore = pltpu.get_barrier_semaphore()
        count = 0
        for axis, size, me in (("fsdp", self.fsdp, self.f), ("ctx", self.ctx, self.x), ("tp", self.tp, self.t)):
            for r in range(1, size):
                pl.semaphore_signal(
                    semaphore, inc=1, device_id={axis: lax.rem(me + r, size)}, device_id_type=MESH
                )
                count += 1
        if self.subs > 1:
            for r in range(1, self.blocks):
                pl.semaphore_signal(
                    semaphore,
                    inc=1,
                    device_id=self.owner(lax.rem(self.block + r, self.blocks)),
                    device_id_type=MESH,
                )
                count += 1
        pl.semaphore_wait(semaphore, count)


class Reduce:
    def __init__(self, k, w, n, d, sizes, tp=True):
        self.k, self.w, self.n, self.d, self.sizes, self.tp = k, w, n, d, sizes, tp
        fsdp, ctx, tps = sizes
        self.rows, self.part = d // fsdp, d // fsdp // ctx
        self.count = 16 if tp else 15

    def scratch(self):
        k, w, n, d = self.k, self.w, self.n, self.d
        fsdp, ctx, tps = self.sizes
        dma = pltpu.SemaphoreType.DMA
        shapes = [
            pltpu.VMEM((n, k, d, w), BF16),
            pltpu.VMEM((n, fsdp - 1, k, self.rows, w), BF16),
            pltpu.VMEM((n, k, self.rows, w), F32),
            pltpu.VMEM((n, k, self.rows, w), BF16),
            pltpu.VMEM((n, ctx - 1, k, self.part, w), BF16),
            pltpu.VMEM((n, k, self.rows, w), BF16),
            dma((n, fsdp - 1)),
            dma((n, fsdp - 1)),
            dma((n, ctx - 1)),
            dma((n, ctx - 1)),
            dma((n, ctx - 1)),
            dma((n, ctx - 1)),
        ]
        if self.tp:
            shapes += [
                pltpu.VMEM((tps - 1, n, k, d, w), BF16),
                pltpu.VMEM((tps - 1, n, k, d, w), BF16),
                dma((tps - 1, n)),
                dma((tps - 1, n)),
            ]
        else:
            shapes += [pltpu.VMEM((tps, k, self.rows, w), F32), dma((tps - 1,)), dma((tps - 1,))]
        return shapes

    def bind(self, place, refs):
        self.place = place
        self.s2, self.r2, self.own, self.s3, self.r3, self.fin = refs[:6]
        self.m2, self.m3, self.m4 = refs[6:8], refs[8:10], refs[10:12]
        if self.tp:
            self.s1, self.r1 = refs[12:14]
            self.m1 = refs[14:16]
        else:
            self.all, self.m1 = refs[12], refs[13:15]

    def d1(self, o, c):
        p = self.place
        to = {"tp": lax.rem(p.t + o, p.tp)}
        if self.tp:
            return remote(
                self.s1.at[o - 1, c], self.r1.at[o - 1, c], self.m1[0].at[o - 1, c], self.m1[1].at[o - 1, c], to
            )
        return remote(self.all.at[p.t], self.all.at[p.t], self.m1[0].at[o - 1], self.m1[1].at[o - 1], to)

    def d2(self, r, c):
        p = self.place
        to = lax.rem(p.f + r, p.fsdp)
        rows = pl.ds(pl.multiple_of(to * self.rows, self.rows), self.rows)
        return remote(
            self.s2.at[c, :, rows, :],
            self.r2.at[c, r - 1],
            self.m2[0].at[c, r - 1],
            self.m2[1].at[c, r - 1],
            {"fsdp": to},
        )

    def spot(self, x):
        return pl.ds(pl.multiple_of(x * self.part, self.part), self.part)

    def d3(self, q, c):
        p = self.place
        to = lax.rem(p.x + q, p.ctx)
        return remote(
            self.s3.at[c, :, self.spot(to), :],
            self.r3.at[c, q - 1],
            self.m3[0].at[c, q - 1],
            self.m3[1].at[c, q - 1],
            {"ctx": to},
        )

    def d4(self, q, c):
        p = self.place
        to = lax.rem(p.x + q, p.ctx)
        mine = self.fin.at[c, :, self.spot(p.x), :]
        return remote(mine, mine, self.m4[0].at[c, q - 1], self.m4[1].at[c, q - 1], {"ctx": to})

    def put(self, o, c, k, value):
        self.s1[o - 1, c, k] = value.astype(BF16)

    def give(self, o, c):
        self.d1(o, c).start()

    def take(self, c, acc):
        p, w = self.place, self.w
        if self.tp:
            for o in range(1, p.tp):
                self.d1(o, c).wait_recv()
            for k in range(self.k):
                total = acc[k, :, 0:w]
                for o in range(1, p.tp):
                    total = total + self.r1[o - 1, c, k].astype(F32)
                acc[k, :, 0:w] = total
        for k in range(self.k):
            self.s2[c, k] = acc[k, :, 0:w].astype(BF16)
        for r in range(1, p.fsdp):
            self.d2(r, c).start()
        for k in range(self.k):
            self.own[c, k] = acc[k, pl.ds(pl.multiple_of(p.f * self.rows, self.rows), self.rows), 0:w]

    def fold(self, c):
        p = self.place
        for r in range(1, p.fsdp):
            self.d2(r, c).wait_recv()
        for k in range(self.k):
            total = self.own[c, k]
            for r in range(1, p.fsdp):
                total = total + self.r2[c, r - 1, k].astype(F32)
            if self.tp:
                self.own[c, k] = total
                self.s3[c, k] = total.astype(BF16)
            else:
                self.all[p.t, k] = total
        if self.tp:
            for q in range(1, p.ctx):
                self.d3(q, c).start()
        else:
            for o in range(1, p.tp):
                self.d1(o, c).start()

    def share(self, c):
        p = self.place
        for o in range(1, p.tp):
            self.d1(o, c).wait_recv()
        for k in range(self.k):
            total = self.all[0, k]
            for o in range(1, p.tp):
                total = total + self.all[o, k]
            self.own[c, k] = total
            self.s3[c, k] = total.astype(BF16)
        for q in range(1, p.ctx):
            self.d3(q, c).start()

    def finish(self, c):
        p = self.place
        for q in range(1, p.ctx):
            self.d3(q, c).wait_recv()
        for k in range(self.k):
            total = self.own[c, k, self.spot(p.x), :]
            for q in range(1, p.ctx):
                total = total + self.r3[c, q - 1, k].astype(F32)
            self.fin[c, k, self.spot(p.x), :] = total.astype(BF16)
        for q in range(1, p.ctx):
            self.d4(q, c).start()

    def close(self):
        p = self.place

        @pl.loop(0, self.n)
        def _(c):
            for q in range(1, p.ctx):
                self.d4(q, c).wait()
                self.d3(q, c).wait_send()
            for r in range(1, p.fsdp):
                self.d2(r, c).wait_send()
            for o in range(1, p.tp):
                self.d1(o, c).wait_send()


class Everywhere:
    def __init__(self, shape, sizes):
        self.shape, self.sizes, self.count = shape, sizes, 9

    def scratch(self):
        dma = pltpu.SemaphoreType.DMA
        shapes = []
        for size in self.sizes:
            shapes += [pltpu.VMEM((size,) + self.shape, F32), dma((size - 1,)), dma((size - 1,))]
        return shapes

    def bind(self, place, refs):
        self.place, self.refs = place, refs

    def copy(self, stage, r):
        p = self.place
        axis, size, me = (
            ("fsdp", p.fsdp, p.f),
            ("ctx", p.ctx, p.x),
            ("tp", p.tp, p.t),
        )[stage]
        buf, send, recv = self.refs[3 * stage : 3 * stage + 3]
        return remote(
            buf.at[me], buf.at[me], send.at[r - 1], recv.at[r - 1], {axis: lax.rem(me + r, size)}
        )

    def start(self, stage, value):
        p = self.place
        me = (p.f, p.x, p.t)[stage]
        self.refs[3 * stage][me] = value
        for r in range(1, self.sizes[stage]):
            self.copy(stage, r).start()

    def total(self, stage):
        buf = self.refs[3 * stage]
        for r in range(1, self.sizes[stage]):
            self.copy(stage, r).wait()
        total = buf[0]
        for r in range(1, self.sizes[stage]):
            total = total + buf[r]
        return total


def norm_back(grad, normed, inverse, gain):
    scaled = grad * gain
    inner = (
        scaled
        - jnp.mean(scaled, axis=-1, keepdims=True)
        - normed * jnp.mean(scaled * normed, axis=-1, keepdims=True)
    )
    return inner * inverse


def half_lanes(rows):
    return lax.broadcasted_iota(jnp.int32, (rows, 128), 1)


def both_halves(values, upper):
    low = half_lanes(values.shape[0]) < 64
    turned = pltpu.roll(values, 64, 1)
    return jnp.where(low, turned, values) if upper else jnp.where(low, values, turned)


class Gather:
    def __init__(self, place, shard, spot, to_tp, refs):
        self.place, self.shard, self.spot, self.to_tp = place, shard, spot, to_tp
        self.fsend, self.frecv, self.tsend, self.trecv, self.local = refs

    def keep(self):
        p = self.place
        return pltpu.make_async_copy(self.shard, self.spot(p.t, p.f), self.local.at[0])

    def across(self, r):
        p = self.place
        return remote(
            self.shard,
            self.spot(p.t, p.f),
            self.fsend.at[r - 1],
            self.frecv.at[r - 1],
            {"fsdp": lax.rem(p.f + r, p.fsdp)},
        )

    def beside(self, o, r):
        p = self.place
        spot = self.spot(p.t, lax.rem(p.f - r + p.fsdp, p.fsdp))
        return remote(
            self.shard if r == 0 else spot,
            spot,
            self.tsend.at[o - 1, r],
            self.trecv.at[o - 1, r],
            {"tp": lax.rem(p.t + o, p.tp)},
        )

    def begin(self):
        p = self.place
        for r in range(1, p.fsdp):
            self.across(r).start()
        if self.to_tp:
            for o in range(1, p.tp):
                self.beside(o, 0).start()
        self.keep().start()

    def forward(self):
        p = self.place
        for r in range(1, p.fsdp):
            self.across(r).wait_recv()
            if self.to_tp:
                for o in range(1, p.tp):
                    self.beside(o, r).start()
        self.keep().wait()

    def arrive(self):
        p = self.place
        if self.to_tp:
            for o in range(1, p.tp):
                for r in range(p.fsdp):
                    self.beside(o, r).wait_recv()

    def close(self):
        p = self.place
        for r in range(1, p.fsdp):
            self.across(r).wait_send()
        if self.to_tp:
            for o in range(1, p.tp):
                for r in range(p.fsdp):
                    self.beside(o, r).wait_send()


INPUTS = ["pic_start", "pic_mode", "tokens", "routes", "upstream"]
INPUTS += ["kv_shard", "wq_shard", "wo_shard", "up_shard", "down_shard"]
INPUTS += ["router_in", "bias_in", "gain1_in", "bias1_in", "gain2_in", "bias2_in", "down_bias_in"]
OUTPUTS = ["out_hbm", "grad_hbm", "ud_out", "wo_out", "wq_out", "kr_out", "vec_out", "bias_out"]
FIRST = ["kv", "rt", "wq"]
FSDP_ONLY = ["kv", "rt"]


def layer_kernel(dims, names, *refs):
    sizes, sequences, tokens, width, experts, pics, length, reducers = dims
    fsdp, ctx, tps = sizes
    named = INPUTS + OUTPUTS + names
    a = types.SimpleNamespace(**dict(zip(named, refs[: len(named)])))
    rest = refs[len(named) :]
    r_ud, r_wo, r_wq, r_kr, r_vec, r_bias = reducers
    place = Place(sizes, sequences)
    for reducer in reducers:
        reducer.bind(place, rest[: reducer.count])
        rest = rest[reducer.count :]
    tiles = tokens // TQ
    cw, chunks = r_ud.w, r_ud.n
    rows_t = min(1024, tokens)
    big = min(BIG, tokens)
    shard_rows = width // fsdp

    def span(index, size):
        return pl.ds(pl.multiple_of(index * size, size), size)

    spots = dict(
        kv=lambda t, f: a.wkv.at[span(f, shard_rows), :],
        rt=lambda t, f: a.rpad.at[0:16, span(f, shard_rows)],
        wq=lambda t, f: a.wq.at[t, :, span(f, shard_rows)],
        wo=lambda t, f: a.wo.at[t, :, span(f, shard_rows)],
    )
    shards = dict(kv=a.kv_shard, rt=a.rt_shard, wq=a.wq_shard, wo=a.wo_shard)
    later = ["wo"]
    for c in range(chunks):
        cut = slice(c * cw, (c + 1) * cw)
        up, down = "up%d" % c, "down%d" % c
        later += [up, down]
        shards[up], shards[down] = a.up_shard.at[:, cut], a.down_shard.at[cut, :]
        spots[up] = lambda t, f, cut=cut: a.up.at[t, span(f, shard_rows), cut]
        spots[down] = lambda t, f, cut=cut: a.down.at[t, cut, span(f, shard_rows)]
    weights = {}
    for name in FIRST + later:
        weights[name] = Gather(place, shards[name], spots[name], name not in FSDP_ONLY, rest[:5])
        rest = rest[5:]

    own_slice = (place.seq, pl.ds(pl.multiple_of(place.sub * tokens, tokens), tokens))
    loads = [
        pltpu.make_async_copy(source.at[own_slice[0], own_slice[1], :], target, a.load_sem.at[k])
        for k, (source, target) in enumerate(
            ((a.tokens, a.tok), (a.upstream, a.ups))
        )
    ]
    loads.append(
        pltpu.make_async_copy(
            a.routes.at[place.seq, :, pl.ds(pl.multiple_of(place.sub * tokens, tokens), tokens)], a.rt, a.load_sem.at[2]
        )
    )
    for load in loads:
        load.start()

    router = a.router_in[...].astype(F32)
    a.rt_shard[...] = jnp.concatenate([router, router], axis=0).astype(BF16)
    a.rpad[16:, :] = jnp.zeros((112, width), BF16)
    a.bias_shard[...] = a.bias_in[...].astype(F32)
    a.bias_raw[place.t] = a.bias_shard[...]
    place.barrier()
    for name in FIRST:
        weights[name].begin()

    def bias_copy(o):
        spot = a.bias_raw.at[place.t]
        return remote(
            a.bias_shard, spot, a.bias_sem.at[0, o - 1], a.bias_sem.at[1, o - 1], {"tp": lax.rem(place.t + o, tps)}
        )

    for o in range(1, tps):
        bias_copy(o).start()

    def row(ref):
        values = ref[...].astype(F32)
        return jnp.concatenate([values[k : k + 1, :] for k in range(values.shape[0])], axis=1)

    gain1, bias1 = row(a.gain1_in), row(a.bias1_in)
    q_base = place.block * tokens
    starts = picture_starts(a.pic_start, a.pic_mode, place.seq, pics)
    lanes = half_lanes(TQ)
    own_rows = pl.ds(pl.multiple_of(q_base, tokens), tokens)

    def tile_rows(i):
        return span(i, TQ)

    def gates(rows):
        return [a.meta[rows, k : k + 1] for k in range(4)]

    def expert_of(c):
        return 2 * c + jnp.where(lanes >= 64, 1, 0)

    def normalise(x):
        center = x - jnp.mean(x, axis=-1, keepdims=True)
        inverse = lax.rsqrt(jnp.mean(center * center, axis=-1, keepdims=True) + TINY)
        return center * inverse, inverse

    def choose(full, r):
        expert = r.astype(jnp.int32)
        chosen = jnp.zeros((TQ, 128), F32)
        for c in range(experts // 2):
            chosen = jnp.where(expert == expert_of(c), full[:, c * 128 : (c + 1) * 128], chosen)
        return chosen + pltpu.roll(chosen, 64, 1)

    loads[0].wait()
    loads[2].wait()

    @pl.loop(0, tiles)
    def _(i):
        rows = tile_rows(i)
        normed, _ = normalise(a.tok[rows, :].astype(F32))
        a.hid1[rows, :] = (normed * gain1 + bias1).astype(BF16)

    a.kv[pl.ds(length, TQ), :] = jnp.zeros((TQ, 128), BF16)
    weights["kv"].forward()

    @pl.loop(0, tiles)
    def _(i):
        rows = tile_rows(i)
        pair = dot(a.hid1[rows, :], a.wkv[...])
        a.kv[pl.ds(pl.multiple_of(q_base + i * TQ, TQ), TQ), :] = pair.astype(BF16)

    after_me, before_me = place.block + 1 < place.blocks, place.block > 0

    def pass_on(d):
        keys = pl.ds(pl.multiple_of((place.block - d) * tokens, tokens), tokens)
        to = place.owner(lax.rem(place.block + 1, place.blocks))
        return remote(a.kv.at[keys, :], a.kv.at[keys, :], a.kv_sem.at[0, d], a.kv_sem.at[1, d], to)

    def reach_back():
        keys = pl.ds(pl.multiple_of(q_base, TQ), TQ)
        to = place.owner(lax.rem(place.block + place.blocks - 1, place.blocks))
        return remote(a.kv.at[keys, :], a.kv.at[keys, :], a.near_sem.at[2], a.near_sem.at[3], to)

    @pl.when(after_me)
    def _():
        pass_on(0).start()

    @pl.when(before_me)
    def _():
        reach_back().start()

    weights["rt"].forward()

    @pl.loop(0, tiles)
    def _(i):
        rows = tile_rows(i)
        logits = dot_nt(a.hid1[rows, :], a.rpad[...])
        pairs = jnp.concatenate([a.rt[:, rows].astype(F32)] * 4, axis=0).T
        r0, r1 = pairs[:, 0:1].astype(jnp.int32), pairs[:, 1:2].astype(jnp.int32)
        l0 = jnp.sum(jnp.where(lanes == r0, logits, 0.0), axis=-1, keepdims=True)
        l1 = jnp.sum(jnp.where(lanes == r1, logits, 0.0), axis=-1, keepdims=True)
        top = jnp.maximum(l0, l1)
        e0, e1 = jnp.exp(l0 - top), jnp.exp(l1 - top)
        a.meta[rows, 0:1] = e0 / (e0 + e1)
        a.meta[rows, 1:2] = e1 / (e0 + e1)
        a.meta[rows, 2:3] = r0.astype(F32)
        a.meta[rows, 3:4] = r1.astype(F32)

    weights["wq"].forward()
    for name in later:
        weights[name].begin()
    weights["wq"].arrive()

    @pl.loop(0, tiles)
    def _(i):
        rows = tile_rows(i)
        _, _, r0, r1 = gates(rows)
        full = dot_nt(a.hid1[rows, :], a.wq[...].reshape(width, width))
        for s, r in enumerate((r0, r1)):
            a.q[s, rows, :] = jnp.where(lanes < 64, choose(full, r) * 0.125, 0.0).astype(BF16)

    @pl.loop(0, tiles)
    def _(i):
        a.top[i] = jnp.full((1, 2 * TQ), NEG, F32)
        a.total[i] = jnp.zeros((1, 2 * TQ), F32)
    a.dqt[...] = jnp.zeros_like(a.dqt)

    def look(i, k0, size, masked):
        rows = tile_rows(i)
        keys = pl.ds(pl.multiple_of(k0, TK), size)
        q = jnp.concatenate([a.q[0, rows, :], a.q[1, rows, :]], axis=0)
        pair = a.kv[keys, :]
        scores = dot_nt(pair, q)
        if masked:
            scores = jnp.where(mask_of(q_base + i * TQ, k0, size, TQ, starts), scores, NEG)
        before = a.top[i]
        now = jnp.maximum(before, jnp.max(scores, axis=0, keepdims=True))
        probs = jnp.exp(scores - now)
        scale = jnp.exp(before - now)
        a.top[i] = now
        a.total[i] = a.total[i] * scale + jnp.sum(probs, axis=0, keepdims=True)
        a.dqt[i] = a.dqt[i] * scale + dot_tn(pair, probs.astype(BF16))

    @pl.when(after_me)
    def _():
        reach_back().wait_recv()

    @pl.loop(0, tiles)
    def _(i):
        look(i, q_base + i * TK, 2 * TK, True)

    for i in range(1, tiles):
        look(i, q_base, i * TK, False)

    @pl.loop(0, place.blocks - 1)
    def _(j):
        @pl.when(j < place.block)
        def _():
            pass_on(j).wait_recv()

            @pl.when(after_me)
            def _():
                pass_on(j + 1).start()

            @pl.loop(0, tokens // big)
            def _(k):
                @pl.loop(0, tiles)
                def _(i):
                    look(i, (place.block - 1 - j) * tokens + k * big, big, False)

        @pl.when(j == place.blocks - 2)
        def _():
            weights["wo"].forward()

    weights["up0"].forward()
    weights["down0"].forward()

    @pl.loop(0, tiles)
    def _(i):
        rows = tile_rows(i)
        both = (a.dqt[i] / a.total[i]).T
        a.att[0, rows, :] = both[:TQ]
        a.att[1, rows, :] = both[TQ:]
        a.logt[i] = a.top[i] + jnp.log(a.total[i])

    gain2, bias2, down_bias = row(a.gain2_in), row(a.bias2_in), row(a.down_bias_in)
    a.vec[...] = jnp.zeros_like(a.vec)
    a.bias_acc[...] = jnp.zeros_like(a.bias_acc)
    a.woacc[...] = jnp.zeros_like(a.woacc)
    weights["wo"].arrive()

    @pl.loop(0, tiles)
    def _(i):
        rows = tile_rows(i)
        g0, g1, r0, r1 = gates(rows)
        after = a.tok[rows, :].astype(F32)
        out_w = a.wo[...].reshape(width, width)
        for s, (g, r) in enumerate(((g0, r0), (g1, r1))):
            twice = both_halves(a.att[s, rows, :], True)
            expert = r.astype(jnp.int32)
            for c in range(experts // 2):
                a.wide[s, rows, c * 128 : (c + 1) * 128] = jnp.where(expert == expert_of(c), twice, 0.0).astype(BF16)
            projected = dot(a.wide[s, rows, :], out_w)
            a.proj[s, rows, :] = projected
            after = after + g * projected
        normed, inverse = normalise(after)
        a.normed2[rows, :] = normed
        a.inv2[rows, :] = inverse
        a.hid2[rows, :] = (normed * gain2 + bias2).astype(BF16)
        a.out_acc[rows, :] = after + down_bias
        a.mid[rows, :] = jnp.zeros_like(after)

    loads[1].wait()
    for o in range(1, tps):
        bias_copy(o).wait_recv()
    lines = cw // 128
    for t in range(tps):
        for c in range(chunks):
            a.up_bias[t * chunks + c] = jnp.concatenate(
                [a.bias_raw[t, c * lines + k : c * lines + k + 1, :] for k in range(lines)], axis=1
            )

    def feed(t, c):
        cols = span(c, cw)
        whole = tokens == rows_t
        if not whole:
            a.gacc[...] = jnp.zeros_like(a.gacc)

        @pl.loop(0, tokens // rows_t)
        def _(i):
            rows = span(i, rows_t)
            h2, u = a.hid2[rows, :], a.ups[rows, :]
            pre = dot(h2, a.up[t, :, cols]) + a.up_bias[t * chunks + c]
            sig = 1.0 / (1.0 + jnp.exp(-pre))
            active = (pre * sig).astype(BF16)
            a.out_acc[rows, :] += dot(active, a.down[t, cols, :])
            down_part = dot_tn(u, active)
            a.gacc[1, :, 0:cw] = down_part if whole else a.gacc[1, :, 0:cw] + down_part
            slope = sig * (1.0 + pre * (1.0 - sig))
            grad = dot_nt(u, a.down[t, cols, :]) * slope
            low = grad.astype(BF16)
            a.bias_acc[t * chunks + c] += jnp.sum(low.astype(F32), axis=0, keepdims=True)
            up_part = dot_tn(h2, low)
            a.gacc[0, :, 0:cw] = up_part if whole else a.gacc[0, :, 0:cw] + up_part
            a.mid[rows, :] += dot_nt(low, a.up[t, :, cols])

    @pl.loop(0, chunks)
    def _(c):
        for k in range(chunks):

            @pl.when(c == k)
            def _():
                weights["up%d" % k].arrive()
                weights["down%d" % k].arrive()

        for o in range(1, tps):
            feed(lax.rem(place.t + o, tps), c)
            for k in range(2):
                r_ud.put(o, c, k, a.gacc[k, :, 0:cw])
            r_ud.give(o, c)
        for k in range(1, chunks):

            @pl.when(c + 1 == k)
            def _():
                weights["up%d" % k].forward()
                weights["down%d" % k].forward()

        feed(place.t, c)
        r_ud.take(c, a.gacc)

    r_bias.start(2, a.bias_acc[...])

    def share_out(low, hbm, slot):
        spot = hbm.at[own_slice[0], own_slice[1], :]
        copies = [
            remote(
                low, spot, a.out_sem.at[0, slot, o - 1], a.out_sem.at[1, slot, o - 1], {"tp": lax.rem(place.t + o, tps)}
            )
            for o in range(1, tps)
        ]
        copies.append(pltpu.make_async_copy(low, spot, a.loc_sem.at[slot]))
        for copy in copies:
            copy.start()
        return copies

    def add_row(k, value):
        a.vec[k : k + 1, :] += jnp.sum(value, axis=0, keepdims=True)

    @pl.loop(0, tiles)
    def _(i):
        rows = tile_rows(i)
        g0, g1, r0, r1 = gates(rows)
        out_w = a.wo[...].reshape(width, width)
        a.res_low[rows, :] = a.out_acc[rows, :].astype(BF16)
        upstream = a.ups[rows, :].astype(F32)
        grad, normed = a.mid[rows, :], a.normed2[rows, :]
        resid = upstream + norm_back(grad, normed, a.inv2[rows, :], gain2)
        a.mid[rows, :] = resid
        add_row(2, grad * normed)
        add_row(3, grad)
        add_row(4, upstream)
        d0 = jnp.sum(a.proj[0, rows, :] * resid, axis=-1, keepdims=True)
        d1 = jnp.sum(a.proj[1, rows, :] * resid, axis=-1, keepdims=True)
        mean = g0 * d0 + g1 * d1
        for s, (g, r) in enumerate(((g0, r0), (g1, r1))):
            low = (g * resid).astype(BF16)
            a.woacc[0] += dot_tn(low, a.wide[s, rows, :])
            chosen = jnp.where(lanes >= 64, choose(dot_nt(low, out_w), r), 0.0).astype(BF16)
            a.da[s, rows, :] = chosen
            product = chosen.astype(F32) * jnp.where(lanes >= 64, a.att[s, rows, :], 0.0)
            a.delta[i, :, s * TQ : (s + 1) * TQ] = jnp.sum(product.T, axis=0, keepdims=True)
        lane_expert = lax.rem(lanes, experts)
        lg = jnp.where(lane_expert == r0.astype(jnp.int32), g0 * (d0 - mean), 0.0)
        lg = lg + jnp.where(lane_expert == r1.astype(jnp.int32), g1 * (d1 - mean), 0.0)
        high = lg.astype(BF16).astype(F32)
        a.lgp[rows, :] = jnp.where(
            lanes < experts, high, jnp.where(lanes < 2 * experts, lg - high, 0.0)
        ).astype(BF16)

    out_copies = share_out(a.res_low, a.out_hbm, 0)

    def hand_out(reducer, acc):
        w = reducer.w
        for t in range(tps):

            @pl.when(t != place.t)
            def _():
                o = lax.rem(t - place.t + tps, tps)
                reducer.s1[o - 1, 0, 0] = acc[0, :, t * w : (t + 1) * w].astype(BF16)
                reducer.give(o, 0)

    def take_own(reducer, acc):
        w = reducer.w
        for t in range(tps):

            @pl.when(t == place.t)
            def _():
                a.gacc[0, :, 0:w] = acc[0, :, t * w : (t + 1) * w]

        reducer.take(0, a.gacc)

    hand_out(r_wo, a.woacc)
    r_bias.start(0, r_bias.total(2))

    a.dqt[...] = jnp.zeros_like(a.dqt)
    a.dkv[...] = jnp.zeros_like(a.dkv)

    def attend(i, k0, size, masked):
        rows = tile_rows(i)
        keys = pl.ds(pl.multiple_of(k0, TK), size)
        q = jnp.concatenate([a.q[0, rows, :], a.q[1, rows, :]], axis=0)
        d_att = jnp.concatenate([a.da[0, rows, :], a.da[1, rows, :]], axis=0)
        pair = a.kv[keys, :]
        scores = dot_nt(pair, q)
        if masked:
            scores = jnp.where(mask_of(q_base + i * TQ, k0, size, TQ, starts), scores, NEG)
        probs = jnp.exp(scores - a.logt[i])
        prob_grad = dot_nt(pair, d_att)
        score_grad = (probs * (prob_grad - a.delta[i])).astype(BF16)
        a.dkv[keys, :] += dot(score_grad, q) + dot(probs.astype(BF16), d_att)
        a.dqt[i] += dot_tn(pair, score_grad)

    def dkv_copy(block):
        return remote(
            a.dkv_send.at[block],
            a.dkv_recv.at[block],
            a.dkv_sem.at[0, block],
            a.dkv_sem.at[1, block],
            place.owner(lax.rem(place.block + place.blocks - 1, place.blocks)),
        )

    def hand_down(block):
        keys = span(block, tokens)

        @pl.when(after_me)
        def _():
            dkv_copy(block).wait_recv()
            a.dkv[keys, :] += a.dkv_recv[block].astype(F32)

        a.dkv_send[block] = a.dkv[keys, :].astype(BF16)
        dkv_copy(block).start()

    r_ud.fold(0)

    @pl.loop(0, place.blocks - 1)
    def _(j):
        @pl.when(j < place.block)
        def _():
            @pl.loop(0, tokens // big)
            def _(k):
                @pl.loop(0, tiles)
                def _(i):
                    attend(i, j * tokens + k * big, big, False)

            ready = j - jnp.where(after_me, 1, 0)

            @pl.when(ready >= 0)
            def _():
                hand_down(ready)

    take_own(r_wo, a.woacc)
    r_bias.start(1, r_bias.total(0))

    @pl.loop(0, tiles)
    def _(i):
        attend(i, q_base + i * TK, 2 * TK, True)

    for i in range(1, tiles):
        attend(i, q_base, i * TK, False)

    @pl.when(after_me & before_me)
    def _():
        hand_down(place.block - 1)

    r_ud.fold(chunks - 1)
    r_wo.fold(0)

    r_ud.finish(0)

    def near_copy():
        return remote(
            a.near_send,
            a.near_buf,
            a.near_sem.at[0],
            a.near_sem.at[1],
            place.owner(lax.rem(place.block + 1, place.blocks)),
        )

    @pl.when(after_me)
    def _():
        a.near_send[...] = a.dkv[pl.ds(pl.multiple_of((place.block + 1) * tokens, TQ), TQ), :].astype(BF16)
        near_copy().start()

    @pl.loop(0, tiles)
    def _(i):
        rows = tile_rows(i)
        _, _, r0, r1 = gates(rows)
        dq = (a.dqt[i] * 0.125).T
        first, second = both_halves(dq[:TQ], False), both_halves(dq[TQ:], False)
        for c in range(experts // 2):
            column = jnp.where(r0.astype(jnp.int32) == expert_of(c), first, 0.0)
            column = jnp.where(r1.astype(jnp.int32) == expert_of(c), second, column)
            a.dqw[rows, c * 128 : (c + 1) * 128] = column.astype(BF16)

    a.woacc[0] = dot_tn(a.hid1[...], a.dqw[...])
    hand_out(r_wq, a.woacc)

    take_own(r_wq, a.woacc)

    @pl.when(after_me)
    def _():
        dkv_copy(place.block).wait_recv()
        a.dkv[own_rows, :] += a.dkv_recv[place.block].astype(F32)

    @pl.when(before_me)
    def _():
        near_copy().wait_recv()
        a.dkv[pl.ds(pl.multiple_of(q_base, TQ), TQ), :] += a.near_buf[...].astype(F32)

    a.pairg[:, 0:128] = a.dkv[own_rows, :].astype(BF16)
    a.pairg[:, 128:256] = a.lgp[...]
    a.gacc[0, :, 0:256] = dot_tn(a.hid1[...], a.pairg[...])
    r_kr.take(0, a.gacc)

    r_wq.fold(0)

    @pl.loop(0, tiles)
    def _(i):
        rows = tile_rows(i)
        normed, inverse = normalise(a.tok[rows, :].astype(F32))
        grad = dot(a.dqw[rows, :], a.wq[...].reshape(width, width))
        grad = grad + dot_nt(a.pairg[rows, 0:128], a.wkv[...]) + dot(a.lgp[rows, :], a.rpad[...])
        add_row(0, grad * normed)
        add_row(1, grad)
        a.grad_low[rows, :] = (a.mid[rows, :] + norm_back(grad, normed, inverse, gain1)).astype(BF16)

    grad_copies = share_out(a.grad_low, a.grad_hbm, 1)
    r_vec.start(2, a.vec[...])
    r_kr.fold(0)
    r_vec.start(0, r_vec.total(2))
    r_ud.finish(chunks - 1)
    r_wo.finish(0)
    r_kr.share(0)
    r_vec.start(1, r_vec.total(0))
    r_wq.finish(0)
    r_kr.finish(0)
    a.vec_out[...] = r_vec.total(1)
    a.bias_out[...] = r_bias.total(1)
    for reducer, out in ((r_ud, a.ud_out), (r_wo, a.wo_out), (r_wq, a.wq_out), (r_kr, a.kr_out)):
        reducer.close()
        out[...] = reducer.fin[...]

    @pl.loop(0, place.block)
    def _(j):
        dkv_copy(j).wait_send()

    @pl.when(after_me)
    def _():
        near_copy().wait_send()

        @pl.loop(0, place.block + 1)
        def _(d):
            pass_on(d).wait_send()

    @pl.when(before_me)
    def _():
        reach_back().wait_send()

    for name in FIRST + later:
        weights[name].close()
    for o in range(1, tps):
        bias_copy(o).wait_send()
    for copy in out_copies + grad_copies:
        copy.wait()


def run_layer(sizes, sequences, shape, experts, arrays):
    fsdp, ctx, tps = sizes
    subs = tps // sequences
    width = shape[2]
    tokens = shape[1] // subs
    length = shape[1] * ctx
    blocks = ctx * subs
    tiles = tokens // TQ
    local_hidden = arrays[8].shape[1]
    cw = min(512, local_hidden)
    chunks = local_hidden // cw
    w = width // tps
    reducers = (
        Reduce(2, cw, chunks, width, sizes),
        Reduce(1, w, 1, width, sizes),
        Reduce(1, w, 1, width, sizes),
        Reduce(1, 256, 1, width, sizes, tp=False),
        Everywhere((8, width), sizes),
        Everywhere((tps * chunks, 1, cw), sizes),
    )
    dims = (sizes, sequences, tokens, width, experts, arrays[0].shape[1], length, reducers)
    rows = width // fsdp
    dma = pltpu.SemaphoreType.DMA
    vmem = pltpu.VMEM
    scratch = dict(
        tok=vmem((tokens, width), BF16),
        rt=vmem((2, tokens), jnp.int32),
        ups=vmem((tokens, width), BF16),
        load_sem=dma((3,)),
        wkv=vmem((width, 128), BF16),
        rt_shard=vmem((16, rows), BF16),
        rpad=vmem((128, width), BF16),
        wq=vmem((tps, w, width), BF16),
        wo=vmem((tps, w, width), BF16),
        up=vmem((tps, width, local_hidden), BF16),
        down=vmem((tps, local_hidden, width), BF16),
        bias_shard=vmem((local_hidden // 128, 128), F32),
        bias_raw=vmem((tps, local_hidden // 128, 128), F32),
        up_bias=vmem((tps * chunks, 1, cw), F32),
        bias_sem=dma((2, tps - 1)),
        meta=vmem((tokens, 8), F32),
        hid1=vmem((tokens, width), BF16),
        q=vmem((2, tokens, 128), BF16),
        kv=vmem((length + TQ, 128), BF16),
        kv_sem=dma((2, blocks)),
        near_sem=dma((4,)),
        top=vmem((tiles, 1, 2 * TQ), F32),
        total=vmem((tiles, 1, 2 * TQ), F32),
        att=vmem((2, tokens, 128), F32),
        logt=vmem((tiles, 1, 2 * TQ), F32),
        wide=vmem((2, tokens, width), BF16),
        proj=vmem((2, tokens, width), F32),
        normed2=vmem((tokens, width), F32),
        hid2=vmem((tokens, width), BF16),
        out_acc=vmem((tokens, width), F32),
        mid=vmem((tokens, width), F32),
        inv2=vmem((tokens, 1), F32),
        gacc=vmem((2, width, max(cw, 256)), F32),
        woacc=vmem((1, width, width), F32),
        da=vmem((2, tokens, 128), BF16),
        delta=vmem((tiles, 1, 2 * TQ), F32),
        lgp=vmem((tokens, 128), BF16),
        dqt=vmem((tiles, 128, 2 * TQ), F32),
        dkv=vmem((length + TQ, 128), F32),
        dkv_send=vmem((blocks - 1, tokens, 128), BF16),
        dkv_recv=vmem((blocks - 1, tokens, 128), BF16),
        dkv_sem=dma((2, blocks - 1)),
        dqw=vmem((tokens, width), BF16),
        pairg=vmem((tokens, 256), BF16),
        vec=vmem((8, width), F32),
        bias_acc=vmem((tps * chunks, 1, cw), F32),
        res_low=vmem((tokens, width), BF16),
        grad_low=vmem((tokens, width), BF16),
        near_buf=vmem((TQ, 128), BF16),
        near_send=vmem((TQ, 128), BF16),
        loc_sem=dma((2,)),
        out_sem=dma((2, 2, tps - 1)),
    )
    shapes = list(scratch.values())
    for reducer in reducers:
        shapes += reducer.scratch()
    for _ in range(len(FIRST) + 1 + 2 * chunks):
        shapes += [dma((fsdp - 1,)), dma((fsdp - 1,)), dma((tps - 1, fsdp)), dma((tps - 1, fsdp)), dma((1,))]
    return pl.pallas_call(
        functools.partial(layer_kernel, dims, list(scratch)),
        in_specs=[SMEM, SMEM] + [ANY] * 8 + [VMEM] * 7,
        out_specs=[ANY, ANY] + [VMEM] * 6,
        out_shape=[
            jax.ShapeDtypeStruct(shape, BF16),
            jax.ShapeDtypeStruct(shape, BF16),
            jax.ShapeDtypeStruct((chunks, 2, rows, cw), BF16),
            jax.ShapeDtypeStruct((1, 1, rows, w), BF16),
            jax.ShapeDtypeStruct((1, 1, rows, w), BF16),
            jax.ShapeDtypeStruct((1, 1, rows, 256), BF16),
            jax.ShapeDtypeStruct((8, width), F32),
            jax.ShapeDtypeStruct((tps * chunks, 1, cw), F32),
        ],
        scratch_shapes=shapes,
        compiler_params=pltpu.CompilerParams(
            vmem_limit_bytes=63 << 20, collective_id=1, has_side_effects=True
        ),
        name="layer",
    )(*arrays)


def settle_kernel(experts, *refs):
    given, made, held, sem = refs[:8], refs[8:22], refs[22:30], refs[30]
    out_to, grad_to, up_to, down_to, wo_to, wq_to, pair_to, router_to, bias_to, *vectors = made
    small = [pltpu.make_async_copy(given[k], held[k], sem.at[k]) for k in range(2, 8)]
    rows = given[0].shape[1] // 4
    pieces = [(k, i, j) for i in range(given[0].shape[0]) for j in range(4) for k in range(2)]
    loads, copies = [], []
    for n, (k, i, j) in enumerate(pieces):
        spot = (i, slice(j * rows, (j + 1) * rows), slice(None))
        loads.append(pltpu.make_async_copy(given[k].at[spot], held[k].at[spot], sem.at[8 + n]))
        copies.append(pltpu.make_async_copy(held[k].at[spot], made[k].at[spot], sem.at[8 + len(pieces) + n]))
    for load in loads + small:
        load.start()
    for load, copy in zip(loads, copies):
        load.wait()
        copy.start()
    for load in small:
        load.wait()
    ud, wo, wq, kr, vec, bias = held[2:]
    chunks, _, rows, cw = ud.shape
    for c in range(chunks):
        up_to[:, c * cw : (c + 1) * cw] = ud[c, 0].astype(F32)
        down_to[c * cw : (c + 1) * cw, :] = ud[c, 1].astype(F32).T
        bias_to[:, c * cw : (c + 1) * cw] = bias[lax.axis_index("tp") * chunks + c]
    wo_to[...] = wo[0, 0].astype(F32).T
    wq_to[...] = wq[0, 0].astype(F32).T
    pair_to[...] = kr[0, 0, :, 0:128].astype(F32)
    router = kr[0, 0, :, 128:256].astype(F32).T
    router_to[...] = router[0:experts] + router[experts : 2 * experts]
    for k, to in enumerate(vectors):
        to[...] = vec[k : k + 1, :]
    for copy in copies:
        copy.wait()


def run_settle(tps, experts, results):
    out, grad, ud, wo, wq, kr, vec, bias = results
    chunks, _, rows, cw = ud.shape
    w, width = wo.shape[3], vec.shape[1]

    def f32(*shape):
        return jax.ShapeDtypeStruct(shape, F32)

    return pl.pallas_call(
        functools.partial(settle_kernel, experts),
        in_specs=[ANY] * 8,
        out_specs=[ANY, ANY] + [VMEM] * 12,
        out_shape=[
            jax.ShapeDtypeStruct(out.shape, BF16),
            jax.ShapeDtypeStruct(out.shape, BF16),
            f32(rows, chunks * cw),
            f32(chunks * cw, rows),
            f32(w, rows),
            f32(w, rows),
            f32(rows, 128),
            f32(experts, rows),
            f32(1, chunks * cw),
        ]
        + [f32(1, width)] * 5,
        scratch_shapes=[pltpu.VMEM(r.shape, r.dtype) for r in results] + [pltpu.SemaphoreType.DMA((8 + 16 * results[0].shape[0],))],
        compiler_params=pltpu.CompilerParams(vmem_limit_bytes=60 << 20),
        name="settle",
    )(*results)


def per_device(
    mesh_sizes,
    tokens,
    expert_routes,
    picture_start,
    picture_mode,
    norm1_gain,
    norm1_bias,
    router_weight,
    query_weight,
    output_weight,
    key_value_weight,
    norm2_gain,
    norm2_bias,
    up_weight,
    up_bias,
    down_weight,
    down_bias,
    upstream_tokens,
):
    local_experts, rows_d, head = query_weight.shape
    experts = local_experts * mesh_sizes[2]
    width = tokens.shape[2]
    heads = local_experts * head

    def lines(vector):
        return vector.reshape(-1, 128)

    results = run_layer(
        mesh_sizes,
        tokens.shape[0],
        tokens.shape,
        experts,
        (
            picture_start,
            picture_mode,
            tokens,
            jnp.transpose(expert_routes, (0, 2, 1)),
            upstream_tokens,
            key_value_weight,
            jnp.transpose(query_weight, (0, 2, 1)).reshape(heads, rows_d),
            output_weight.reshape(heads, rows_d),
            up_weight,
            down_weight,
            router_weight.T,
            lines(up_bias),
            lines(norm1_gain),
            lines(norm1_bias),
            lines(norm2_gain),
            lines(norm2_bias),
            lines(down_bias),
        ),
    )
    outs = run_settle(mesh_sizes[2], experts, results)
    result, input_grad, up_out, down_out, wo_out, wq_out, pair_out, router_out, bias_out, *vectors = outs
    gain1, bias1, gain2, bias2, down_bias_sum = (v.reshape(width) for v in vectors)
    return (
        result,
        input_grad,
        gain1,
        bias1,
        router_out.T,
        jnp.transpose(wq_out.reshape(local_experts, head, rows_d), (0, 2, 1)),
        wo_out.reshape(output_weight.shape),
        pair_out,
        gain2,
        bias2,
        up_out,
        bias_out.reshape(-1),
        down_out,
        down_bias_sum,
    )


def solution(mesh):
    rows = P("fsdp", "ctx", None)
    placed = (
        rows,
        rows,
        P("fsdp", None),
        P("fsdp", None),
        P(),
        P(),
        P("fsdp", None),
        P("tp", "fsdp", None),
        P("tp", None, "fsdp"),
        P("fsdp", None),
        P(),
        P(),
        P("fsdp", "tp"),
        P("tp"),
        P("tp", "fsdp"),
        P(),
        rows,
    )
    sizes = tuple(mesh.shape[axis] for axis in ("fsdp", "ctx", "tp"))
    return jax.shard_map(
        functools.partial(per_device, sizes),
        mesh=mesh,
        in_specs=placed,
        out_specs=(
            rows,
            rows,
            P(),
            P(),
            P("fsdp", None),
            P("tp", "fsdp", None),
            P("tp", None, "fsdp"),
            P("fsdp", None),
            P(),
            P(),
            P("fsdp", "tp"),
            P("tp"),
            P("tp", "fsdp"),
            P(),
        ),
        check_vma=False,
    )
```
